32 devices in a mesh: gx: 4 (over y, core), gy: 8 (over z, x).
Axes of the slice: x: 2, y: 2, z: 4, core: 2. Of those that a mesh axis runs over, the one named last changes fastest.
Arguments:
- text_tokens: bfloat16 [256, 100, 768], P(('gx', 'gy')), may hold values from -6 to 6
- image_regions: bfloat16 [256, 36, 1024], P(('gx', 'gy')), may hold values from -6 to 6
- caption_lengths: int32 [256], P(('gx', 'gy')), may hold values from 8 to 100, as said below
- region_mask: int32 [256, 36], P(('gx', 'gy')), may hold values 0 or 1
- text_cotangent: bfloat16 [256, 100, 768], P(('gx', 'gy')), may hold values from -6 to 6
- image_cotangent: bfloat16 [256, 36, 1024], P(('gx', 'gy')), may hold values from -6 to 6
- text_query: bfloat16 [768, 1024], P(('gx', 'gy')), may hold values from -0.21875 to 0.21875
- image_key: bfloat16 [1024, 1024], P(('gx', 'gy')), may hold values from -0.1875 to 0.1875
- image_value: bfloat16 [1024, 1024], P(('gx', 'gy')), may hold values from -0.1875 to 0.1875
- text_merge: bfloat16 [1024, 768], P(('gx', 'gy')), may hold values from -1 to 1
- text_gain_cross: bfloat16 [768], P(('gx', 'gy')), may hold values from 0.5 to 1.5
- image_query: bfloat16 [1024, 1024], P(('gx', 'gy')), may hold values from -0.1875 to 0.1875
- text_key: bfloat16 [768, 1024], P(('gx', 'gy')), may hold values from -0.21875 to 0.21875
- text_value: bfloat16 [768, 1024], P(('gx', 'gy')), may hold values from -0.21875 to 0.21875
- image_merge: bfloat16 [1024, 1024], P(('gx', 'gy')), may hold values from -1.25 to 1.25
- image_gain_cross: bfloat16 [1024], P(('gx', 'gy')), may hold values from 0.5 to 1.5
- text_up: bfloat16 [768, 3072], P(('gx', 'gy')), may hold values from -0.21875 to 0.21875
- text_bias: bfloat16 [3072], P(('gx', 'gy')), may hold values from -3 to 3
- text_down: bfloat16 [3072, 768], P(('gx', 'gy')), may hold values from -0.109375 to 0.109375
- text_gain_ffn: bfloat16 [768], P(('gx', 'gy')), may hold values from 0.5 to 1.5
- image_up: bfloat16 [1024, 1024], P(('gx', 'gy')), may hold values from -0.1875 to 0.1875
- image_bias: bfloat16 [1024], P(('gx', 'gy')), may hold values from -3 to 3
- image_down: bfloat16 [1024, 1024], P(('gx', 'gy')), may hold values from -0.1875 to 0.1875
- image_gain_ffn: bfloat16 [1024], P(('gx', 'gy')), may hold values from 0.5 to 1.5
- text_self: bfloat16 [768, 2304], P(('gx', 'gy')), may hold values from -0.21875 to 0.21875
- text_mix: bfloat16 [768, 768], P(('gx', 'gy')), may hold values from -1.5 to 1.5
- text_gain_self: bfloat16 [768], P(('gx', 'gy')), may hold values from 0.5 to 1.5
- image_self: bfloat16 [1024, 3072], P(('gx', 'gy')), may hold values from -0.1875 to 0.1875
- image_mix: bfloat16 [1024, 1024], P(('gx', 'gy')), may hold values from -1 to 1
- image_gain_self: bfloat16 [1024], P(('gx', 'gy')), may hold values from 0.5 to 1.5
Outputs:
- text_output: bfloat16 [256, 100, 768], P(('gx', 'gy'))
- image_output: bfloat16 [256, 36, 1024], P(('gx', 'gy'))
- grad_text: float32 [256, 100, 768], P(('gx', 'gy'))
- grad_image: float32 [256, 36, 1024], P(('gx', 'gy'))
- grad_text_query: float32 [768, 1024], P(('gx', 'gy'))
- grad_image_key: float32 [1024, 1024], P(('gx', 'gy'))
- grad_image_value: float32 [1024, 1024], P(('gx', 'gy'))
- grad_text_merge: float32 [1024, 768], P(('gx', 'gy'))
- grad_text_gain_cross: float32 [768], P(('gx', 'gy'))
- grad_image_query: float32 [1024, 1024], P(('gx', 'gy'))
- grad_text_key: float32 [768, 1024], P(('gx', 'gy'))
- grad_text_value: float32 [768, 1024], P(('gx', 'gy'))
- grad_image_merge: float32 [1024, 1024], P(('gx', 'gy'))
- grad_image_gain_cross: float32 [1024], P(('gx', 'gy'))
- grad_text_up: float32 [768, 3072], P(('gx', 'gy'))
- grad_text_bias: float32 [3072], P(('gx', 'gy'))
- grad_text_down: float32 [3072, 768], P(('gx', 'gy'))
- grad_text_gain_ffn: float32 [768], P(('gx', 'gy'))
- grad_image_up: float32 [1024, 1024], P(('gx', 'gy'))
- grad_image_bias: float32 [1024], P(('gx', 'gy'))
- grad_image_down: float32 [1024, 1024], P(('gx', 'gy'))
- grad_image_gain_ffn: float32 [1024], P(('gx', 'gy'))
- grad_text_self: float32 [768, 2304], P(('gx', 'gy'))
- grad_text_mix: float32 [768, 768], P(('gx', 'gy'))
- grad_text_gain_self: float32 [768], P(('gx', 'gy'))
- grad_image_self: float32 [1024, 3072], P(('gx', 'gy'))
- grad_image_mix: float32 [1024, 1024], P(('gx', 'gy'))
- grad_image_gain_self: float32 [1024], P(('gx', 'gy'))
The draws below stay inside these ranges and needn't reach their ends.
Inputs may be any that keep to these rules, and one draw needn't show every extreme that they name: `caption_lengths`: each caption has between 8 and 100 tokens; some caption has each of these two lengths.
All inputs are finite; a program needn't handle non-finite values. No bound on the sum of `region_mask` on one device may be relied on, other than what follows from the above.
Results may differ from the reference program's by a relative error of at most 0.024.
Values may be sent and summed in bfloat16 or wider, within the bound.
No kernel may reach another device: no remote copies, remote signals or barrier semaphores. Data moves between devices by JAX's collectives and lax.ppermute only.
A program may use at most 320 MiB of HBM per device.

```python
import math
import jax
import jax.numpy as jnp
from jax import lax

D = 768
VIS = 1024
INNER = 1024
HEADS = 8
FF = 3072
FFV = 1024
TEXT_HEADS = 12
IMAGE_HEADS = 8
TEXT = 100
REGIONS = 36
PAIR_DEV = 8
PAIRS = 256


def draw_caption_lengths(key, part):
    shortest = 1 + TEXT // 13
    drawn = jax.random.randint(key, (PAIRS,), shortest, TEXT + 1).astype(jnp.int32)
    return drawn.at[0].set(TEXT).at[1].set(shortest)


def with_ends(array, stream_key, smallest, high):
    longest = array.shape.index(max(array.shape))
    spots = []
    for shift in (0, 1):
        where = [jax.random.randint(jax.random.fold_in(stream_key, axis), (), 0, length) for axis, length in enumerate(array.shape)]
        where[longest] = (where[longest] + shift) % array.shape[longest]
        spots.append(tuple(where))
    return array.at[spots[0]].set(smallest).at[spots[1]].set(high)


def raised(values, own_key, source, target, parts, factor):
    def block_of(dim):
        return (jnp.arange(values.shape[dim]) // (values.shape[dim] // parts)).reshape((-1,) + (1,) * (values.ndim - 1 - dim))

    first = jax.random.permutation(own_key, parts)[block_of(target)]
    other_side = (block_of(target) + parts // 2) % parts
    return jnp.where((block_of(source) == first) | (block_of(source) == other_side), factor * values, values)


def block_scale(key, dims, cuts, smallest, high):
    def one(axis_at, blocks):
        heights = jax.random.uniform(jax.random.fold_in(jax.random.fold_in(key, 6), axis_at), (blocks,), jnp.float32, smallest / len(cuts), high / len(cuts))
        return jnp.repeat(jnp.exp(heights), dims[axis_at] // blocks).reshape((-1,) + (1,) * (len(dims) - axis_at - 1))

    factor_of = one(*cuts[0])
    for cut in cuts[1:]:
        factor_of = factor_of * one(*cut)
    return factor_of


def bell_draw(own_key, shape, scale, most, cuts=(), kind=jnp.bfloat16):
    values = jax.random.normal(own_key, shape, jnp.float32) * scale
    if len(cuts) > 0:
        values = block_scale(own_key, shape, cuts, -0.22, 0.18) * values
    return jnp.clip(values, min=-most, max=most).astype(kind)


def bell_draw_with(rng, extent, scale, limit, cuts, heavy, dtype=jnp.bfloat16):
    values = scale * jax.random.normal(rng, extent, jnp.float32)
    if cuts:
        values = values * block_scale(rng, extent, cuts, -0.22, 0.18)
    return jnp.clip(raised(values, jax.random.fold_in(rng, 3), *heavy), -limit, limit).astype(dtype)


def setup_inputs(seed: int = 0) -> dict:
    key_of = jax.random.split(jax.random.key(seed), 31)
    text_tokens = bell_draw(key_of[0], (PAIRS, TEXT, D), 1.0, 6.0, ((0, 32),))
    image_regions = bell_draw(key_of[1], (PAIRS, REGIONS, VIS), 1.0, 6.0, ((0, 32),))
    caption_lengths = draw_caption_lengths(jax.random.fold_in(key_of[30], 71), 0)
    region_mask = with_ends((jax.random.randint(key_of[3], (PAIRS, REGIONS), 0, 4) < 3).astype(jnp.int32), jax.random.fold_in(key_of[3], 1), 0, 1)
    text_cotangent = bell_draw_with(key_of[4], (PAIRS, TEXT, D), 1.0, 6.0, ((0, 32),), (0, 2, 32, 2.75))
    image_cotangent = bell_draw(key_of[5], (PAIRS, REGIONS, VIS), 1.0, 6.0, ((0, 32),))
    text_query = bell_draw(key_of[6], (D, INNER), D ** -0.5, 0.21875, ((0, 32),))
    image_key = bell_draw(key_of[7], (VIS, INNER), VIS ** -0.5, 0.1875, ((0, 32),))
    image_value = bell_draw(key_of[8], (VIS, INNER), VIS ** -0.5, 0.1875, ((0, 32),))
    text_merge = bell_draw(key_of[9], (INNER, D), (INNER // 25) ** -0.5, 1.0, ((0, 32),))
    text_gain_cross = jnp.clip(1.0 + 0.1 * jax.random.normal(key_of[10], (D,), jnp.float32), 0.5, 1.5).astype(jnp.bfloat16)
    image_query = bell_draw(key_of[11], (VIS, INNER), VIS ** -0.5, 0.1875, ((0, 32),))
    text_key = bell_draw(key_of[12], (D, INNER), D ** -0.5, 0.21875, ((0, 32),))
    text_value = bell_draw(key_of[13], (D, INNER), D ** -0.5, 0.21875, ((0, 32),))
    image_merge = bell_draw(key_of[14], (INNER, VIS), (INNER // 49) ** -0.5, 1.25, ((0, 32),))
    image_gain_cross = jnp.clip(1.0 + 0.1 * jax.random.normal(key_of[15], (VIS,), jnp.float32), 0.5, 1.5).astype(jnp.bfloat16)
    text_up = bell_draw(key_of[16], (D, FF), D ** -0.5, 0.21875, ((0, 32),))
    text_bias = bell_draw(key_of[17], (FF,), 0.5, 3.0, ((0, 32),))
    text_down = bell_draw(key_of[18], (FF, D), FF ** -0.5, 0.109375, ((0, 32),))
    text_gain_ffn = jnp.clip(1.0 + 0.1 * jax.random.normal(key_of[19], (D,), jnp.float32), 0.5, 1.5).astype(jnp.bfloat16)
    image_up = bell_draw(key_of[20], (VIS, FFV), VIS ** -0.5, 0.1875, ((0, 32),))
    image_bias = bell_draw(key_of[21], (FFV,), 0.5, 3.0, ((0, 32),))
    image_down = bell_draw(key_of[22], (FFV, VIS), FFV ** -0.5, 0.1875, ((0, 32),))
    image_gain_ffn = jnp.clip(1.0 + 0.1 * jax.random.normal(key_of[23], (VIS,), jnp.float32), 0.5, 1.5).astype(jnp.bfloat16)
    text_self = bell_draw(key_of[24], (D, 3 * D), D ** -0.5, 0.21875, ((0, 32),))
    text_mix = bell_draw(key_of[25], (D, D), (D // 49) ** -0.5, 1.5, ((0, 32),))
    text_gain_self = jnp.clip(1.0 + 0.1 * jax.random.normal(key_of[26], (D,), jnp.float32), 0.5, 1.5).astype(jnp.bfloat16)
    image_self = bell_draw(key_of[27], (VIS, 3 * VIS), VIS ** -0.5, 0.1875, ((0, 32),))
    image_mix = bell_draw(key_of[28], (VIS, VIS), (VIS // 25) ** -0.5, 1.0, ((0, 32),))
    image_gain_self = jnp.clip(1.0 + 0.1 * jax.random.normal(key_of[29], (VIS,), jnp.float32), 0.5, 1.5).astype(jnp.bfloat16)
    return {"text_tokens": text_tokens, "image_regions": image_regions, "caption_lengths": caption_lengths, "region_mask": region_mask, "text_cotangent": text_cotangent, "image_cotangent": image_cotangent, "text_query": text_query, "image_key": image_key, "image_value": image_value, "text_merge": text_merge, "text_gain_cross": text_gain_cross, "image_query": image_query, "text_key": text_key, "text_value": text_value, "image_merge": image_merge, "image_gain_cross": image_gain_cross, "text_up": text_up, "text_bias": text_bias, "text_down": text_down, "text_gain_ffn": text_gain_ffn, "image_up": image_up, "image_bias": image_bias, "image_down": image_down, "image_gain_ffn": image_gain_ffn, "text_self": text_self, "text_mix": text_mix, "text_gain_self": text_gain_self, "image_self": image_self, "image_mix": image_mix, "image_gain_self": image_gain_self}


EPSILON = 1e-05
MASKED = -1000000000.0
PRECISE = lax.Precision.HIGHEST

@jax.custom_vjp
def low(v):
    return lax.optimization_barrier(v.astype(jnp.bfloat16)).astype(jnp.float32)

@jax.custom_vjp
def low_back(v):
    return v

def low_keep(v):
    return (low(v), None)

def low_pass(kept, grad):
    return (grad,)

def back_keep(v):
    return (v, None)

def back_low(kept, grad):
    return (low(grad),)
low.defvjp(low_keep, low_pass)
low_back.defvjp(back_keep, back_low)

def matmul(left, right):
    return jnp.dot(left, right, precision=PRECISE)

def rounded_product(rows, weight):
    return low_back(low(matmul(rows, weight)))

def norm_rows(values_in, gain_vec):
    centred = values_in - lax.optimization_barrier(jnp.mean(values_in, -1, keepdims=True))
    spread = lax.optimization_barrier(jnp.mean(centred * centred, -1, keepdims=True))
    return centred * lax.rsqrt(spread + EPSILON) * gain_vec

def attention(queries, keys, values, live, heads):
    groups = live.shape[0]
    size = queries.shape[1] // heads
    query_heads = queries.reshape(groups, -1, heads, size)
    key_heads = keys.reshape(groups, -1, heads, size)
    value_heads = values.reshape(groups, -1, heads, size)
    scores = low_back(jnp.einsum('bqhd,bkhd->bhqk', query_heads, key_heads, precision=PRECISE) * (1.0 / math.sqrt(size)))
    scores = jnp.where(live[:, None, None, :], scores, MASKED)
    probs = low(jax.nn.softmax(scores, axis=-1))
    mixed = jnp.einsum('bhqk,bkhd->bqhd', probs, value_heads, precision=PRECISE)
    return low_back(low(mixed.reshape(queries.shape)))

def feed(normed, up_weight, bias_vec, down_weight):
    hidden = low_back(matmul(low(normed), up_weight) + bias_vec)
    return low_back(matmul(low(jax.nn.gelu(hidden, approximate=True)), down_weight))

def self_branch(normed, joint_weight, mix_weight, live, heads):
    width = normed.shape[1]
    triple = rounded_product(low(normed), joint_weight)
    mixed = attention(triple[:, :width], triple[:, width:2 * width], triple[:, 2 * width:], live, heads)
    return low_back(matmul(mixed, mix_weight))

def forward(text_block, image_block, params, text_live, image_live):
    text_query, image_key, image_value, text_merge, text_gain_cross, image_query, text_key, text_value, image_merge, image_gain_cross, text_up, text_bias, text_down, text_gain_ffn, image_up, image_bias, image_down, image_gain_ffn, text_self, text_mix, text_gain_self, image_self, image_mix, image_gain_self = params
    groups = text_block.shape[0]
    text_rows = text_block.reshape(groups * TEXT, D)
    image_rows = image_block.reshape(groups * REGIONS, VIS)
    cross_text = attention(rounded_product(text_rows, text_query), rounded_product(image_rows, image_key), rounded_product(image_rows, image_value), image_live, HEADS)
    cross_image = attention(rounded_product(image_rows, image_query), rounded_product(text_rows, text_key), rounded_product(text_rows, text_value), text_live, HEADS)
    first_text = norm_rows(text_rows + low_back(matmul(cross_text, text_merge)), text_gain_cross)
    first_image = norm_rows(image_rows + low_back(matmul(cross_image, image_merge)), image_gain_cross)
    second_text = norm_rows(first_text + feed(first_text, text_up, text_bias, text_down), text_gain_ffn)
    second_image = norm_rows(first_image + feed(first_image, image_up, image_bias, image_down), image_gain_ffn)
    text_keep = text_live.astype(jnp.float32).reshape(-1, 1)
    image_keep = image_live.astype(jnp.float32).reshape(-1, 1)
    text_out = norm_rows(second_text + self_branch(second_text, text_self, text_mix, text_live, TEXT_HEADS), text_gain_self) * text_keep
    image_out = norm_rows(second_image + self_branch(second_image, image_self, image_mix, image_live, IMAGE_HEADS), image_gain_self) * image_keep
    return (text_out, image_out)

def reference(text_tokens, image_regions, caption_lengths, region_mask, text_cotangent, image_cotangent, text_query, image_key, image_value, text_merge, text_gain_cross, image_query, text_key, text_value, image_merge, image_gain_cross, text_up, text_bias, text_down, text_gain_ffn, image_up, image_bias, image_down, image_gain_ffn, text_self, text_mix, text_gain_self, image_self, image_mix, image_gain_self):
    params = tuple((weight.astype(jnp.float32) for weight in (text_query, image_key, image_value, text_merge, text_gain_cross, image_query, text_key, text_value, image_merge, image_gain_cross, text_up, text_bias, text_down, text_gain_ffn, image_up, image_bias, image_down, image_gain_ffn, text_self, text_mix, text_gain_self, image_self, image_mix, image_gain_self)))
    group_size = PAIR_DEV * 4
    group_count = PAIRS // group_size

    def split_groups(array_in):
        return array_in.reshape((group_count, group_size) + array_in.shape[1:])

    def one_group(totals, pieces):
        text_block, image_block, length_block, live_block, text_cot, image_cot = pieces
        text_live = jnp.arange(TEXT)[None, :] < length_block[:, None]
        image_live = live_block > 0

        def through(text_in, image_in, *weights_in):
            return forward(text_in, image_in, weights_in, text_live, image_live)
        result, pullback = jax.vjp(through, text_block.astype(jnp.float32), image_block.astype(jnp.float32), *params)
        gradients = pullback((text_cot.astype(jnp.float32).reshape(group_size * TEXT, D), image_cot.astype(jnp.float32).reshape(group_size * REGIONS, VIS)))
        totals = tuple((summed + piece_grad for summed, piece_grad in zip(totals, gradients[2:])))
        return (totals, (result[0].reshape(group_size, TEXT, D).astype(jnp.bfloat16), result[1].reshape(group_size, REGIONS, VIS).astype(jnp.bfloat16), gradients[0], gradients[1]))
    initial = tuple((jnp.zeros_like(weight) for weight in params))
    sums, stacked = lax.scan(one_group, initial, (split_groups(text_tokens), split_groups(image_regions), split_groups(caption_lengths), split_groups(region_mask), split_groups(text_cotangent), split_groups(image_cotangent)))
    text_output = stacked[0].reshape(PAIRS, TEXT, D)
    image_output = stacked[1].reshape(PAIRS, REGIONS, VIS)
    grad_text = stacked[2].reshape(PAIRS, TEXT, D)
    grad_image = stacked[3].reshape(PAIRS, REGIONS, VIS)
    return (text_output, image_output, grad_text, grad_image, sums[0], sums[1], sums[2], sums[3], sums[4], sums[5], sums[6], sums[7], sums[8], sums[9], sums[10], sums[11], sums[12], sums[13], sums[14], sums[15], sums[16], sums[17], sums[18], sums[19], sums[20], sums[21], sums[22], sums[23])
```

```python
import functools
import math

import jax
import jax.numpy as jnp
from jax import lax
from jax.experimental import pallas as pl
from jax.experimental.pallas import tpu as pltpu
from jax.sharding import PartitionSpec as P

HEADS = 8
TEXT_HEADS = 12
IMAGE_HEADS = 8
EPSILON = 1e-05
MASKED = -1000000000.0
PADDED = -2000000000.0
LANES = 128
AXES = ("gx", "gy")
F32 = jnp.float32
BF16 = jnp.bfloat16
VECTOR_NAMES = (
    "text_gain_cross",
    "image_gain_cross",
    "text_bias",
    "text_gain_ffn",
    "image_bias",
    "image_gain_ffn",
    "text_gain_self",
    "image_gain_self",
)


def project(left, right):
    return jnp.dot(left, right, preferred_element_type=F32)


def project_back(left, right):
    return lax.dot_general(left, right, (((1,), (1,)), ((), ())), preferred_element_type=F32)


def weight_grad(left, right):
    return lax.dot_general(left, right, (((0,), (0,)), ((), ())), preferred_element_type=F32)


def round_up(size, step):
    return -(-size // step) * step


def stack_halves(rows):
    wide = rows.astype(F32)
    first = lax.broadcasted_iota(jnp.int32, wide.shape, 1) < LANES // 2
    zero = jnp.zeros_like(wide)
    return jnp.concatenate([jnp.where(first, wide, zero), jnp.where(first, zero, wide)], 0).astype(BF16)


def join_halves(rows):
    count = rows.shape[0] // 2
    first = lax.broadcasted_iota(jnp.int32, (count, LANES), 1) < LANES // 2
    return jnp.where(first, rows[:count], rows[count:])


def softmax_rows(queries, keys, fill, scale):
    scores = project_back(queries, keys) * scale
    scores = jnp.where(fill < 0.0, fill, scores)
    powers = jnp.exp(scores - jnp.max(scores, -1, keepdims=True))
    return powers / jnp.sum(powers, -1, keepdims=True)


def head_forward(queries, keys, values, fill, size):
    scale = 1.0 / math.sqrt(size)
    split = size < LANES
    probs = softmax_rows(stack_halves(queries) if split else queries, keys, fill, scale)
    mixed = project(probs.astype(BF16), values)
    return (join_halves(mixed) if split else mixed).astype(BF16)


def head_backward(queries, keys, values, fill, size, d_mixed):
    scale = 1.0 / math.sqrt(size)
    split = size < LANES
    if split:
        queries, d_mixed = stack_halves(queries), stack_halves(d_mixed)
    probs = softmax_rows(queries, keys, fill, scale)
    d_probs = project_back(d_mixed, values)
    d_values = weight_grad(probs.astype(BF16), d_mixed)
    d_scores = probs * (d_probs - jnp.sum(probs * d_probs, -1, keepdims=True))
    d_scores = jnp.where(fill < 0.0, 0.0, d_scores).astype(BF16)
    d_queries = project(d_scores, keys) * scale
    d_keys = weight_grad(d_scores, queries) * scale
    if split:
        d_queries = join_halves(d_queries)
    return d_queries.astype(BF16), d_keys.astype(BF16), d_values.astype(BF16)


def lane_blocks(width):
    return [slice(at, at + LANES) for at in range(0, width, LANES)]


def shifted(block, by):
    return slice(block.start + by, block.stop + by)


def cross_forward_kernel(size, text_ref, image_ref, text_fill_ref, image_fill_ref, mixed_text_ref, mixed_image_ref):
    width = text_ref.shape[-1] // 3
    text_fill, image_fill = text_fill_ref[0], image_fill_ref[0]
    for own in lane_blocks(width):
        key, value = shifted(own, width), shifted(own, 2 * width)
        mixed_text_ref[0, :, own] = head_forward(
            text_ref[0, :, own], image_ref[0, :, key], image_ref[0, :, value], image_fill, size
        )
        mixed_image_ref[0, :, own] = head_forward(
            image_ref[0, :, own], text_ref[0, :, key], text_ref[0, :, value], text_fill, size
        )


def cross_backward_kernel(
    size, text_ref, image_ref, text_fill_ref, image_fill_ref, d_text_ref, d_image_ref, out_text_ref, out_image_ref
):
    width = text_ref.shape[-1] // 3
    text_fill, image_fill = text_fill_ref[0], image_fill_ref[0]
    for own in lane_blocks(width):
        key, value = shifted(own, width), shifted(own, 2 * width)
        d_query, d_key, d_value = head_backward(
            text_ref[0, :, own], image_ref[0, :, key], image_ref[0, :, value], image_fill, size, d_text_ref[0, :, own]
        )
        out_text_ref[0, :, own] = d_query
        out_image_ref[0, :, key] = d_key
        out_image_ref[0, :, value] = d_value
        d_query, d_key, d_value = head_backward(
            image_ref[0, :, own], text_ref[0, :, key], text_ref[0, :, value], text_fill, size, d_image_ref[0, :, own]
        )
        out_image_ref[0, :, own] = d_query
        out_text_ref[0, :, key] = d_key
        out_text_ref[0, :, value] = d_value


def self_forward_kernel(size, triple_ref, fill_ref, mixed_ref):
    width = triple_ref.shape[-1] // 3
    fill = fill_ref[0]
    for own in lane_blocks(width):
        key, value = shifted(own, width), shifted(own, 2 * width)
        mixed_ref[0, :, own] = head_forward(
            triple_ref[0, :, own], triple_ref[0, :, key], triple_ref[0, :, value], fill, size
        )


def self_backward_kernel(size, triple_ref, fill_ref, d_mixed_ref, out_ref):
    width = triple_ref.shape[-1] // 3
    fill = fill_ref[0]
    for own in lane_blocks(width):
        key, value = shifted(own, width), shifted(own, 2 * width)
        d_query, d_key, d_value = head_backward(
            triple_ref[0, :, own], triple_ref[0, :, key], triple_ref[0, :, value], fill, size, d_mixed_ref[0, :, own]
        )
        out_ref[0, :, own] = d_query
        out_ref[0, :, key] = d_key
        out_ref[0, :, value] = d_value


def per_pair(kernel, inputs, out_widths, flops):
    pairs = inputs[0].shape[0]

    def spec(rows, width):
        return pl.BlockSpec((1, rows, width), lambda pair: (pair, 0, 0))

    moved = sum(array.size * array.dtype.itemsize for array in inputs)
    moved += sum(pairs * rows * width * 2 for rows, width in out_widths)
    return pl.pallas_call(
        kernel,
        grid=(pairs,),
        in_specs=[spec(*array.shape[1:]) for array in inputs],
        out_specs=[spec(rows, width) for rows, width in out_widths],
        out_shape=[jax.ShapeDtypeStruct((pairs, rows, width), BF16) for rows, width in out_widths],
        compiler_params=pltpu.CompilerParams(vmem_limit_bytes=48 * 1024 * 1024),
        cost_estimate=pl.CostEstimate(flops=flops, bytes_accessed=moved, transcendentals=0),
    )(*inputs)


def beside(array, parts):
    rows, width = array.shape
    return jnp.concatenate([array[at * (rows // parts) : (at + 1) * (rows // parts)] for at in range(parts)], 1)


def gather(packed):
    return lax.all_gather(packed, AXES, axis=0, tiled=False)


def whole(block, parts=1):
    devices, rows, width = block.shape
    if parts > 1:
        block = block.reshape(devices, rows, parts, width // parts).transpose(0, 2, 1, 3)
    return block.reshape(devices * rows * parts, width // parts)


def owned_rows(matrix, devices, parts=1):
    rows, width = matrix.shape
    rows //= devices
    if parts == 1:
        return matrix.reshape(devices, rows, width)
    block = matrix.reshape(devices, parts, rows // parts, width).transpose(0, 2, 1, 3)
    return block.reshape(devices, rows // parts, parts * width)


def mesh_bits(sizes):
    bits = []
    for axis in AXES:
        bits += [(axis, bit) for bit in reversed(range(sizes[axis].bit_length() - 1))]
    return bits


def halve(total, bits, which):
    axis, bit = which
    place = bits.index(which)
    own = (lax.axis_index(axis) >> bit) & 1
    count = lax.axis_size(axis)
    away = lax.dynamic_index_in_dim(total, 1 - own, place, keepdims=False)
    kept = lax.dynamic_index_in_dim(total, own, place, keepdims=False)
    got = lax.ppermute(away, axis, [(at, at ^ (1 << bit)) for at in range(count)])
    left = [one for one in bits if one != which]
    return kept.astype(F32) + got.astype(F32), left


def sum_to_owners(packed, sizes):
    bits = mesh_bits(sizes)
    low = (sizes["gy"].bit_length() - 1) // 2
    core = [("gx", 0)] if sizes["gx"] > 1 else []
    rows = [one for one in bits if one[0] == "gx" and one not in core]
    columns = [one for one in bits if one[0] == "gy" and one[1] < low]
    rest = [one for one in bits if one[0] == "gy" and one[1] >= low]
    width = packed.shape[-1]
    total = packed.reshape((2,) * len(bits) + packed.shape[1:])
    for which in core:
        total, bits = halve(total, bits, which)
        total = total.astype(BF16)
    halves = []
    for part, order in ((0, columns + rows), (1, rows + columns)):
        part_total, part_bits = total[..., part * width // 2 : (part + 1) * width // 2], bits
        for which in order:
            part_total, part_bits = halve(part_total, part_bits, which)
            part_total = part_total.astype(BF16)
        halves.append(part_total)
    total, bits = jnp.concatenate(halves, -1), part_bits
    for which in rest:
        total, bits = halve(total.astype(BF16), bits, which)
    return total.astype(F32)


def normed_rows(values_in):
    centred = values_in - jnp.mean(values_in, -1, keepdims=True)
    rate = lax.rsqrt(jnp.mean(centred * centred, -1, keepdims=True) + EPSILON)
    return centred * rate, rate


def normed_back(unit, rate, gain, d_out):
    d_unit = d_out * gain
    mean_unit = jnp.mean(d_unit, -1, keepdims=True)
    mean_cross = jnp.mean(d_unit * unit, -1, keepdims=True)
    return rate * (d_unit - mean_unit - unit * mean_cross), jnp.sum(d_out * unit, 0)


GELU_RATE = math.sqrt(2.0 / math.pi)
GELU_CUBE = 0.044715


def gelu(values_in):
    inner = jnp.tanh(GELU_RATE * (values_in + GELU_CUBE * values_in * values_in * values_in))
    return 0.5 * values_in * (1.0 + inner)


def gelu_slope(values_in):
    square = values_in * values_in
    inner = jnp.tanh(GELU_RATE * values_in * (1.0 + GELU_CUBE * square))
    return 0.5 * (1.0 + inner) + 0.5 * values_in * (1.0 - inner * inner) * GELU_RATE * (1.0 + 3.0 * GELU_CUBE * square)


def per_device(sizes, *given):
    (
        text_tokens,
        image_regions,
        caption_lengths,
        region_mask,
        text_cotangent,
        image_cotangent,
        text_query,
        image_key,
        image_value,
        text_merge,
        text_gain_cross,
        image_query,
        text_key,
        text_value,
        image_merge,
        image_gain_cross,
        text_up,
        text_bias,
        text_down,
        text_gain_ffn,
        image_up,
        image_bias,
        image_down,
        image_gain_ffn,
        text_self,
        text_mix,
        text_gain_self,
        image_self,
        image_mix,
        image_gain_self,
    ) = given
    devices = sizes["gx"] * sizes["gy"]
    pairs, length, text_width = text_tokens.shape
    regions, image_width = image_regions.shape[1:]
    inner = text_query.shape[1]

    vectors = (
        text_gain_cross,
        image_gain_cross,
        text_bias,
        text_gain_ffn,
        image_bias,
        image_gain_ffn,
        text_gain_self,
        image_gain_self,
    )
    vector = jnp.concatenate(vectors)
    half_rows = image_merge.shape[0] // 2
    row_text, row_image = text_query.shape[0], image_query.shape[0]
    merge_rows = text_merge.shape[0] // 4
    vector_block = jnp.pad(vector[None, :], ((0, half_rows - 1), (0, image_width - vector.shape[0])))
    packed_cross = jnp.concatenate(
        [
            jnp.concatenate([text_query, text_key, text_value], 1),
            jnp.concatenate([image_query, image_key, image_value], 1),
            jnp.concatenate([beside(image_merge, 2), vector_block], 1),
            beside(text_merge, 4),
        ],
        0,
    )
    packed_text = jnp.concatenate([text_up, beside(text_down, 4), jnp.concatenate([text_self, text_mix], 1)], 0)
    packed_image = jnp.concatenate([image_self, jnp.concatenate([image_up, image_down, image_mix], 1)], 0)
    all_cross = gather(packed_cross)
    all_text = gather(packed_text)
    all_image = gather(packed_image)

    at = row_text
    weight_text = whole(all_cross[:, :at])
    weight_image = whole(all_cross[:, at : at + row_image])
    at += row_image
    full_image_merge = whole(all_cross[:, at : at + half_rows, : 2 * image_width], 2)
    all_vectors = all_cross[:, at, 2 * image_width :]
    at += half_rows
    full_text_merge = whole(all_cross[:, at : at + merge_rows], 4)
    full = {}
    at = 0
    for name, piece in zip(VECTOR_NAMES, vectors):
        full[name] = all_vectors[:, at : at + piece.shape[0]].reshape(-1).astype(F32)
        at += piece.shape[0]
    full_text_up = whole(all_text[:, :row_text])
    full_text_down = whole(all_text[:, row_text : 2 * row_text], 4)
    full_text_self = whole(all_text[:, 2 * row_text :, : 3 * text_width])
    full_text_mix = whole(all_text[:, 2 * row_text :, 3 * text_width :])
    full_image_self = whole(all_image[:, :row_image])
    full_image_up = whole(all_image[:, row_image:, :image_width])
    full_image_down = whole(all_image[:, row_image:, image_width : 2 * image_width])
    full_image_mix = whole(all_image[:, row_image:, 2 * image_width :])

    text_slots, image_slots = round_up(length, 8), round_up(regions, 8)

    def padded(array, slots):
        array = jnp.pad(array, ((0, 0), (0, slots - array.shape[1]), (0, 0)))
        return array.reshape(pairs * slots, array.shape[2])

    def rows_of(array):
        return array.reshape(-1, array.shape[-1])

    def pairs_of(array):
        return array.reshape(pairs, array.shape[0] // pairs, array.shape[1])

    text_rows, image_rows = padded(text_tokens, text_slots), padded(image_regions, image_slots)
    d_text_out = padded(text_cotangent, text_slots).astype(F32)
    d_image_out = padded(image_cotangent, image_slots).astype(F32)
    text_at = jnp.arange(text_slots)[None, :]
    text_live = text_at < caption_lengths[:, None]
    image_live = jnp.pad(region_mask, ((0, 0), (0, image_slots - regions))) > 0
    text_fill = jnp.where(text_live, 0.0, jnp.where(text_at < length, MASKED, PADDED))[:, None, :]
    image_at = jnp.arange(image_slots)[None, :]
    image_fill = jnp.where(image_live, 0.0, jnp.where(image_at < regions, MASKED, PADDED))[:, None, :]
    text_keep = text_live.astype(F32).reshape(-1, 1)
    image_keep = image_live.astype(F32).reshape(-1, 1)

    triple_text = project(text_rows, weight_text).astype(BF16)
    triple_image = project(image_rows, weight_image).astype(BF16)
    cross_size = inner // HEADS
    cross_flops = 4 * pairs * text_slots * image_slots * inner * 2
    cross_text, cross_image = per_pair(
        functools.partial(cross_forward_kernel, cross_size),
        [pairs_of(triple_text), pairs_of(triple_image), text_fill, image_fill],
        [(text_slots, inner), (image_slots, inner)],
        cross_flops,
    )
    cross_text, cross_image = rows_of(cross_text), rows_of(cross_image)
    unit_text_1, rate_text_1 = normed_rows(text_rows.astype(F32) + project(cross_text, full_text_merge))
    unit_image_1, rate_image_1 = normed_rows(image_rows.astype(F32) + project(cross_image, full_image_merge))

    def stream(
        unit_1, rate_1, gain_1, up, bias, down, gain_2, joint, mix, gain_3, fill, keep, d_out, size, slots, flops
    ):
        width = unit_1.shape[1]
        first = unit_1 * gain_1
        first_low = first.astype(BF16)
        hidden = project(first_low, up) + bias
        active = gelu(hidden).astype(BF16)
        hidden = hidden.astype(BF16)
        unit_2, rate_2 = normed_rows(first + project(active, down))
        second = unit_2 * gain_2
        second_low = second.astype(BF16)
        triple = project(second_low, joint).astype(BF16)
        (mixed,) = per_pair(
            functools.partial(self_forward_kernel, size), [pairs_of(triple), fill], [(slots, width)], flops
        )
        mixed = rows_of(mixed)
        unit_3, rate_3 = normed_rows(second + project(mixed, mix))
        out = (unit_3 * gain_3 * keep).astype(BF16)

        d_third, g_gain_3 = normed_back(unit_3, rate_3, gain_3, d_out * keep)
        d_branch = d_third.astype(BF16)
        g_mix = weight_grad(mixed, d_branch).astype(BF16)
        d_mixed = project_back(d_branch, mix).astype(BF16)
        (d_triple,) = per_pair(
            functools.partial(self_backward_kernel, size),
            [pairs_of(triple), fill, pairs_of(d_mixed)],
            [(slots, 3 * width)],
            flops * 5 // 2,
        )
        d_triple = rows_of(d_triple)
        g_joint = weight_grad(second_low, d_triple).astype(BF16)
        d_second = d_third + project_back(d_triple, joint)
        d_sum, g_gain_2 = normed_back(unit_2, rate_2, gain_2, d_second)
        d_sum_low = d_sum.astype(BF16)
        g_down = weight_grad(active, d_sum_low).astype(BF16)
        d_hidden = (gelu_slope(hidden.astype(F32)) * project_back(d_sum_low, down)).astype(BF16)
        g_bias = jnp.sum(d_hidden.astype(F32), 0)
        g_up = weight_grad(first_low, d_hidden).astype(BF16)
        d_first = d_sum + project_back(d_hidden, up)
        d_resid, g_gain_1 = normed_back(unit_1, rate_1, gain_1, d_first)
        return out, d_resid, (g_mix, g_joint, g_down, g_up), (g_gain_1, g_bias, g_gain_2, g_gain_3)

    out_text, d_resid_text, (g_text_mix, g_text_self, g_text_down, g_text_up), vectors_text = stream(
        unit_text_1,
        rate_text_1,
        full["text_gain_cross"],
        full_text_up,
        full["text_bias"],
        full_text_down,
        full["text_gain_ffn"],
        full_text_self,
        full_text_mix,
        full["text_gain_self"],
        text_fill,
        text_keep,
        d_text_out,
        text_width // TEXT_HEADS,
        text_slots,
        4 * pairs * text_slots * text_slots * text_width * 2,
    )
    packed_text_grad = jnp.concatenate(
        [
            owned_rows(g_text_up, devices),
            owned_rows(g_text_down, devices, 4),
            jnp.concatenate([owned_rows(g_text_self, devices), owned_rows(g_text_mix, devices)], 2),
        ],
        1,
    )
    sum_text = sum_to_owners(packed_text_grad, sizes)
    out_image, d_resid_image, (g_image_mix, g_image_self, g_image_down, g_image_up), vectors_image = stream(
        unit_image_1,
        rate_image_1,
        full["image_gain_cross"],
        full_image_up,
        full["image_bias"],
        full_image_down,
        full["image_gain_ffn"],
        full_image_self,
        full_image_mix,
        full["image_gain_self"],
        image_fill,
        image_keep,
        d_image_out,
        image_width // IMAGE_HEADS,
        image_slots,
        4 * pairs * image_slots * image_slots * image_width,
    )
    packed_image_grad = jnp.concatenate(
        [
            owned_rows(g_image_self, devices),
            jnp.concatenate(
                [
                    owned_rows(g_image_up, devices),
                    owned_rows(g_image_down, devices),
                    owned_rows(g_image_mix, devices),
                ],
                2,
            ),
        ],
        1,
    )
    sum_image = sum_to_owners(packed_image_grad, sizes)

    d_merge_text = d_resid_text.astype(BF16)
    d_merge_image = d_resid_image.astype(BF16)
    g_text_merge = weight_grad(cross_text, d_merge_text).astype(BF16)
    g_image_merge = weight_grad(cross_image, d_merge_image).astype(BF16)
    d_heads_text = project_back(d_merge_text, full_text_merge).astype(BF16)
    d_heads_image = project_back(d_merge_image, full_image_merge).astype(BF16)
    d_triple_text, d_triple_image = per_pair(
        functools.partial(cross_backward_kernel, cross_size),
        [
            pairs_of(triple_text),
            pairs_of(triple_image),
            text_fill,
            image_fill,
            pairs_of(d_heads_text),
            pairs_of(d_heads_image),
        ],
        [(text_slots, 3 * inner), (image_slots, 3 * inner)],
        cross_flops * 5 // 2,
    )
    d_triple_text, d_triple_image = rows_of(d_triple_text), rows_of(d_triple_image)
    g_weight_text = weight_grad(text_rows, d_triple_text).astype(BF16)
    g_weight_image = weight_grad(image_rows, d_triple_image).astype(BF16)
    grad_text = d_resid_text + project_back(d_triple_text, weight_text)
    grad_image = d_resid_image + project_back(d_triple_image, weight_image)
    g_vectors = (
        vectors_text[0],
        vectors_image[0],
        vectors_text[1],
        vectors_text[2],
        vectors_image[1],
        vectors_image[2],
        vectors_text[3],
        vectors_image[3],
    )
    vector_rows = jnp.concatenate([piece.reshape(devices, -1) for piece in g_vectors], 1).astype(BF16)
    vector_rows = jnp.pad(
        vector_rows[:, None, :], ((0, 0), (0, half_rows - 1), (0, image_width - vector_rows.shape[1]))
    )
    packed_cross_grad = jnp.concatenate(
        [
            owned_rows(g_weight_text, devices),
            owned_rows(g_weight_image, devices),
            jnp.concatenate([owned_rows(g_image_merge, devices, 2), vector_rows], 2),
            owned_rows(g_text_merge, devices, 4),
        ],
        1,
    )
    sum_cross = sum_to_owners(packed_cross_grad, sizes)

    def apart(block, parts):
        return jnp.concatenate(jnp.split(block, parts, 1), 0)

    at = row_text
    sum_text_query, sum_text_key, sum_text_value = jnp.split(sum_cross[:at], 3, 1)
    sum_image_query, sum_image_key, sum_image_value = jnp.split(sum_cross[at : at + row_image], 3, 1)
    at += row_image
    sum_image_merge = apart(sum_cross[at : at + half_rows, : 2 * image_width], 2)
    sum_vectors = sum_cross[at, 2 * image_width :]
    at += half_rows
    sum_text_merge = apart(sum_cross[at:], 4)
    owned_vector = {}
    at = 0
    for name, piece in zip(VECTOR_NAMES, vectors):
        owned_vector[name] = sum_vectors[at : at + piece.shape[0]]
        at += piece.shape[0]
    return (
        pairs_of(out_text)[:, :length],
        pairs_of(out_image)[:, :regions],
        pairs_of(grad_text)[:, :length],
        pairs_of(grad_image)[:, :regions],
        sum_text_query,
        sum_image_key,
        sum_image_value,
        sum_text_merge,
        owned_vector["text_gain_cross"],
        sum_image_query,
        sum_text_key,
        sum_text_value,
        sum_image_merge,
        owned_vector["image_gain_cross"],
        sum_text[:row_text],
        owned_vector["text_bias"],
        apart(sum_text[row_text : 2 * row_text], 4),
        owned_vector["text_gain_ffn"],
        sum_image[row_image:, :image_width],
        owned_vector["image_bias"],
        sum_image[row_image:, image_width : 2 * image_width],
        owned_vector["image_gain_ffn"],
        sum_text[2 * row_text :, : 3 * text_width],
        sum_text[2 * row_text :, 3 * text_width :],
        owned_vector["text_gain_self"],
        sum_image[:row_image],
        sum_image[row_image:, 2 * image_width :],
        owned_vector["image_gain_self"],
    )


def solution(mesh):
    split = {1: P(AXES), 2: P(AXES, None), 3: P(AXES, None, None)}
    in_ranks = (3, 3, 1, 2, 3, 3) + tuple(
        1 if at in (4, 9, 11, 13, 15, 17, 20, 23) else 2 for at in range(24)
    )
    out_ranks = (3, 3, 3, 3) + in_ranks[6:]
    return jax.shard_map(
        functools.partial(per_device, dict(mesh.shape)),
        mesh=mesh,
        in_specs=tuple(split[rank] for rank in in_ranks),
        out_specs=tuple(split[rank] for rank in out_ranks),
        check_vma=False,
    )
```

```python
import functools
import math

import jax
import jax.numpy as jnp
from jax import lax
from jax.experimental import pallas as pl
from jax.experimental.pallas import tpu as pltpu
from jax.sharding import PartitionSpec as P

HEADS = 8
TEXT_HEADS = 12
IMAGE_HEADS = 8
EPSILON = 1e-05
MASKED = -1000000000.0
PADDED = -2000000000.0
LANES = 128
AXES = ("gx", "gy")
F32 = jnp.float32
BF16 = jnp.bfloat16
VMEM_BYTES = 48 * 1024 * 1024
VECTOR_NAMES = (
    "text_gain_cross",
    "image_gain_cross",
    "text_bias",
    "text_gain_ffn",
    "image_bias",
    "image_gain_ffn",
    "text_gain_self",
    "image_gain_self",
)


def project(left, right):
    return jnp.dot(left, right, preferred_element_type=F32)


def project_back(left, right):
    return lax.dot_general(left, right, (((1,), (1,)), ((), ())), preferred_element_type=F32)


def weight_grad(left, right):
    return lax.dot_general(left, right, (((0,), (0,)), ((), ())), preferred_element_type=F32)


def round_up(size, step):
    return -(-size // step) * step


def stack_halves(rows):
    wide = rows.astype(F32)
    first = lax.broadcasted_iota(jnp.int32, wide.shape, 1) < LANES // 2
    zero = jnp.zeros_like(wide)
    return jnp.concatenate([jnp.where(first, wide, zero), jnp.where(first, zero, wide)], 0).astype(BF16)


def join_halves(rows):
    count = rows.shape[0] // 2
    first = lax.broadcasted_iota(jnp.int32, (count, LANES), 1) < LANES // 2
    return jnp.where(first, rows[:count], rows[count:])


def probabilities(keys, queries, fill, scale):
    scores = project_back(keys, queries) * scale
    scores = jnp.where(fill < 0.0, fill, scores)
    powers = jnp.exp(scores - jnp.max(scores, 0, keepdims=True))
    return powers * (1.0 / jnp.sum(powers, 0, keepdims=True))


def head_blocks(queries_ref, size):
    count, _, width = queries_ref.shape
    return [(pair, slice(at, at + LANES)) for pair in range(count) for at in range(0, width, LANES)], size < LANES


def attend_kernel(size, queries_ref, keys_ref, values_ref, fill_ref, mixed_ref):
    scale = 1.0 / math.sqrt(size)
    blocks, split = head_blocks(queries_ref, size)
    queries = [stack_halves(queries_ref[p, :, b]) if split else queries_ref[p, :, b] for p, b in blocks]
    probs = [
        probabilities(keys_ref[p, :, b], query, fill_ref[p][:, :1], scale).astype(BF16)
        for (p, b), query in zip(blocks, queries)
    ]
    mixed = [weight_grad(prob, values_ref[p, :, b]) for (p, b), prob in zip(blocks, probs)]
    for (p, b), rows in zip(blocks, mixed):
        mixed_ref[p, :, b] = (join_halves(rows) if split else rows).astype(BF16)


def attend_back_kernel(
    size, queries_ref, keys_ref, values_ref, fill_ref, d_mixed_ref, d_queries_ref, d_keys_ref, d_values_ref
):
    scale = 1.0 / math.sqrt(size)
    blocks, split = head_blocks(queries_ref, size)
    fills = [fill_ref[p][:, :1] for p, _ in blocks]
    queries = [stack_halves(queries_ref[p, :, b]) if split else queries_ref[p, :, b] for p, b in blocks]
    grads = [stack_halves(d_mixed_ref[p, :, b]) if split else d_mixed_ref[p, :, b] for p, b in blocks]
    probs = [
        probabilities(keys_ref[p, :, b], query, fill, scale) for (p, b), query, fill in zip(blocks, queries, fills)
    ]
    d_probs = [project_back(values_ref[p, :, b], grad) for (p, b), grad in zip(blocks, grads)]
    for (p, b), prob, grad in zip(blocks, probs, grads):
        d_values_ref[p, :, b] = project(prob.astype(BF16), grad).astype(BF16)
    d_scores = [
        prob * (d_prob - jnp.sum(prob * d_prob, 0, keepdims=True)) for prob, d_prob in zip(probs, d_probs)
    ]
    d_scores = [jnp.where(fill < 0.0, 0.0, one).astype(BF16) for fill, one in zip(fills, d_scores)]
    for (p, b), one, query in zip(blocks, d_scores, queries):
        d_keys_ref[p, :, b] = (project(one, query) * scale).astype(BF16)
    for (p, b), one in zip(blocks, d_scores):
        rows = weight_grad(one, keys_ref[p, :, b]) * scale
        d_queries_ref[p, :, b] = (join_halves(rows) if split else rows).astype(BF16)


def attention_call(kernel, together, inputs, outputs, flops):
    pairs = inputs[0][0].shape[0]
    together = math.gcd(pairs, together)

    def spec(rows, width, column):
        return pl.BlockSpec((together, rows, width), lambda step: (step, 0, column))

    moved = sum(pairs * array.shape[1] * width * array.dtype.itemsize for array, width, _ in inputs)
    moved += sum(pairs * rows * width * 2 for rows, width in outputs)
    return pl.pallas_call(
        kernel,
        grid=(pairs // together,),
        in_specs=[spec(array.shape[1], width, column) for array, width, column in inputs],
        out_specs=[spec(rows, width, 0) for rows, width in outputs],
        out_shape=[jax.ShapeDtypeStruct((pairs, rows, width), BF16) for rows, width in outputs],
        compiler_params=pltpu.CompilerParams(vmem_limit_bytes=VMEM_BYTES),
        cost_estimate=pl.CostEstimate(flops=flops, bytes_accessed=moved, transcendentals=0),
    )(*[array for array, _, _ in inputs])


def attend(queries, keys, values, fill, width, heads):
    pairs, count = queries[0].shape[:2]
    inputs = [(array, width, column) for array, column in (queries, keys, values)] + [(fill, LANES, 0)]
    flops = 4 * pairs * count * keys[0].shape[1] * max(width, heads * LANES)
    kernel = functools.partial(attend_kernel, width // heads)
    return attention_call(kernel, 4, inputs, [(count, width)], flops)[0]


def attend_back(queries, keys, values, fill, d_mixed, width, heads):
    pairs, count = queries[0].shape[:2]
    inputs = [(array, width, column) for array, column in (queries, keys, values)]
    inputs += [(fill, LANES, 0), (d_mixed, width, 0)]
    keyed = keys[0].shape[1]
    flops = 10 * pairs * count * keyed * max(width, heads * LANES)
    kernel = functools.partial(attend_back_kernel, width // heads)
    return attention_call(kernel, 2, inputs, [(count, width), (keyed, width), (keyed, width)], flops)


def tie(*values):
    return lax.optimization_barrier(values)


def gather(packed):
    return lax.all_gather(packed, AXES, axis=0, tiled=False)


def whole(block):
    return block.reshape(-1, block.shape[-1])


def owned_rows(matrix, devices):
    return matrix.reshape(devices, matrix.shape[0] // devices, matrix.shape[1])


def mesh_bits(sizes):
    bits = []
    for axis in AXES:
        bits += [(axis, bit) for bit in reversed(range(sizes[axis].bit_length() - 1))]
    return bits


class OwnerSum:
    def __init__(self, packed, sizes):
        bits = mesh_bits(sizes)
        low = (sizes["gy"].bit_length() - 1) // 2
        core = [("gx", 0)] if sizes["gx"] > 1 else []
        rows = [one for one in bits if one[0] == "gx" and one not in core]
        columns = [one for one in bits if one[0] == "gy" and one[1] < low]
        rest = [one for one in bits if one[0] == "gy" and one[1] >= low]
        self.width = packed.shape[-1]
        self.parts = [(packed.reshape((2,) * len(bits) + packed.shape[1:]), bits)]
        self.plan = [[which] for which in core]
        self.plan += [list(pair) for pair in zip(columns + rows, rows + columns)]
        self.plan += [[which] for which in rest]
        self.flying = None

    def advance(self, *others):
        if self.flying is not None:
            last = not self.plan
            self.parts = [
                ((kept.astype(F32) + got.astype(F32)).astype(F32 if last else BF16), bits)
                for kept, got, bits in self.flying
            ]
            self.flying = None
        if self.plan:
            step = self.plan.pop(0)
            if len(step) == 2 and len(self.parts) == 1:
                total, bits = self.parts[0]
                self.parts = [(total[..., : self.width // 2], bits), (total[..., self.width // 2 :], bits)]
            if len(step) == 1 and len(self.parts) == 2:
                self.parts = [(jnp.concatenate([self.parts[0][0], self.parts[1][0]], -1), self.parts[0][1])]
            sends = []
            for (total, bits), (axis, bit) in zip(self.parts, step):
                place = bits.index((axis, bit))
                own = (lax.axis_index(axis) >> bit) & 1
                away = lax.dynamic_index_in_dim(total, 1 - own, place, keepdims=False)
                kept = lax.dynamic_index_in_dim(total, own, place, keepdims=False)
                sends.append((away, kept, axis, bit, [one for one in bits if one != (axis, bit)]))
            held = tie(*[one[0] for one in sends], *others)
            others = held[len(sends) :]
            self.flying = []
            for away, (_, kept, axis, bit, left) in zip(held, sends):
                count = lax.axis_size(axis)
                got = lax.ppermute(away, axis, [(at, at ^ (1 << bit)) for at in range(count)])
                self.flying.append((kept, got, left))
        return others[0] if len(others) == 1 else others

    def result(self):
        while self.plan or self.flying is not None:
            self.advance()
        return self.parts[0][0].astype(F32)


def normed_rows(values_in):
    centred = values_in - jnp.mean(values_in, -1, keepdims=True)
    rate = lax.rsqrt(jnp.mean(centred * centred, -1, keepdims=True) + EPSILON)
    return centred * rate, rate


def normed_back(unit, rate, gain, d_out):
    d_unit = d_out * gain
    mean_unit = jnp.mean(d_unit, -1, keepdims=True)
    mean_cross = jnp.mean(d_unit * unit, -1, keepdims=True)
    return rate * (d_unit - mean_unit - unit * mean_cross), jnp.sum(d_out * unit, 0)


GELU_RATE = math.sqrt(2.0 / math.pi)
GELU_CUBE = 0.044715


def gelu(values_in):
    inner = jnp.tanh(GELU_RATE * (values_in + GELU_CUBE * values_in * values_in * values_in))
    return 0.5 * values_in * (1.0 + inner)


def gelu_slope(values_in):
    square = values_in * values_in
    inner = jnp.tanh(GELU_RATE * values_in * (1.0 + GELU_CUBE * square))
    return 0.5 * (1.0 + inner) + 0.5 * values_in * (1.0 - inner * inner) * GELU_RATE * (1.0 + 3.0 * GELU_CUBE * square)


def per_device(sizes, *given):
    (
        text_tokens,
        image_regions,
        caption_lengths,
        region_mask,
        text_cotangent,
        image_cotangent,
        text_query,
        image_key,
        image_value,
        text_merge,
        text_gain_cross,
        image_query,
        text_key,
        text_value,
        image_merge,
        image_gain_cross,
        text_up,
        text_bias,
        text_down,
        text_gain_ffn,
        image_up,
        image_bias,
        image_down,
        image_gain_ffn,
        text_self,
        text_mix,
        text_gain_self,
        image_self,
        image_mix,
        image_gain_self,
    ) = given
    devices = sizes["gx"] * sizes["gy"]
    pairs, length, text_width = text_tokens.shape
    regions, image_width = image_regions.shape[1:]
    inner = text_query.shape[1]

    vectors = (
        text_gain_cross,
        image_gain_cross,
        text_bias,
        text_gain_ffn,
        image_bias,
        image_gain_ffn,
        text_gain_self,
        image_gain_self,
    )
    vector = jnp.concatenate(vectors)
    vector_rows = 8
    vector_block = jnp.pad(vector[None, :], ((0, vector_rows - 1), (0, inner - vector.shape[0])))
    cross_pieces = [text_query, text_key, text_value, image_query, image_key, image_value, image_merge]
    packed_cross = jnp.concatenate(
        cross_pieces + [jnp.pad(text_merge, ((0, 0), (0, inner - text_width))), vector_block], 0
    )
    text_pieces = jnp.split(text_up, text_up.shape[1] // text_width, 1) + [text_down]
    text_pieces += jnp.split(text_self, 3, 1) + [text_mix]
    packed_text = jnp.concatenate(text_pieces, 0)
    image_pieces = [image_up, image_down] + jnp.split(image_self, 3, 1) + [image_mix]
    packed_image = jnp.concatenate(image_pieces, 0)

    def starts(pieces):
        marks = [0]
        for piece in pieces:
            marks.append(marks[-1] + piece.shape[0])
        return list(zip(marks[:-1], marks[1:]))

    cross_at = starts(cross_pieces + [text_merge, vector_block])
    text_at, image_at = starts(text_pieces), starts(image_pieces)
    all_cross = gather(packed_cross)
    all_cross, packed_text = tie(all_cross, packed_text)
    all_text = gather(packed_text)
    all_text, packed_image = tie(all_text, packed_image)
    all_image = gather(packed_image)

    def taken(block, at):
        return whole(block[:, at[0] : at[1]])

    def side_by_side(block, spans):
        return jnp.concatenate([taken(block, at) for at in spans], 1)

    weight_text = side_by_side(all_cross, cross_at[:3])
    weight_image = side_by_side(all_cross, cross_at[3:6])
    full_image_merge = taken(all_cross, cross_at[6])
    full_text_merge = taken(all_cross, cross_at[7])[:, :text_width]
    all_vectors = all_cross[:, cross_at[8][0]]
    full = {}
    at = 0
    for name, piece in zip(VECTOR_NAMES, vectors):
        full[name] = all_vectors[:, at : at + piece.shape[0]].reshape(-1).astype(F32)
        at += piece.shape[0]
    full_text_up = side_by_side(all_text, text_at[:-5])
    full_text_down = taken(all_text, text_at[-5])
    full_text_self = side_by_side(all_text, text_at[-4:-1])
    full_text_mix = taken(all_text, text_at[-1])
    full_image_up = taken(all_image, image_at[0])
    full_image_down = taken(all_image, image_at[1])
    full_image_self = side_by_side(all_image, image_at[2:5])
    full_image_mix = taken(all_image, image_at[5])

    text_slots, image_slots = round_up(length, 8), round_up(regions, 8)

    def padded(array, slots):
        array = jnp.pad(array, ((0, 0), (0, slots - array.shape[1]), (0, 0)))
        return array.reshape(pairs * slots, array.shape[2])

    def rows_of(array):
        return array.reshape(-1, array.shape[-1])

    def pairs_of(array):
        return array.reshape(pairs, array.shape[0] // pairs, array.shape[1])

    def fill_of(live, count):
        slots = live.shape[1]
        fill = jnp.where(live, 0.0, jnp.where(jnp.arange(slots)[None, :] < count, MASKED, PADDED))
        return jnp.broadcast_to(fill[:, :, None], (pairs, slots, LANES)).astype(F32)

    text_rows, image_rows = padded(text_tokens, text_slots), padded(image_regions, image_slots)
    d_text_out = padded(text_cotangent, text_slots)
    d_image_out = padded(image_cotangent, image_slots)
    text_live = jnp.arange(text_slots)[None, :] < caption_lengths[:, None]
    image_live = jnp.pad(region_mask, ((0, 0), (0, image_slots - regions))) > 0
    text_fill, image_fill = fill_of(text_live, length), fill_of(image_live, regions)
    text_keep = text_live.astype(F32).reshape(-1, 1)
    image_keep = image_live.astype(F32).reshape(-1, 1)

    triple_text = pairs_of(project(text_rows, weight_text).astype(BF16))
    triple_image = pairs_of(project(image_rows, weight_image).astype(BF16))
    cross_text = rows_of(
        attend((triple_text, 0), (triple_image, 1), (triple_image, 2), image_fill, inner, HEADS)
    )
    cross_image = rows_of(attend((triple_image, 0), (triple_text, 1), (triple_text, 2), text_fill, inner, HEADS))
    unit_text_1, rate_text_1 = normed_rows(text_rows.astype(F32) + project(cross_text, full_text_merge))
    unit_image_1, rate_image_1 = normed_rows(image_rows.astype(F32) + project(cross_image, full_image_merge))

    def forward(unit_1, gain_1, up, bias, down, gain_2, joint, mix, gain_3, fill, keep, heads):
        width = unit_1.shape[1]
        first = unit_1 * gain_1
        first_low = first.astype(BF16)
        hidden = project(first_low, up) + bias
        active = gelu(hidden).astype(BF16)
        slope = gelu_slope(hidden).astype(BF16)
        unit_2, rate_2 = normed_rows(first + project(active, down))
        second = unit_2 * gain_2
        second_low = second.astype(BF16)
        triple = pairs_of(project(second_low, joint).astype(BF16))
        mixed = rows_of(attend((triple, 0), (triple, 1), (triple, 2), fill, width, heads))
        unit_3, rate_3 = normed_rows(second + project(mixed, mix))
        out = (unit_3 * gain_3 * keep).astype(BF16)
        return out, (first_low, active, slope, unit_2, rate_2, second_low, triple, mixed, unit_3, rate_3)

    def self_backward(saved, gain_2, joint, mix, gain_3, fill, keep, d_out, heads):
        _, _, _, unit_2, rate_2, second_low, triple, mixed, unit_3, rate_3 = saved
        width = unit_2.shape[1]
        d_third, g_gain_3 = normed_back(unit_3, rate_3, gain_3, d_out.astype(F32) * keep)
        d_branch = d_third.astype(BF16)
        g_mix = weight_grad(mixed, d_branch).astype(BF16)
        d_mixed = pairs_of(project_back(d_branch, mix).astype(BF16))
        d_triple = attend_back((triple, 0), (triple, 1), (triple, 2), fill, d_mixed, width, heads)
        d_triple = rows_of(jnp.concatenate(d_triple, -1))
        g_joint = weight_grad(second_low, d_triple).astype(BF16)
        d_second = d_third + project_back(d_triple, joint)
        d_sum, g_gain_2 = normed_back(unit_2, rate_2, gain_2, d_second)
        return d_sum, g_mix, g_joint, g_gain_2, g_gain_3

    def feed_backward(saved, d_sum, unit_1, rate_1, gain_1, up, down):
        first_low, active, slope = saved[:3]
        d_sum_low = d_sum.astype(BF16)
        g_down = weight_grad(active, d_sum_low).astype(BF16)
        d_hidden = (slope.astype(F32) * project_back(d_sum_low, down)).astype(BF16)
        g_bias = jnp.sum(d_hidden.astype(F32), 0)
        g_up = weight_grad(first_low, d_hidden).astype(BF16)
        d_first = d_sum + project_back(d_hidden, up)
        d_resid, g_gain_1 = normed_back(unit_1, rate_1, gain_1, d_first)
        return d_resid, g_up, g_down, g_bias, g_gain_1

    def split_rows(matrix, parts):
        return [owned_rows(piece, devices) for piece in jnp.split(matrix, parts, 1)]

    out_text, saved_text = forward(
        unit_text_1,
        full["text_gain_cross"],
        full_text_up,
        full["text_bias"],
        full_text_down,
        full["text_gain_ffn"],
        full_text_self,
        full_text_mix,
        full["text_gain_self"],
        text_fill,
        text_keep,
        TEXT_HEADS,
    )
    d_sum_text, g_text_mix, g_text_self, g_text_gain_ffn, g_text_gain_self = self_backward(
        saved_text,
        full["text_gain_ffn"],
        full_text_self,
        full_text_mix,
        full["text_gain_self"],
        text_fill,
        text_keep,
        d_text_out,
        TEXT_HEADS,
    )
    d_resid_text, g_text_up, g_text_down, g_text_bias, g_text_gain_cross = feed_backward(
        saved_text, d_sum_text, unit_text_1, rate_text_1, full["text_gain_cross"], full_text_up, full_text_down
    )
    ups = text_up.shape[1] // text_width
    sum_text = OwnerSum(
        jnp.concatenate(
            split_rows(g_text_up, ups)
            + [owned_rows(g_text_down, devices)]
            + split_rows(g_text_self, 3)
            + [owned_rows(g_text_mix, devices)],
            1,
        ),
        sizes,
    )
    d_resid_text = sum_text.advance(d_resid_text)

    d_merge_text = d_resid_text.astype(BF16)
    g_text_merge = weight_grad(cross_text, d_merge_text).astype(BF16)
    d_heads_text = pairs_of(project_back(d_merge_text, full_text_merge).astype(BF16))
    d_query_text, d_key_image, d_value_image = map(
        rows_of,
        attend_back((triple_text, 0), (triple_image, 1), (triple_image, 2), image_fill, d_heads_text, inner, HEADS),
    )
    g_text_query = weight_grad(text_rows, d_query_text).astype(BF16)
    g_image_key = weight_grad(image_rows, d_key_image).astype(BF16)
    g_image_value = weight_grad(image_rows, d_value_image).astype(BF16)
    unit_image_1 = sum_text.advance(unit_image_1)
    sum_first = OwnerSum(
        jnp.concatenate(
            [
                owned_rows(g_text_query, devices),
                owned_rows(g_image_key, devices),
                owned_rows(g_image_value, devices),
                owned_rows(jnp.pad(g_text_merge, ((0, 0), (0, inner - text_width))), devices),
            ],
            1,
        ),
        sizes,
    )
    unit_image_1 = sum_first.advance(unit_image_1)

    out_image, saved_image = forward(
        unit_image_1,
        full["image_gain_cross"],
        full_image_up,
        full["image_bias"],
        full_image_down,
        full["image_gain_ffn"],
        full_image_self,
        full_image_mix,
        full["image_gain_self"],
        image_fill,
        image_keep,
        IMAGE_HEADS,
    )
    d_image_out = sum_text.advance(d_image_out, *saved_image)[0]
    d_sum_image, g_image_mix, g_image_self, g_image_gain_ffn, g_image_gain_self = self_backward(
        saved_image,
        full["image_gain_ffn"],
        full_image_self,
        full_image_mix,
        full["image_gain_self"],
        image_fill,
        image_keep,
        d_image_out,
        IMAGE_HEADS,
    )
    d_sum_image = sum_first.advance(d_sum_image)
    d_resid_image, g_image_up, g_image_down, g_image_bias, g_image_gain_cross = feed_backward(
        saved_image,
        d_sum_image,
        unit_image_1,
        rate_image_1,
        full["image_gain_cross"],
        full_image_up,
        full_image_down,
    )
    d_resid_image = sum_text.advance(d_resid_image)
    sum_image = OwnerSum(
        jnp.concatenate(
            [owned_rows(g_image_up, devices), owned_rows(g_image_down, devices)]
            + split_rows(g_image_self, 3)
            + [owned_rows(g_image_mix, devices)],
            1,
        ),
        sizes,
    )
    d_resid_image = sum_image.advance(d_resid_image)

    d_merge_image = d_resid_image.astype(BF16)
    g_image_merge = weight_grad(cross_image, d_merge_image).astype(BF16)
    d_heads_image = pairs_of(project_back(d_merge_image, full_image_merge).astype(BF16))
    d_query_image, d_key_text, d_value_text = map(
        rows_of,
        attend_back((triple_image, 0), (triple_text, 1), (triple_text, 2), text_fill, d_heads_image, inner, HEADS),
    )
    d_query_image = sum_first.advance(d_query_image)
    d_key_text = sum_image.advance(d_key_text)
    g_image_query = weight_grad(image_rows, d_query_image).astype(BF16)
    g_text_key = weight_grad(text_rows, d_key_text).astype(BF16)
    g_text_value = weight_grad(text_rows, d_value_text).astype(BF16)
    g_vectors = (
        g_text_gain_cross,
        g_image_gain_cross,
        g_text_bias,
        g_text_gain_ffn,
        g_image_bias,
        g_image_gain_ffn,
        g_text_gain_self,
        g_image_gain_self,
    )
    g_vector = jnp.concatenate([piece.reshape(devices, -1) for piece in g_vectors], 1).astype(BF16)
    g_vector = jnp.pad(g_vector[:, None, :], ((0, 0), (0, vector_rows - 1), (0, inner - g_vector.shape[1])))
    sum_last = OwnerSum(
        jnp.concatenate(
            [
                owned_rows(g_image_query, devices),
                owned_rows(g_text_key, devices),
                owned_rows(g_text_value, devices),
                owned_rows(g_image_merge, devices),
                g_vector,
            ],
            1,
        ),
        sizes,
    )
    d_resid_text, d_resid_image = sum_last.advance(d_resid_text, d_resid_image)
    grad_text = d_resid_text + project_back(
        jnp.concatenate([d_query_text, d_key_text, d_value_text], 1), weight_text
    )
    grad_image = d_resid_image + project_back(
        jnp.concatenate([d_query_image, d_key_image, d_value_image], 1), weight_image
    )

    def owned(total, pieces):
        return [total[start:end] for start, end in starts(pieces)]

    done = [one.result() for one in (sum_text, sum_first, sum_image, sum_last)]
    text_sums = owned(done[0], text_pieces)
    sum_text_query, sum_image_key, sum_image_value, sum_text_merge = owned(
        done[1], [text_query, image_key, image_value, text_merge]
    )
    image_sums = owned(done[2], image_pieces)
    sum_image_query, sum_text_key, sum_text_value, sum_image_merge, sum_vector = owned(
        done[3], [image_query, text_key, text_value, image_merge, vector_block]
    )
    owned_vector = {}
    at = 0
    for name, piece in zip(VECTOR_NAMES, vectors):
        owned_vector[name] = sum_vector[0, at : at + piece.shape[0]]
        at += piece.shape[0]
    return (
        pairs_of(out_text)[:, :length],
        pairs_of(out_image)[:, :regions],
        pairs_of(grad_text)[:, :length],
        pairs_of(grad_image)[:, :regions],
        sum_text_query,
        sum_image_key,
        sum_image_value,
        sum_text_merge[:, :text_width],
        owned_vector["text_gain_cross"],
        sum_image_query,
        sum_text_key,
        sum_text_value,
        sum_image_merge,
        owned_vector["image_gain_cross"],
        jnp.concatenate(text_sums[:-5], 1),
        owned_vector["text_bias"],
        text_sums[-5],
        owned_vector["text_gain_ffn"],
        image_sums[0],
        owned_vector["image_bias"],
        image_sums[1],
        owned_vector["image_gain_ffn"],
        jnp.concatenate(text_sums[-4:-1], 1),
        text_sums[-1],
        owned_vector["text_gain_self"],
        jnp.concatenate(image_sums[2:5], 1),
        image_sums[5],
        owned_vector["image_gain_self"],
    )


def solution(mesh):
    split = {1: P(AXES), 2: P(AXES, None), 3: P(AXES, None, None)}
    in_ranks = (3, 3, 1, 2, 3, 3) + tuple(
        1 if at in (4, 9, 11, 13, 15, 17, 20, 23) else 2 for at in range(24)
    )
    out_ranks = (3, 3, 3, 3) + in_ranks[6:]
    return jax.shard_map(
        functools.partial(per_device, dict(mesh.shape)),
        mesh=mesh,
        in_specs=tuple(split[rank] for rank in in_ranks),
        out_specs=tuple(split[rank] for rank in out_ranks),
        check_vma=False,
    )
```

```python
import functools
import math

import jax
import jax.numpy as jnp
from jax import lax
from jax.experimental import pallas as pl
from jax.experimental.pallas import tpu as pltpu
from jax.sharding import PartitionSpec as P

HEADS = 8
TEXT_HEADS = 12
IMAGE_HEADS = 8
EPSILON = 1e-05
MASKED = -1000000000.0
PADDED = -2000000000.0
LANES = 128
AXES = ("gx", "gy")
F32 = jnp.float32
BF16 = jnp.bfloat16
VMEM_BYTES = 48 * 1024 * 1024
VECTOR_NAMES = (
    "text_gain_cross",
    "image_gain_cross",
    "text_bias",
    "text_gain_ffn",
    "image_bias",
    "image_gain_ffn",
    "text_gain_self",
    "image_gain_self",
)


def project(left, right):
    return jnp.dot(left, right, preferred_element_type=F32)


def project_back(left, right):
    return lax.dot_general(left, right, (((1,), (1,)), ((), ())), preferred_element_type=F32)


def weight_grad(left, right):
    return lax.dot_general(left, right, (((0,), (0,)), ((), ())), preferred_element_type=F32)


def round_up(size, step):
    return -(-size // step) * step


def stack_halves(rows):
    wide = rows.astype(F32)
    first = lax.broadcasted_iota(jnp.int32, wide.shape, 1) < LANES // 2
    zero = jnp.zeros_like(wide)
    return jnp.concatenate([jnp.where(first, wide, zero), jnp.where(first, zero, wide)], 0).astype(BF16)


def join_halves(rows):
    count = rows.shape[0] // 2
    first = lax.broadcasted_iota(jnp.int32, (count, LANES), 1) < LANES // 2
    return jnp.where(first, rows[:count], rows[count:])


def probabilities(keys, queries, fill, scale):
    scores = project_back(keys, queries) * scale
    scores = jnp.where(fill < 0.0, fill, scores)
    powers = jnp.exp(scores - jnp.max(scores, 0, keepdims=True))
    return powers * (1.0 / jnp.sum(powers, 0, keepdims=True))


def head_blocks(queries_ref, size):
    count, _, width = queries_ref.shape
    return [(pair, slice(at, at + LANES)) for pair in range(count) for at in range(0, width, LANES)], size < LANES


def attend_kernel(size, queries_ref, keys_ref, values_ref, fill_ref, mixed_ref):
    scale = 1.0 / math.sqrt(size)
    blocks, split = head_blocks(queries_ref, size)
    queries = [stack_halves(queries_ref[p, :, b]) if split else queries_ref[p, :, b] for p, b in blocks]
    probs = [
        probabilities(keys_ref[p, :, b], query, fill_ref[p][:, :1], scale).astype(BF16)
        for (p, b), query in zip(blocks, queries)
    ]
    mixed = [weight_grad(prob, values_ref[p, :, b]) for (p, b), prob in zip(blocks, probs)]
    for (p, b), rows in zip(blocks, mixed):
        mixed_ref[p, :, b] = (join_halves(rows) if split else rows).astype(BF16)


def attend_back_kernel(
    size, queries_ref, keys_ref, values_ref, fill_ref, d_mixed_ref, d_queries_ref, d_keys_ref, d_values_ref
):
    scale = 1.0 / math.sqrt(size)
    blocks, split = head_blocks(queries_ref, size)
    fills = [fill_ref[p][:, :1] for p, _ in blocks]
    queries = [stack_halves(queries_ref[p, :, b]) if split else queries_ref[p, :, b] for p, b in blocks]
    grads = [stack_halves(d_mixed_ref[p, :, b]) if split else d_mixed_ref[p, :, b] for p, b in blocks]
    probs = [
        probabilities(keys_ref[p, :, b], query, fill, scale) for (p, b), query, fill in zip(blocks, queries, fills)
    ]
    d_probs = [project_back(values_ref[p, :, b], grad) for (p, b), grad in zip(blocks, grads)]
    for (p, b), prob, grad in zip(blocks, probs, grads):
        d_values_ref[p, :, b] = project(prob.astype(BF16), grad).astype(BF16)
    d_scores = [
        prob * (d_prob - jnp.sum(prob * d_prob, 0, keepdims=True)) for prob, d_prob in zip(probs, d_probs)
    ]
    d_scores = [jnp.where(fill < 0.0, 0.0, one).astype(BF16) for fill, one in zip(fills, d_scores)]
    for (p, b), one, query in zip(blocks, d_scores, queries):
        d_keys_ref[p, :, b] = (project(one, query) * scale).astype(BF16)
    for (p, b), one in zip(blocks, d_scores):
        rows = weight_grad(one, keys_ref[p, :, b]) * scale
        d_queries_ref[p, :, b] = (join_halves(rows) if split else rows).astype(BF16)


def attention_call(kernel, together, inputs, outputs, flops):
    pairs = inputs[0][0].shape[0]
    together = math.gcd(pairs, together)

    def spec(rows, width, column):
        return pl.BlockSpec((together, rows, width), lambda step: (step, 0, column))

    moved = sum(pairs * array.shape[1] * width * array.dtype.itemsize for array, width, _ in inputs)
    moved += sum(pairs * rows * width * 2 for rows, width in outputs)
    return pl.pallas_call(
        kernel,
        grid=(pairs // together,),
        in_specs=[spec(array.shape[1], width, column) for array, width, column in inputs],
        out_specs=[spec(rows, width, 0) for rows, width in outputs],
        out_shape=[jax.ShapeDtypeStruct((pairs, rows, width), BF16) for rows, width in outputs],
        compiler_params=pltpu.CompilerParams(vmem_limit_bytes=VMEM_BYTES),
        cost_estimate=pl.CostEstimate(flops=flops, bytes_accessed=moved, transcendentals=0),
    )(*[array for array, _, _ in inputs])


def attend(queries, keys, values, fill, width, heads):
    pairs, count = queries[0].shape[:2]
    inputs = [(array, width, column) for array, column in (queries, keys, values)] + [(fill, LANES, 0)]
    flops = 4 * pairs * count * keys[0].shape[1] * max(width, heads * LANES)
    kernel = functools.partial(attend_kernel, width // heads)
    return attention_call(kernel, 4, inputs, [(count, width)], flops)[0]


def attend_back(queries, keys, values, fill, d_mixed, width, heads):
    pairs, count = queries[0].shape[:2]
    inputs = [(array, width, column) for array, column in (queries, keys, values)]
    inputs += [(fill, LANES, 0), (d_mixed, width, 0)]
    keyed = keys[0].shape[1]
    flops = 10 * pairs * count * keyed * max(width, heads * LANES)
    kernel = functools.partial(attend_back_kernel, width // heads)
    return attention_call(kernel, 2, inputs, [(count, width), (keyed, width), (keyed, width)], flops)


def tie(*values):
    return lax.optimization_barrier(values)


def gather(packed):
    return lax.all_gather(packed, AXES, axis=0, tiled=False)


def gather_by_exchange(packed, sizes):
    core, rows, columns, rest = mesh_axes_bits(sizes)
    order = mesh_bits(sizes)

    def doubled(block, have, which):
        axis, bit = which
        count = lax.axis_size(axis)
        got = lax.ppermute(block, axis, [(at, at ^ (1 << bit)) for at in range(count)])
        first = ((lax.axis_index(axis) >> bit) & 1) == 0
        have = sorted(have + [which], key=order.index)
        lower, upper = jnp.where(first, block, got), jnp.where(first, got, block)
        return jnp.stack([lower, upper], have.index(which)), have

    block, have = packed, []
    for which in reversed(rest):
        block, have = doubled(block, have, which)
    width = packed.shape[1]
    halves = [(block[..., : width // 2], have), (block[..., width // 2 :], have)]
    for steps in zip(rows + columns, columns + rows):
        halves = [doubled(block, have, which) for (block, have), which in zip(halves, steps)]
    block, have = jnp.concatenate([halves[0][0], halves[1][0]], -1), halves[0][1]
    for which in core:
        block, have = doubled(block, have, which)
    return block.reshape((-1,) + packed.shape)


def whole(block):
    return block.reshape(-1, block.shape[-1])


def owned_rows(matrix, devices):
    return matrix.reshape(devices, matrix.shape[0] // devices, matrix.shape[1])


def mesh_bits(sizes):
    bits = []
    for axis in AXES:
        bits += [(axis, bit) for bit in reversed(range(sizes[axis].bit_length() - 1))]
    return bits


def mesh_axes_bits(sizes):
    low = (sizes["gy"].bit_length() - 1) // 2
    bits = mesh_bits(sizes)[::-1]
    core = [one for one in bits if one == ("gx", 0)]
    rows = [one for one in bits if one[0] == "gx" and one[1] > 0]
    columns = [one for one in bits if one[0] == "gy" and one[1] < low]
    rest = [one for one in bits if one[0] == "gy" and one[1] >= low]
    return core, rows, columns, rest


def grad_kernel(per_core, left_ref, right_ref, core_ref, *refs):
    away_ref, kept_ref, whole_ref = refs[-3:]
    own = core_ref[0]
    grad = weight_grad(left_ref[...], right_ref[...])
    groups, _, width = whole_ref.shape
    if grad.shape[1] < width:
        grad = jnp.pad(grad, ((0, 0), (0, width - grad.shape[1])))
    whole_ref[...] = grad.reshape(whole_ref.shape)
    for group in range(groups // 2):
        shape = kept_ref.shape[1:]
        kept_ref[group] = whole_ref[2 * group + own].reshape(shape).astype(BF16)
        away_ref[group] = whole_ref[2 * group + 1 - own].reshape(shape).astype(BF16)


def grad_rows_kernel(left_ref, right_ref, core_ref, *refs):
    away_ref, kept_ref = refs[-2:]
    stays = pl.program_id(0) % 2 == core_ref[0]
    shape = kept_ref.shape[1:]
    grad = weight_grad(left_ref[...], right_ref[...]).astype(BF16).reshape(shape)

    @pl.when(stays)
    def _():
        kept_ref[0] = grad

    @pl.when(jnp.logical_not(stays))
    def _():
        away_ref[0] = grad


def place_kernel(terms_ref, core_ref, *refs):
    away_ref, kept_ref = refs[-2:]
    own = core_ref[0]
    for group in range(kept_ref.shape[0]):
        kept_ref[group] = terms_ref[group, own]
        away_ref[group] = terms_ref[group, 1 - own]


def pack_terms(pieces, rows, width, sizes):
    groups, others = sizes["gx"] // 2, sizes["gy"]
    core = (lax.axis_index("gx") & 1).astype(jnp.int32).reshape(1)
    shape = jax.ShapeDtypeStruct((groups, others, rows, width), BF16)
    buffers = []
    for piece in pieces:
        first, scratch = piece[0], []
        scalar = pl.BlockSpec(memory_space=pltpu.SMEM)
        if len(piece) == 2:
            terms = piece[1].reshape((groups, 2, others) + piece[1].shape[1:])
            count = terms.shape[3]
            kernel, arrays, grid, flops = place_kernel, [terms], (1,), 0
            in_specs = [pl.BlockSpec(terms.shape, lambda step: (0,) * 5)]
            place = pl.BlockSpec((groups, others, count, width), lambda step, at=first // count: (0, 0, at, 0))
        else:
            left, right = piece[1:]
            height, tall = left.shape
            count = tall // (2 * groups * others)
            arrays, flops = [left, right], 2 * height * tall * right.shape[1]
            if right.shape[1] <= width and tall >= 2048:
                kernel, grid = grad_rows_kernel, (2 * groups,)
                in_specs = [
                    pl.BlockSpec((height, tall // (2 * groups)), lambda step: (0, step)),
                    pl.BlockSpec(right.shape, lambda step: (0, 0)),
                ]
                place = pl.BlockSpec((1, others, count, width), lambda step, at=first // count: (step // 2, 0, at, 0))
            else:
                each = min(width, right.shape[1])
                kernel, grid = functools.partial(grad_kernel, groups), (right.shape[1] // each,)
                in_specs = [
                    pl.BlockSpec(left.shape, lambda step: (0, 0)),
                    pl.BlockSpec((height, each), lambda step: (0, step)),
                ]
                place = pl.BlockSpec(
                    (groups, others, count, width), lambda step, at=first // count: (0, 0, at + step, 0)
                )
                scratch = [pltpu.VMEM((2 * groups, tall // (2 * groups), width), F32)]
        assert first % count == 0
        arrays = arrays + [core] + buffers
        in_specs = in_specs + [scalar] + [pl.BlockSpec(memory_space=pl.ANY)] * len(buffers)
        moved = sum(array.size * 2 for array in arrays[:2]) + 4 * flops // 2048
        buffers = list(pl.pallas_call(
            kernel,
            grid=grid,
            in_specs=in_specs,
            out_specs=[place, place],
            out_shape=[shape, shape],
            scratch_shapes=scratch,
            input_output_aliases={len(arrays) - 2: 0, len(arrays) - 1: 1} if buffers else {},
            compiler_params=pltpu.CompilerParams(vmem_limit_bytes=VMEM_BYTES),
            cost_estimate=pl.CostEstimate(flops=flops, bytes_accessed=moved, transcendentals=0),
        )(*arrays))
    return buffers


def split_kernel(where_ref, kept_ref, got_ref, away_x_ref, kept_x_ref, away_y_ref, kept_y_ref):
    x, y = where_ref[0], where_ref[1]
    half = kept_ref.shape[-1] // 2

    def added(at, columns):
        return (kept_ref[0, 0, 0, at, :, columns].astype(F32) + got_ref[0, 0, 0, at, :, columns].astype(F32)).astype(BF16)

    left, right = slice(0, half), slice(half, 2 * half)
    kept_x_ref[0, 0, 0] = added(x, left)
    away_x_ref[0, 0, 0] = added(1 - x, left)
    stays = pl.program_id(2) == y

    @pl.when(stays)
    def _():
        for at in range(2):
            kept_y_ref[0, 0, at] = added(at, right)

    @pl.when(jnp.logical_not(stays))
    def _():
        for at in range(2):
            away_y_ref[0, 0, at] = added(at, right)


def split_terms(kept, got):
    groups, others, rows, width = kept.shape
    where = jnp.stack([lax.axis_index("gy") & 1, (lax.axis_index("gx") >> 1) & 1]).astype(jnp.int32)
    shape = (groups // 2, 2, others // 2, 2, rows, width)
    half = width // 2
    inside = pl.BlockSpec((1, 1, 1, 2, rows, width), lambda high, z, y, where: (high, y, z, 0, 0, 0))
    along_x = pl.BlockSpec((1, 1, 1, rows, half), lambda high, z, y, where: (high, y, z, 0, 0))
    along_y = pl.BlockSpec((1, 1, 2, rows, half), lambda high, z, y, where: (high, z, 0, 0, 0))
    shape_x = jax.ShapeDtypeStruct((groups // 2, 2, others // 2, rows, half), BF16)
    shape_y = jax.ShapeDtypeStruct((groups // 2, others // 2, 2, rows, half), BF16)
    return pl.pallas_call(
        split_kernel,
        grid_spec=pltpu.PrefetchScalarGridSpec(
            num_scalar_prefetch=1,
            grid=(groups // 2, others // 2, 2),
            in_specs=[inside, inside],
            out_specs=[along_x, along_x, along_y, along_y],
        ),
        out_shape=[shape_x, shape_x, shape_y, shape_y],
        compiler_params=pltpu.CompilerParams(vmem_limit_bytes=VMEM_BYTES),
        cost_estimate=pl.CostEstimate(flops=kept.size, bytes_accessed=6 * kept.size, transcendentals=0),
    )(where, kept.reshape(shape), got.reshape(shape))


class OwnerSum:
    def __init__(self, pieces, rows, width, sizes):
        bits = mesh_bits(sizes)
        core, y_bits, x_bits, z_bits = mesh_axes_bits(sizes)
        self.width = width
        self.flying = None
        self.plan = [list(pair) for pair in zip(x_bits + y_bits, y_bits + x_bits)] + [[which] for which in z_bits]
        devices = sizes["gx"] * sizes["gy"]
        self.whole_tiles = len(core) == 1 and bool(y_bits) and bool(x_bits) and len(x_bits) == len(y_bits)
        for piece in pieces:
            self.whole_tiles &= len(piece) == 2 or piece[1].shape[1] % (8 * devices) == 0
        if self.whole_tiles:
            away, kept = pack_terms(pieces, rows, width, sizes)
            self.waiting = [(away, kept) + core[0] + ([one for one in bits if one not in core],)]
        else:
            packed = jnp.zeros((devices, rows, width), BF16)
            for piece in pieces:
                blocks = [piece[1]]
                if len(piece) == 3:
                    grad = weight_grad(*piece[1:]).astype(BF16)
                    blocks = jnp.split(grad, max(1, grad.shape[1] // width), 1)
                at = piece[0]
                for block in blocks:
                    block = block.reshape(devices, -1, block.shape[-1])
                    packed = lax.dynamic_update_slice(packed, block, (0, at, 0))
                    at += block.shape[1]
            self.waiting = None
            self.parts = [(packed.reshape((2,) * len(bits) + packed.shape[1:]), bits)]
            self.plan = [[which] for which in core] + self.plan

    def advance(self, *others):
        sends, self.waiting = self.waiting, None
        if self.flying is not None:
            held = tie(*[got for _, got, _ in self.flying], *others)
            others = held[len(self.flying) :]
            if self.whole_tiles and self.flying[0][0].ndim == 4 and self.flying[0][0].shape[-1] == self.width and len(self.plan[0]) == 2:
                sends = self.first_split(held[0])
            else:
                self.parts = [
                    ((kept.astype(F32) + got.astype(F32)).astype(BF16 if self.plan else F32), bits)
                    for (kept, _, bits), got in zip(self.flying, held)
                ]
            self.flying = None
        if sends is None and self.plan:
            sends = self.halves()
        if sends is not None:
            held = tie(*[one[0] for one in sends], *others)
            others = held[len(sends) :]
            self.flying = []
            for away, (_, kept, axis, bit, left) in zip(held, sends):
                count = lax.axis_size(axis)
                got = lax.ppermute(away, axis, [(at, at ^ (1 << bit)) for at in range(count)])
                self.flying.append((kept, got, left))
        return others[0] if len(others) == 1 else others

    def first_split(self, got):
        kept, _, bits = self.flying[0]
        out = split_terms(kept, got)
        sends = []
        for part, which in enumerate(self.plan.pop(0)):
            left = [one for one in bits if one != which]
            away, kept = (one.reshape((2,) * len(left) + one.shape[-2:]) for one in out[2 * part : 2 * part + 2])
            sends.append((away, kept) + which + (left,))
        return sends

    def halves(self):
        step = self.plan.pop(0)
        if len(step) == 2 and len(self.parts) == 1:
            total, bits = self.parts[0]
            self.parts = [(total[..., : self.width // 2], bits), (total[..., self.width // 2 :], bits)]
        if len(step) == 1 and len(self.parts) == 2:
            self.parts = [(jnp.concatenate([self.parts[0][0], self.parts[1][0]], -1), self.parts[0][1])]
        sends = []
        for (total, bits), (axis, bit) in zip(self.parts, step):
            place = bits.index((axis, bit))
            own = (lax.axis_index(axis) >> bit) & 1
            away = lax.dynamic_index_in_dim(total, 1 - own, place, keepdims=False)
            kept = lax.dynamic_index_in_dim(total, own, place, keepdims=False)
            sends.append((away, kept, axis, bit, [one for one in bits if one != (axis, bit)]))
        return sends

    def result(self):
        while self.plan or self.flying is not None:
            self.advance()
        return self.parts[0][0].astype(F32)


def normed_rows(values_in):
    centred = values_in - jnp.mean(values_in, -1, keepdims=True)
    rate = lax.rsqrt(jnp.mean(centred * centred, -1, keepdims=True) + EPSILON)
    return centred * rate, rate


def normed_back(unit, rate, gain, d_out):
    d_unit = d_out * gain
    mean_unit = jnp.mean(d_unit, -1, keepdims=True)
    mean_cross = jnp.mean(d_unit * unit, -1, keepdims=True)
    return rate * (d_unit - mean_unit - unit * mean_cross), jnp.sum(d_out * unit, 0)


GELU_RATE = math.sqrt(2.0 / math.pi)
GELU_CUBE = 0.044715


def gelu(values_in):
    inner = jnp.tanh(GELU_RATE * (values_in + GELU_CUBE * values_in * values_in * values_in))
    return 0.5 * values_in * (1.0 + inner)


def gelu_slope(values_in):
    square = values_in * values_in
    inner = jnp.tanh(GELU_RATE * values_in * (1.0 + GELU_CUBE * square))
    return 0.5 * (1.0 + inner) + 0.5 * values_in * (1.0 - inner * inner) * GELU_RATE * (1.0 + 3.0 * GELU_CUBE * square)


def per_device(sizes, *given):
    (
        text_tokens,
        image_regions,
        caption_lengths,
        region_mask,
        text_cotangent,
        image_cotangent,
        text_query,
        image_key,
        image_value,
        text_merge,
        text_gain_cross,
        image_query,
        text_key,
        text_value,
        image_merge,
        image_gain_cross,
        text_up,
        text_bias,
        text_down,
        text_gain_ffn,
        image_up,
        image_bias,
        image_down,
        image_gain_ffn,
        text_self,
        text_mix,
        text_gain_self,
        image_self,
        image_mix,
        image_gain_self,
    ) = given
    devices = sizes["gx"] * sizes["gy"]
    pairs, length, text_width = text_tokens.shape
    regions, image_width = image_regions.shape[1:]
    inner = text_query.shape[1]

    vectors = (
        text_gain_cross,
        image_gain_cross,
        text_bias,
        text_gain_ffn,
        image_bias,
        image_gain_ffn,
        text_gain_self,
        image_gain_self,
    )
    vector_block = jnp.concatenate(
        [jnp.pad(vector[None, :], ((0, 0), (0, text_width - vector.shape[0]))) for vector in vectors], 0
    )
    first_pieces = [text_query, image_key, image_value]
    packed_first = jnp.concatenate(first_pieces + [jnp.pad(text_merge, ((0, 0), (0, inner - text_width)))], 0)
    text_pieces = jnp.split(text_up, text_up.shape[1] // text_width, 1) + [text_down]
    text_pieces += jnp.split(text_self, 3, 1) + [text_mix, vector_block]
    packed_text = jnp.concatenate(text_pieces, 0)
    image_pieces = [image_query, text_key, text_value, image_merge, image_up, image_down]
    image_pieces += jnp.split(image_self, 3, 1) + [image_mix]
    packed_image = jnp.concatenate(image_pieces, 0)

    def starts(pieces):
        marks = [0]
        for piece in pieces:
            marks.append(marks[-1] + piece.shape[0])
        return list(zip(marks[:-1], marks[1:]))

    def taken(block, at):
        return whole(block[:, at[0] : at[1]])

    def side_by_side(block, spans):
        return jnp.concatenate([taken(block, at) for at in spans], 1)

    first_at = starts(first_pieces + [text_merge])
    text_at, image_at = starts(text_pieces), starts(image_pieces)
    all_text = gather(packed_text)
    all_first = gather_by_exchange(packed_first, sizes)
    weight_text_query = taken(all_first, first_at[0])
    weight_image_held = side_by_side(all_first, first_at[1:3])
    full_text_merge = taken(all_first, first_at[3])[:, :text_width]

    text_slots, image_slots = round_up(length, 8), round_up(regions, 8)

    def padded(array, slots):
        array = jnp.pad(array, ((0, 0), (0, slots - array.shape[1]), (0, 0)))
        return array.reshape(pairs * slots, array.shape[2])

    def rows_of(array):
        return array.reshape(-1, array.shape[-1])

    def pairs_of(array):
        return array.reshape(pairs, array.shape[0] // pairs, array.shape[1])

    def fill_of(live, count):
        slots = live.shape[1]
        fill = jnp.where(live, 0.0, jnp.where(jnp.arange(slots)[None, :] < count, MASKED, PADDED))
        return jnp.broadcast_to(fill[:, :, None], (pairs, slots, LANES)).astype(F32)

    text_rows, image_rows = padded(text_tokens, text_slots), padded(image_regions, image_slots)
    d_text_out = padded(text_cotangent, text_slots)
    d_image_out = padded(image_cotangent, image_slots)
    text_live = jnp.arange(text_slots)[None, :] < caption_lengths[:, None]
    image_live = jnp.pad(region_mask, ((0, 0), (0, image_slots - regions))) > 0
    text_fill, image_fill = fill_of(text_live, length), fill_of(image_live, regions)
    text_keep = text_live.astype(F32).reshape(-1, 1)
    image_keep = image_live.astype(F32).reshape(-1, 1)

    query_text = pairs_of(project(text_rows, weight_text_query).astype(BF16))
    held_image = pairs_of(project(image_rows, weight_image_held).astype(BF16))
    mixed_cross = attend((query_text, 0), (held_image, 0), (held_image, 1), image_fill, inner, HEADS)
    mixed_cross, packed_image = tie(mixed_cross, packed_image)
    all_image = gather(packed_image)
    cross_text = rows_of(mixed_cross)
    unit_text_1, rate_text_1 = normed_rows(text_rows.astype(F32) + project(cross_text, full_text_merge))

    ups = text_up.shape[1] // text_width
    full_text_up = side_by_side(all_text, text_at[:ups])
    full_text_down = taken(all_text, text_at[ups])
    full_text_self = side_by_side(all_text, text_at[ups + 1 : ups + 4])
    full_text_mix = taken(all_text, text_at[ups + 4])
    full = {
        name: all_text[:, text_at[ups + 5][0] + at, : piece.shape[0]].reshape(-1).astype(F32)
        for at, (name, piece) in enumerate(zip(VECTOR_NAMES, vectors))
    }

    def forward(unit_1, gain_1, up, bias, down, gain_2, joint, mix, gain_3, fill, keep, heads):
        width = unit_1.shape[1]
        first = unit_1 * gain_1
        first_low = first.astype(BF16)
        hidden = project(first_low, up) + bias
        active = gelu(hidden).astype(BF16)
        slope = gelu_slope(hidden).astype(BF16)
        unit_2, rate_2 = normed_rows(first + project(active, down))
        second = unit_2 * gain_2
        second_low = second.astype(BF16)
        triple = pairs_of(project(second_low, joint).astype(BF16))
        mixed = rows_of(attend((triple, 0), (triple, 1), (triple, 2), fill, width, heads))
        unit_3, rate_3 = normed_rows(second + project(mixed, mix))
        out = (unit_3 * gain_3 * keep).astype(BF16)
        return out, (first_low, active, slope, unit_2, rate_2, second_low, triple, mixed, unit_3, rate_3)

    def self_backward(saved, gain_2, joint, mix, gain_3, fill, keep, d_out, heads):
        _, _, _, unit_2, rate_2, second_low, triple, mixed, unit_3, rate_3 = saved
        width = unit_2.shape[1]
        d_third, g_gain_3 = normed_back(unit_3, rate_3, gain_3, d_out.astype(F32) * keep)
        d_branch = d_third.astype(BF16)
        d_mixed = pairs_of(project_back(d_branch, mix).astype(BF16))
        d_triple = attend_back((triple, 0), (triple, 1), (triple, 2), fill, d_mixed, width, heads)
        d_triple = rows_of(jnp.concatenate(d_triple, -1))
        d_second = d_third + project_back(d_triple, joint)
        d_sum, g_gain_2 = normed_back(unit_2, rate_2, gain_2, d_second)
        return d_sum, (mixed, d_branch), (second_low, d_triple), g_gain_2, g_gain_3

    def feed_backward(saved, d_sum, unit_1, rate_1, gain_1, up, down):
        first_low, active, slope = saved[:3]
        d_sum_low = d_sum.astype(BF16)
        d_hidden = (slope.astype(F32) * project_back(d_sum_low, down)).astype(BF16)
        g_bias = jnp.sum(d_hidden.astype(F32), 0)
        d_first = d_sum + project_back(d_hidden, up)
        d_resid, g_gain_1 = normed_back(unit_1, rate_1, gain_1, d_first)
        return d_resid, (first_low, d_hidden), (active, d_sum_low), g_bias, g_gain_1

    out_text, saved_text = forward(
        unit_text_1,
        full["text_gain_cross"],
        full_text_up,
        full["text_bias"],
        full_text_down,
        full["text_gain_ffn"],
        full_text_self,
        full_text_mix,
        full["text_gain_self"],
        text_fill,
        text_keep,
        TEXT_HEADS,
    )
    d_sum_text, g_text_mix, g_text_self, g_text_gain_ffn, g_text_gain_self = self_backward(
        saved_text,
        full["text_gain_ffn"],
        full_text_self,
        full_text_mix,
        full["text_gain_self"],
        text_fill,
        text_keep,
        d_text_out,
        TEXT_HEADS,
    )
    d_resid_text, g_text_up, g_text_down, g_text_bias, g_text_gain_cross = feed_backward(
        saved_text, d_sum_text, unit_text_1, rate_text_1, full["text_gain_cross"], full_text_up, full_text_down
    )
    row_down, row_self = text_at[ups][0], text_at[ups + 1][0]
    sum_text = OwnerSum(
        [
            (0, *g_text_up),
            (row_down, *g_text_down),
            (row_self, *g_text_self),
            (text_at[ups + 4][0], *g_text_mix),
        ],
        text_at[ups + 4][1],
        text_width,
        sizes,
    )
    d_resid_text = sum_text.advance(d_resid_text)

    d_merge_text = d_resid_text.astype(BF16)
    d_heads_text = pairs_of(project_back(d_merge_text, full_text_merge).astype(BF16))
    d_query_text, d_key_image, d_value_image = map(
        rows_of,
        attend_back((query_text, 0), (held_image, 0), (held_image, 1), image_fill, d_heads_text, inner, HEADS),
    )
    row_image, row_text = image_key.shape[0], text_query.shape[0]
    sum_first = OwnerSum(
        [
            (0, image_rows, d_key_image),
            (row_image, image_rows, d_value_image),
            (2 * row_image, cross_text, d_merge_text),
            (3 * row_image, text_rows, d_query_text),
        ],
        3 * row_image + row_text,
        inner,
        sizes,
    )
    weight_image_query = taken(all_image, image_at[0])
    weight_text_held = side_by_side(all_image, image_at[1:3])
    full_image_merge = taken(all_image, image_at[3])
    full_image_up = taken(all_image, image_at[4])
    full_image_down = taken(all_image, image_at[5])
    full_image_self = side_by_side(all_image, image_at[6:9])
    full_image_mix = taken(all_image, image_at[9])

    image_rows_2 = sum_text.advance(image_rows)
    image_rows_2 = sum_first.advance(image_rows_2)
    query_image = pairs_of(project(image_rows_2, weight_image_query).astype(BF16))
    held_text = pairs_of(project(text_rows, weight_text_held).astype(BF16))
    cross_image = rows_of(attend((query_image, 0), (held_text, 0), (held_text, 1), text_fill, inner, HEADS))
    unit_image_1, rate_image_1 = normed_rows(image_rows.astype(F32) + project(cross_image, full_image_merge))

    out_image, saved_image = forward(
        unit_image_1,
        full["image_gain_cross"],
        full_image_up,
        full["image_bias"],
        full_image_down,
        full["image_gain_ffn"],
        full_image_self,
        full_image_mix,
        full["image_gain_self"],
        image_fill,
        image_keep,
        IMAGE_HEADS,
    )
    d_image_out, *saved_image = sum_text.advance(d_image_out, *saved_image)
    d_sum_image, g_image_mix, g_image_self, g_image_gain_ffn, g_image_gain_self = self_backward(
        saved_image,
        full["image_gain_ffn"],
        full_image_self,
        full_image_mix,
        full["image_gain_self"],
        image_fill,
        image_keep,
        d_image_out,
        IMAGE_HEADS,
    )
    d_sum_image = sum_first.advance(d_sum_image)
    d_resid_image, g_image_up, g_image_down, g_image_bias, g_image_gain_cross = feed_backward(
        saved_image,
        d_sum_image,
        unit_image_1,
        rate_image_1,
        full["image_gain_cross"],
        full_image_up,
        full_image_down,
    )
    d_resid_image = sum_text.advance(d_resid_image)

    d_merge_image = d_resid_image.astype(BF16)
    sum_image = OwnerSum(
        [
            (0, cross_image, d_merge_image),
            (row_image, *g_image_up),
            (2 * row_image, *g_image_down),
            (3 * row_image, *g_image_self),
            (6 * row_image, *g_image_mix),
        ],
        7 * row_image,
        image_width,
        sizes,
    )
    d_merge_image = sum_image.advance(d_merge_image)
    d_heads_image = pairs_of(project_back(d_merge_image, full_image_merge).astype(BF16))
    d_query_image, d_key_text, d_value_text = map(
        rows_of,
        attend_back((query_image, 0), (held_text, 0), (held_text, 1), text_fill, d_heads_image, inner, HEADS),
    )
    d_query_image = sum_first.advance(d_query_image)
    g_vectors = (
        g_text_gain_cross,
        g_image_gain_cross,
        g_text_bias,
        g_text_gain_ffn,
        g_image_bias,
        g_image_gain_ffn,
        g_text_gain_self,
        g_image_gain_self,
    )
    row_vector = 2 * row_text
    vector_rows = max(len(vectors), 2 * row_image - row_vector)
    g_vector = jnp.stack(
        [
            jnp.pad(owned, ((0, 0), (0, inner - owned.shape[1])))
            for owned in (piece.astype(BF16).reshape(devices, -1) for piece in g_vectors)
        ],
        1,
    )
    g_vector = jnp.pad(g_vector, ((0, 0), (0, vector_rows - len(vectors)), (0, 0)))
    row_query = row_vector + vector_rows
    sum_last = OwnerSum(
        [
            (0, text_rows, d_key_text),
            (row_text, text_rows, d_value_text),
            (row_query, image_rows, d_query_image),
            (row_vector, g_vector),
        ],
        row_query + row_image,
        inner,
        sizes,
    )
    token = sum_image.advance(d_key_text)
    token = sum_last.advance(token)
    d_resid_text, d_resid_image, d_key_text = tie(d_resid_text, d_resid_image, token)
    grad_text = (
        d_resid_text
        + project_back(d_query_text, weight_text_query)
        + project_back(jnp.concatenate([d_key_text, d_value_text], 1), weight_text_held)
    )
    grad_image = (
        d_resid_image
        + project_back(d_query_image, weight_image_query)
        + project_back(jnp.concatenate([d_key_image, d_value_image], 1), weight_image_held)
    )
    token = sum_text.advance(d_key_text)
    for _ in range(2):
        token = sum_first.advance(token)
    for _ in range(5):
        token = sum_last.advance(token)
        token = sum_image.advance(token)

    def owned(total, pieces):
        return [total[start:end] for start, end in starts(pieces)]

    done = [one.result() for one in (sum_text, sum_first, sum_image, sum_last)]
    text_sums = owned(done[0], text_pieces[:-1])
    sum_image_key, sum_image_value, sum_text_merge, sum_text_query = owned(
        done[1], [image_key, image_value, text_merge, text_query]
    )
    image_sums = owned(done[2], image_pieces[3:])
    sum_text_key, sum_text_value = owned(done[3], [text_key, text_value])
    sum_vector = done[3][row_vector:row_query]
    sum_image_query = done[3][row_query:]
    owned_vector = {
        name: sum_vector[at, : piece.shape[0]] for at, (name, piece) in enumerate(zip(VECTOR_NAMES, vectors))
    }
    return (
        pairs_of(out_text)[:, :length],
        pairs_of(out_image)[:, :regions],
        pairs_of(grad_text)[:, :length],
        pairs_of(grad_image)[:, :regions],
        sum_text_query,
        sum_image_key,
        sum_image_value,
        sum_text_merge[:, :text_width],
        owned_vector["text_gain_cross"],
        sum_image_query,
        sum_text_key,
        sum_text_value,
        image_sums[0],
        owned_vector["image_gain_cross"],
        jnp.concatenate(text_sums[:ups], 1),
        owned_vector["text_bias"],
        text_sums[ups],
        owned_vector["text_gain_ffn"],
        image_sums[1],
        owned_vector["image_bias"],
        image_sums[2],
        owned_vector["image_gain_ffn"],
        jnp.concatenate(text_sums[ups + 1 : ups + 4], 1),
        text_sums[ups + 4],
        owned_vector["text_gain_self"],
        jnp.concatenate(image_sums[3:6], 1),
        image_sums[6],
        owned_vector["image_gain_self"],
    )


def solution(mesh):
    split = {1: P(AXES), 2: P(AXES, None), 3: P(AXES, None, None)}
    in_ranks = (3, 3, 1, 2, 3, 3) + tuple(
        1 if at in (4, 9, 11, 13, 15, 17, 20, 23) else 2 for at in range(24)
    )
    out_ranks = (3, 3, 3, 3) + in_ranks[6:]
    return jax.shard_map(
        functools.partial(per_device, dict(mesh.shape)),
        mesh=mesh,
        in_specs=tuple(split[rank] for rank in in_ranks),
        out_specs=tuple(split[rank] for rank in out_ranks),
        check_vma=False,
    )
```

```python
import functools
import math

import jax
import jax.numpy as jnp
from jax import lax
from jax.experimental import pallas as pl
from jax.experimental.pallas import tpu as pltpu
from jax.sharding import PartitionSpec as P

HEADS = 8
TEXT_HEADS = 12
IMAGE_HEADS = 8
EPSILON = 1e-05
MASKED = -1000000000.0
PADDED = -2000000000.0
LANES = 128
AXES = ("gx", "gy")
F32 = jnp.float32
BF16 = jnp.bfloat16
VMEM_BYTES = 48 * 1024 * 1024
VECTOR_NAMES = (
    "text_gain_cross",
    "image_gain_cross",
    "text_bias",
    "text_gain_ffn",
    "image_bias",
    "image_gain_ffn",
    "text_gain_self",
    "image_gain_self",
)


def project(left, right):
    return jnp.dot(left, right, preferred_element_type=F32)


def project_back(left, right):
    return lax.dot_general(left, right, (((1,), (1,)), ((), ())), preferred_element_type=F32)


def weight_grad(left, right):
    return lax.dot_general(left, right, (((0,), (0,)), ((), ())), preferred_element_type=F32)


def round_up(size, step):
    return -(-size // step) * step


def takes(microseconds):
    return pl.CostEstimate(flops=0, bytes_accessed=int(3.2e6 * microseconds), transcendentals=0)


class Order:
    last = []


def ordered_call(kernel, arrays, in_specs, **rest):
    after = [one for one in Order.last if all(one is not array for array in arrays)]
    given = len(arrays)

    def body(*refs):
        kernel(*refs[:given], *refs[given + len(after) :])

    out = pl.pallas_call(
        body,
        in_specs=list(in_specs) + [pl.BlockSpec(memory_space=pl.ANY)] * len(after),
        compiler_params=pltpu.CompilerParams(vmem_limit_bytes=VMEM_BYTES),
        **rest,
    )(*arrays, *after)
    Order.last = [out[0] if isinstance(out, (list, tuple)) else out]
    return out


def stack_halves(rows):
    wide = rows.astype(F32)
    first = lax.broadcasted_iota(jnp.int32, wide.shape, 1) < LANES // 2
    zero = jnp.zeros_like(wide)
    return jnp.concatenate([jnp.where(first, wide, zero), jnp.where(first, zero, wide)], 0).astype(BF16)


def join_halves(rows):
    count = rows.shape[0] // 2
    first = lax.broadcasted_iota(jnp.int32, (count, LANES), 1) < LANES // 2
    return jnp.where(first, rows[:count], rows[count:])


def probabilities(keys, queries, fill, scale):
    scores = project_back(keys, queries) * scale
    scores = jnp.where(fill < 0.0, fill, scores)
    powers = jnp.exp(scores - jnp.max(scores, 0, keepdims=True))
    return powers * (1.0 / jnp.sum(powers, 0, keepdims=True))


def head_blocks(queries_ref, size):
    count, _, width = queries_ref.shape
    return [(pair, slice(at, at + LANES)) for pair in range(count) for at in range(0, width, LANES)], size < LANES


def attend_kernel(size, queries_ref, keys_ref, values_ref, fill_ref, mixed_ref):
    scale = 1.0 / math.sqrt(size)
    blocks, split = head_blocks(queries_ref, size)
    queries = [stack_halves(queries_ref[p, :, b]) if split else queries_ref[p, :, b] for p, b in blocks]
    probs = [
        probabilities(keys_ref[p, :, b], query, fill_ref[p][:, :1], scale).astype(BF16)
        for (p, b), query in zip(blocks, queries)
    ]
    mixed = [weight_grad(prob, values_ref[p, :, b]) for (p, b), prob in zip(blocks, probs)]
    for (p, b), rows in zip(blocks, mixed):
        mixed_ref[p, :, b] = (join_halves(rows) if split else rows).astype(BF16)


def attend_back_kernel(
    size, queries_ref, keys_ref, values_ref, fill_ref, d_mixed_ref, d_queries_ref, d_keys_ref, d_values_ref
):
    scale = 1.0 / math.sqrt(size)
    blocks, split = head_blocks(queries_ref, size)
    fills = [fill_ref[p][:, :1] for p, _ in blocks]
    queries = [stack_halves(queries_ref[p, :, b]) if split else queries_ref[p, :, b] for p, b in blocks]
    grads = [stack_halves(d_mixed_ref[p, :, b]) if split else d_mixed_ref[p, :, b] for p, b in blocks]
    probs = [
        probabilities(keys_ref[p, :, b], query, fill, scale) for (p, b), query, fill in zip(blocks, queries, fills)
    ]
    d_probs = [project_back(values_ref[p, :, b], grad) for (p, b), grad in zip(blocks, grads)]
    for (p, b), prob, grad in zip(blocks, probs, grads):
        d_values_ref[p, :, b] = project(prob.astype(BF16), grad).astype(BF16)
    d_scores = [
        prob * (d_prob - jnp.sum(prob * d_prob, 0, keepdims=True)) for prob, d_prob in zip(probs, d_probs)
    ]
    d_scores = [jnp.where(fill < 0.0, 0.0, one).astype(BF16) for fill, one in zip(fills, d_scores)]
    for (p, b), one, query in zip(blocks, d_scores, queries):
        d_keys_ref[p, :, b] = (project(one, query) * scale).astype(BF16)
    for (p, b), one in zip(blocks, d_scores):
        rows = weight_grad(one, keys_ref[p, :, b]) * scale
        d_queries_ref[p, :, b] = (join_halves(rows) if split else rows).astype(BF16)


def attention_call(kernel, together, inputs, outputs, microseconds):
    pairs = inputs[0][0].shape[0]
    together = math.gcd(pairs, together)

    def spec(rows, width, column):
        return pl.BlockSpec((together, rows, width), lambda step: (step, 0, column))

    return ordered_call(
        kernel,
        [array for array, _, _ in inputs],
        [spec(array.shape[1], width, column) for array, width, column in inputs],
        grid=(pairs // together,),
        out_specs=[spec(rows, width, 0) for rows, width in outputs],
        out_shape=[jax.ShapeDtypeStruct((pairs, rows, width), BF16) for rows, width in outputs],
        cost_estimate=takes(microseconds),
    )


def attend(queries, keys, values, fill, width, heads):
    pairs, count = queries[0].shape[:2]
    inputs = [(array, width, column) for array, column in (queries, keys, values)] + [(fill, LANES, 0)]
    kernel = functools.partial(attend_kernel, width // heads)
    return attention_call(kernel, 4, inputs, [(count, width)], 4)[0]


def attend_back(queries, keys, values, fill, d_mixed, width, heads):
    pairs, count = queries[0].shape[:2]
    inputs = [(array, width, column) for array, column in (queries, keys, values)]
    inputs += [(fill, LANES, 0), (d_mixed, width, 0)]
    keyed = keys[0].shape[1]
    kernel = functools.partial(attend_back_kernel, width // heads)
    return attention_call(kernel, 2, inputs, [(count, width), (keyed, width), (keyed, width)], 7)


def tie(*values):
    return lax.optimization_barrier(values)


def gather(packed):
    return lax.all_gather(packed, AXES, axis=0, tiled=False)


def in_vmem(kernel, arrays, shapes, where):
    vmem, scalar = pl.BlockSpec(memory_space=pltpu.VMEM), pl.BlockSpec(memory_space=pltpu.SMEM)
    return ordered_call(
        kernel,
        [jnp.stack(where).astype(jnp.int32), *arrays],
        [scalar] + [vmem] * len(arrays),
        out_specs=[vmem] * len(shapes),
        out_shape=[jax.ShapeDtypeStruct(shape, BF16) for shape in shapes],
        cost_estimate=takes(3),
    )


def bit_of(which):
    return (lax.axis_index(which[0]) >> which[1]) & 1


def exchange(block, which):
    axis, bit = which
    return lax.ppermute(block, axis, [(at, at ^ (1 << bit)) for at in range(lax.axis_size(axis))])


def pack_kernel(pieces, *refs):
    out_ref = refs[-1]
    width = out_ref.shape[1]
    for source, column, row in pieces:
        wide = min(width, refs[source].shape[1] - column)
        out_ref[row : row + refs[source].shape[0], :wide] = refs[source][:, column : column + wide]


def pack_rows(arrays, width):
    arrays = [array[None, :] if array.ndim == 1 else array for array in arrays]
    pieces, row = [], 0
    for source, array in enumerate(arrays):
        for column in range(0, array.shape[1], width):
            pieces.append((source, column, row))
            row += array.shape[0]
    if any(array.shape[0] % 8 and array.shape[0] > 1 for array in arrays):
        blocks = [arrays[source][:, column : column + width] for source, column, _ in pieces]
        return jnp.concatenate([jnp.pad(one, ((0, 0), (0, width - one.shape[1]))) for one in blocks], 0)
    return ordered_call(
        functools.partial(pack_kernel, pieces),
        arrays,
        [pl.BlockSpec(array.shape, lambda step: (0, 0)) for array in arrays],
        grid=(1,),
        out_specs=pl.BlockSpec((row, width), lambda step: (0, 0)),
        out_shape=jax.ShapeDtypeStruct((row, width), BF16),
        cost_estimate=takes(1),
    )


def copy_kernel(pieces, *refs):
    out_ref, done = refs[-2:]
    width = out_ref.shape[1]
    copies = []
    for at, (source, column, row) in enumerate(pieces):
        rows = refs[source].shape[0]
        copies.append(
            pltpu.make_async_copy(
                refs[source].at[:, column : column + width], out_ref.at[row : row + rows, :], done.at[at]
            )
        )
    for one in copies:
        one.start()
    for one in copies:
        one.wait()


def copy_rows(arrays, width):
    pieces, row = [], 0
    for source, array in enumerate(arrays):
        for column in range(0, array.shape[1], width):
            pieces.append((source, column, row))
            row += array.shape[0]
    if any(array.shape[0] % 8 for array in arrays):
        return jnp.concatenate([arrays[source][:, column : column + width] for source, column, _ in pieces], 0)
    anywhere = pl.BlockSpec(memory_space=pl.ANY)
    return ordered_call(
        functools.partial(copy_kernel, pieces),
        arrays,
        [anywhere] * len(arrays),
        out_specs=anywhere,
        out_shape=jax.ShapeDtypeStruct((row, width), BF16),
        scratch_shapes=[pltpu.SemaphoreType.DMA((len(pieces),))],
        cost_estimate=takes(2),
    )


def join_kernel(count, where_ref, *refs):
    outs = refs[2 * count :]
    shares = len(outs) // count
    for part in range(count):
        own, (block_ref, got_ref) = where_ref[part], refs[2 * part : 2 * part + 2]
        for share in range(shares):
            out_ref = outs[part * shares + share]
            width = out_ref.shape[-1]
            columns = slice(share * width, (share + 1) * width)
            for before in range(block_ref.shape[0]):
                out_ref[before, own] = block_ref[before, :, :, columns]
                out_ref[before, 1 - own] = got_ref[before, :, :, columns]


def joined(pairs, shares=1):
    arrays, shapes, where, news = [], [], [], []
    for block, got, have, which in pairs:
        new = [one for one in which[1] if one in have or one == which[0]]
        place = new.index(which[0])
        before, behind = 1 << place, 1 << (len(have) - place)
        rows, width = block.shape[-2:]
        arrays += [one.reshape(before, behind, rows, width) for one in (block, got)]
        shapes += [(before, 2, behind, rows, width // shares)] * shares
        where.append(bit_of(which[0]))
        news.append(new)
    outs = in_vmem(functools.partial(join_kernel, len(pairs)), arrays, shapes, where)
    return [
        (out.reshape((2,) * len(news[at // shares]) + out.shape[-2:]), news[at // shares])
        for at, out in enumerate(outs)
    ]


def unpack_kernel(pieces, own_ref, *refs):
    parts, outs = refs[: len(refs) - len(pieces)], refs[len(refs) - len(pieces) :]
    shares = len(parts) // 2
    for out_ref, firsts in zip(outs, pieces):
        rows = out_ref.shape[3]
        for source in range(2):
            core = own_ref[0] if source == 0 else 1 - own_ref[0]
            at = 0
            for first in firsts:
                for part_ref in parts[source * shares : (source + 1) * shares]:
                    width = part_ref.shape[-1]
                    out_ref[0, core, :, :, at : at + width] = part_ref[0, :, first : first + rows, :]
                    at += width


def gather_weights(pieces, vectors, sizes, meanwhile):
    core, y_bits, x_bits, z_bits = mesh_axes_bits(sizes)
    order = mesh_bits(sizes)
    shards = [shard for group in pieces for shard in group]
    width = shards[0].shape[1]
    packed = pack_rows(shards + list(vectors), width)
    if not sizes["aligned"] or len(core) != 1 or len(x_bits) != len(y_bits) or not z_bits:
        meanwhile()
        gathered, at, out = gather(packed), 0, []
        for group in pieces:
            blocks = []
            for shard in group:
                blocks.append(whole(gathered[:, at : at + shard.shape[0]]))
                at += shard.shape[0]
            out.append(jnp.concatenate(blocks, 1))
        return out + [whole(gathered[:, at:])]
    meanwhile()
    parts = [(packed, [])]
    for step, which in enumerate(reversed(z_bits)):
        block, have = parts[0]
        parts = joined([(block, exchange(block, which), have, (which, order))], 2 if step == len(z_bits) - 1 else 1)
    for steps in zip(y_bits + x_bits, x_bits + y_bits):
        flying = [(block, exchange(block, which), have, (which, order)) for (block, have), which in zip(parts, steps)]
        parts = joined(flying)
    groups, others, rows = sizes["gx"] // 2, sizes["gy"], packed.shape[0]
    halves = [block.reshape(groups, others, rows, width // 2) for block, _ in parts]
    halves += [exchange(block, core[0]) for block in halves]
    firsts, shapes, at = [], [], 0
    for group in pieces:
        firsts.append([])
        for shard in group:
            firsts[-1].append(at)
            at += shard.shape[0]
        shapes.append((groups, 2, others, group[0].shape[0], width * len(group)))
    firsts.append([at])
    shapes.append((groups, 2, others, len(vectors), width))
    out = ordered_call(
        functools.partial(unpack_kernel, firsts),
        [bit_of(core[0]).astype(jnp.int32).reshape(1), *halves],
        [pl.BlockSpec(memory_space=pltpu.SMEM)]
        + [pl.BlockSpec((1, others, rows, width // 2), lambda step: (step, 0, 0, 0))] * 4,
        grid=(groups,),
        out_specs=[pl.BlockSpec((1,) + shape[1:], lambda step: (step, 0, 0, 0, 0)) for shape in shapes],
        out_shape=[jax.ShapeDtypeStruct(shape, BF16) for shape in shapes],
        cost_estimate=takes(6),
    )
    return [whole(block) for block in out]


def whole(block):
    return block.reshape(-1, block.shape[-1])


def owned_rows(matrix, devices):
    return matrix.reshape(devices, matrix.shape[0] // devices, matrix.shape[1])


def mesh_bits(sizes):
    bits = []
    for axis in AXES:
        bits += [(axis, bit) for bit in reversed(range(sizes[axis].bit_length() - 1))]
    return bits


def mesh_axes_bits(sizes):
    low = (sizes["gy"].bit_length() - 1) // 2
    bits = mesh_bits(sizes)[::-1]
    core = [one for one in bits if one == ("gx", 0)]
    rows = [one for one in bits if one[0] == "gx" and one[1] > 0]
    columns = [one for one in bits if one[0] == "gy" and one[1] < low]
    rest = [one for one in bits if one[0] == "gy" and one[1] >= low]
    return core, rows, columns, rest


def grad_kernel(per_core, left_ref, right_ref, core_ref, *refs):
    away_ref, kept_ref, whole_ref = refs[-3:]
    own = core_ref[0]
    grad = weight_grad(left_ref[...], right_ref[...])
    groups, _, width = whole_ref.shape
    if grad.shape[1] < width:
        grad = jnp.pad(grad, ((0, 0), (0, width - grad.shape[1])))
    whole_ref[...] = grad.reshape(whole_ref.shape)
    for group in range(groups // 2):
        shape = kept_ref.shape[1:]
        kept_ref[group] = whole_ref[2 * group + own].reshape(shape).astype(BF16)
        away_ref[group] = whole_ref[2 * group + 1 - own].reshape(shape).astype(BF16)


def grad_rows_kernel(left_ref, right_ref, core_ref, *refs):
    away_ref, kept_ref = refs[-2:]
    stays = pl.program_id(0) % 2 == core_ref[0]
    shape = kept_ref.shape[1:]
    grad = weight_grad(left_ref[...], right_ref[...]).astype(BF16).reshape(shape)

    @pl.when(stays)
    def _():
        kept_ref[0] = grad

    @pl.when(jnp.logical_not(stays))
    def _():
        away_ref[0] = grad


def place_kernel(terms_ref, core_ref, *refs):
    away_ref, kept_ref = refs[-2:]
    own = core_ref[0]
    for group in range(kept_ref.shape[0]):
        kept_ref[group] = terms_ref[group, own]
        away_ref[group] = terms_ref[group, 1 - own]


def pack_terms(pieces, rows, width, sizes):
    groups, others = sizes["gx"] // 2, sizes["gy"]
    core = (lax.axis_index("gx") & 1).astype(jnp.int32).reshape(1)
    shape = jax.ShapeDtypeStruct((groups, others, rows, width), BF16)
    buffers = []
    for piece in pieces:
        first, scratch = piece[0], []
        scalar = pl.BlockSpec(memory_space=pltpu.SMEM)
        if len(piece) == 2:
            terms = piece[1].reshape((groups, 2, others) + piece[1].shape[1:])
            count = terms.shape[3]
            kernel, arrays, grid, flops = place_kernel, [terms], (1,), 0
            in_specs = [pl.BlockSpec(terms.shape, lambda step: (0,) * 5)]
            place = pl.BlockSpec((groups, others, count, width), lambda step, at=first // count: (0, 0, at, 0))
        else:
            left, right = piece[1:]
            height, tall = left.shape
            count = tall // (2 * groups * others)
            arrays, flops = [left, right], 2 * height * tall * right.shape[1]
            if right.shape[1] <= width and tall >= 2048:
                kernel, grid = grad_rows_kernel, (2 * groups,)
                in_specs = [
                    pl.BlockSpec((height, tall // (2 * groups)), lambda step: (0, step)),
                    pl.BlockSpec(right.shape, lambda step: (0, 0)),
                ]
                place = pl.BlockSpec((1, others, count, width), lambda step, at=first // count: (step // 2, 0, at, 0))
            else:
                each = min(width, right.shape[1])
                kernel, grid = functools.partial(grad_kernel, groups), (right.shape[1] // each,)
                in_specs = [
                    pl.BlockSpec(left.shape, lambda step: (0, 0)),
                    pl.BlockSpec((height, each), lambda step: (0, step)),
                ]
                place = pl.BlockSpec(
                    (groups, others, count, width), lambda step, at=first // count: (0, 0, at + step, 0)
                )
                scratch = [pltpu.VMEM((2 * groups, tall // (2 * groups), width), F32)]
        assert first % count == 0
        arrays = arrays + [core] + buffers
        in_specs = in_specs + [scalar] + [pl.BlockSpec(memory_space=pl.ANY)] * len(buffers)
        buffers = list(
            ordered_call(
                kernel,
                arrays,
                in_specs,
                grid=grid,
                out_specs=[place, place],
                out_shape=[shape, shape],
                scratch_shapes=scratch,
                input_output_aliases={len(arrays) - 2: 0, len(arrays) - 1: 1} if buffers else {},
                cost_estimate=takes(1 + flops / 4.5e8),
            )
        )
    return buffers


def whole_kernel(left_ref, right_ref, *refs):
    refs[-1][...] = weight_grad(left_ref[...], right_ref[...]).reshape(refs[-1].shape).astype(BF16)


def scattered(pieces, rows, width, sizes):
    devices = sizes["gx"] * sizes["gy"]
    if not sizes["aligned"]:
        packed = jnp.zeros((devices, rows, width), BF16)
        for first, left, right in pieces:
            grad = weight_grad(left, right).astype(BF16)
            packed = lax.dynamic_update_slice(packed, grad.reshape(devices, -1, width), (0, first, 0))
    else:
        buffers = []
        for first, left, right in pieces:
            count = left.shape[1] // devices
            block = pl.BlockSpec((devices, count, width), lambda step, at=first // count: (0, at, 0))
            buffers = [
                ordered_call(
                    whole_kernel,
                    [left, right] + buffers,
                    [pl.BlockSpec(one.shape, lambda step: (0, 0)) for one in (left, right)]
                    + [pl.BlockSpec(memory_space=pl.ANY)] * len(buffers),
                    grid=(1,),
                    out_specs=block,
                    out_shape=jax.ShapeDtypeStruct((devices, rows, width), BF16),
                    input_output_aliases={2: 0} if buffers else {},
                    cost_estimate=takes(3),
                )
            ]
        (packed,) = buffers
    return lax.psum_scatter(packed.reshape(devices * rows, width), AXES, scatter_dimension=0, tiled=True)


def widen_kernel(low_ref, high_ref):
    high_ref[...] = low_ref[...].astype(F32)


def widened(low):
    whole_block = pl.BlockSpec(low.shape, lambda step: (0, 0))
    return ordered_call(
        widen_kernel,
        [low],
        [whole_block],
        grid=(1,),
        out_specs=whole_block,
        out_shape=jax.ShapeDtypeStruct(low.shape, F32),
        cost_estimate=takes(1),
    )


def split_kernel(where_ref, *refs):
    away_x_ref, kept_x_ref, away_y_ref, kept_y_ref = refs[-4:]
    x, y = where_ref[0], where_ref[1]
    half = kept_x_ref.shape[-1]
    left, right = slice(0, half), slice(half, 2 * half)
    stays = pl.program_id(2) == y
    row = 0
    for kept_ref, got_ref in zip(refs[:-4:2], refs[1:-4:2]):
        rows = slice(row, row + kept_ref.shape[-2])
        row += kept_ref.shape[-2]

        def added(at, columns, kept_ref=kept_ref, got_ref=got_ref):
            total = kept_ref[0, 0, 0, at, :, columns].astype(F32) + got_ref[0, 0, 0, at, :, columns].astype(F32)
            return total.astype(BF16)

        kept_x_ref[0, 0, 0, rows, :] = added(x, left)
        away_x_ref[0, 0, 0, rows, :] = added(1 - x, left)

        @pl.when(stays)
        def _(added=added, rows=rows):
            for at in range(2):
                kept_y_ref[0, 0, at, rows, :] = added(at, right)

        @pl.when(jnp.logical_not(stays))
        def _(added=added, rows=rows):
            for at in range(2):
                away_y_ref[0, 0, at, rows, :] = added(at, right)


def split_terms(pairs):
    groups, others, _, width = pairs[0][0].shape
    rows = sum(kept.shape[2] for kept, _ in pairs)
    where = jnp.stack([lax.axis_index("gy") & 1, (lax.axis_index("gx") >> 1) & 1]).astype(jnp.int32)
    high, z, half = groups // 2, others // 2, width // 2
    arrays = [one.reshape((high, 2, z, 2) + one.shape[2:]) for pair in pairs for one in pair]
    along_x = pl.BlockSpec((1, 1, 1, rows, half), lambda high, z, y: (high, y, z, 0, 0))
    along_y = pl.BlockSpec((1, 1, 2, rows, half), lambda high, z, y: (high, z, 0, 0, 0))
    shape_x = jax.ShapeDtypeStruct((high, 2, z, rows, half), BF16)
    shape_y = jax.ShapeDtypeStruct((high, z, 2, rows, half), BF16)
    size = groups * others * rows * width
    return ordered_call(
        split_kernel,
        [where] + arrays,
        [pl.BlockSpec(memory_space=pltpu.SMEM)]
        + [pl.BlockSpec((1, 1, 1) + array.shape[3:], lambda high, z, y: (high, y, z, 0, 0, 0)) for array in arrays],
        grid=(high, z, 2),
        out_specs=[along_x, along_x, along_y, along_y],
        out_shape=[shape_x, shape_x, shape_y, shape_y],
        cost_estimate=takes(2.8e-6 * size),
    )


def halve_kernel(count, where_ref, *refs):
    outs = refs[2 * count :]
    side = 0
    for part in range(count):
        own, (kept_ref, got_ref) = where_ref[part], refs[2 * part : 2 * part + 2]
        width = kept_ref.shape[-1]
        away_ref, stay_ref = (refs[-2], refs[-1]) if refs[-1].shape[-1] > width else refs[-2 * (count - part) :][:2]
        columns = slice(side, side + width) if refs[-1].shape[-1] > width else slice(0, width)
        side += width
        for before in range(kept_ref.shape[0]):
            for behind in range(kept_ref.shape[2]):
                for out_ref, at in ((away_ref, 1 - own), (stay_ref, own)):
                    total = kept_ref[before, at, behind].astype(F32) + got_ref[before, at, behind].astype(F32)
                    out_ref[before, behind, :, columns] = total.astype(BF16)


def halve_terms(parts, steps, join):
    arrays, where, shapes, lefts = [], [], [], []
    for (kept, got, bits), which in zip(parts, steps):
        place = bits.index(which)
        rows, width = kept.shape[-2:]
        before, behind = 1 << place, 1 << (len(bits) - place - 1)
        arrays += [one.reshape(before, 2, behind, rows, width) for one in (kept, got)]
        where.append(bit_of(which))
        lefts.append([one for one in bits if one != which])
        shapes += [(before, behind, rows, width)] * 2
    if join:
        shapes = [shape[:-1] + (2 * shape[-1],) for shape in shapes[:2]]
    outs = in_vmem(functools.partial(halve_kernel, len(parts)), arrays, shapes, where)
    outs = [out.reshape((2,) * len(lefts[0]) + out.shape[-2:]) for out in outs]
    return [
        tuple(outs[2 * at : 2 * at + 2]) + which + (left,)
        for at, (which, left) in enumerate(zip(steps[: len(outs) // 2], lefts))
    ]


def added_kernel(kept_ref, got_ref, total_ref):
    total_ref[...] = kept_ref[...].astype(F32) + got_ref[...].astype(F32)


def added(kept, got):
    vmem = pl.BlockSpec(memory_space=pltpu.VMEM)
    return ordered_call(
        added_kernel,
        [kept, got],
        [vmem, vmem],
        out_specs=vmem,
        out_shape=jax.ShapeDtypeStruct(kept.shape, F32),
        cost_estimate=takes(1),
    )


class OwnerSum:
    def __init__(self, width, sizes):
        core, y_bits, x_bits, z_bits = mesh_axes_bits(sizes)
        self.width, self.sizes, self.core, self.bits = width, sizes, core, mesh_bits(sizes)
        self.plan = [list(pair) for pair in zip(x_bits + y_bits, y_bits + x_bits)] + [[which] for which in z_bits]
        self.kernels = sizes["aligned"] and len(core) == 1 and bool(y_bits) and len(x_bits) == len(y_bits)
        self.terms, self.flying, self.parts = [], [], None

    def add(self, rows, *pieces):
        devices = self.sizes["gx"] * self.sizes["gy"]
        if self.kernels:
            away, kept = pack_terms(pieces, rows, self.width, self.sizes)
            self.terms.append((kept, exchange(away, self.core[0])))
            return
        packed = jnp.zeros((devices, rows, self.width), BF16)
        for piece in pieces:
            blocks = [piece[1]]
            if len(piece) == 3:
                grad = weight_grad(*piece[1:]).astype(BF16)
                blocks = jnp.split(grad, max(1, grad.shape[1] // self.width), 1)
            at = piece[0]
            for block in blocks:
                block = block.reshape(devices, -1, block.shape[-1])
                packed = lax.dynamic_update_slice(packed, block, (0, at, 0))
                at += block.shape[1]
        self.terms.append(packed)

    def advance(self):
        sends = None
        if self.terms and self.kernels:
            sends = self.first_split()
        elif self.terms:
            packed = jnp.concatenate(self.terms, 1)
            self.parts = [(packed.reshape((2,) * len(self.bits) + packed.shape[1:]), self.bits)]
            self.plan = [[which] for which in self.core] + self.plan
        elif self.plan and self.kernels:
            sends = self.next_sends()
        elif self.kernels:
            self.parts = [(added(*self.flying[0][:2]), [])]
        else:
            self.parts = [
                ((kept.astype(F32) + got.astype(F32)).astype(BF16 if self.plan else F32), bits)
                for kept, got, bits in self.flying
            ]
        self.terms, self.flying = [], []
        if sends is None and self.plan:
            sends = self.halves()
        for away, kept, axis, bit, left in sends or []:
            self.flying.append((kept, exchange(away, (axis, bit)), left))

    def first_split(self):
        bits = [one for one in self.bits if one not in self.core]
        out = split_terms(self.terms)
        sends = []
        for part, which in enumerate(self.plan.pop(0)):
            left = [one for one in bits if one != which]
            away, kept = (one.reshape((2,) * len(left) + one.shape[-2:]) for one in out[2 * part : 2 * part + 2])
            sends.append((away, kept) + which + (left,))
        return sends

    def next_sends(self):
        steps = self.plan.pop(0)
        join = len(steps) < len(self.flying)
        return halve_terms(self.flying, steps * 2 if join else steps, join)

    def halves(self):
        step = self.plan.pop(0)
        if len(step) == 2 and len(self.parts) == 1:
            total, bits = self.parts[0]
            self.parts = [(total[..., : self.width // 2], bits), (total[..., self.width // 2 :], bits)]
        if len(step) == 1 and len(self.parts) == 2:
            self.parts = [(jnp.concatenate([self.parts[0][0], self.parts[1][0]], -1), self.parts[0][1])]
        sends = []
        for (total, bits), (axis, bit) in zip(self.parts, step):
            place = bits.index((axis, bit))
            own = (lax.axis_index(axis) >> bit) & 1
            away = lax.dynamic_index_in_dim(total, 1 - own, place, keepdims=False)
            kept = lax.dynamic_index_in_dim(total, own, place, keepdims=False)
            sends.append((away, kept, axis, bit, [one for one in bits if one != (axis, bit)]))
        return sends

    def result(self):
        while self.plan or self.flying:
            self.advance()
        return self.parts[0][0].astype(F32)


def normed_rows(values_in):
    centred = values_in - jnp.mean(values_in, -1, keepdims=True)
    rate = lax.rsqrt(jnp.mean(centred * centred, -1, keepdims=True) + EPSILON)
    return centred * rate, rate


def normed_back(unit, rate, gain, d_out):
    d_unit = d_out * gain
    mean_unit = jnp.mean(d_unit, -1, keepdims=True)
    mean_cross = jnp.mean(d_unit * unit, -1, keepdims=True)
    return rate * (d_unit - mean_unit - unit * mean_cross), jnp.sum(d_out * unit, 0)


GELU_RATE = math.sqrt(2.0 / math.pi)
GELU_CUBE = 0.044715


def gelu(values_in):
    inner = jnp.tanh(GELU_RATE * (values_in + GELU_CUBE * values_in * values_in * values_in))
    return 0.5 * values_in * (1.0 + inner)


def gelu_slope(values_in):
    square = values_in * values_in
    inner = jnp.tanh(GELU_RATE * values_in * (1.0 + GELU_CUBE * square))
    return 0.5 * (1.0 + inner) + 0.5 * values_in * (1.0 - inner * inner) * GELU_RATE * (1.0 + 3.0 * GELU_CUBE * square)


def per_device(sizes, *given):
    (
        text_tokens,
        image_regions,
        caption_lengths,
        region_mask,
        text_cotangent,
        image_cotangent,
        text_query,
        image_key,
        image_value,
        text_merge,
        text_gain_cross,
        image_query,
        text_key,
        text_value,
        image_merge,
        image_gain_cross,
        text_up,
        text_bias,
        text_down,
        text_gain_ffn,
        image_up,
        image_bias,
        image_down,
        image_gain_ffn,
        text_self,
        text_mix,
        text_gain_self,
        image_self,
        image_mix,
        image_gain_self,
    ) = given
    matrices = [array for array in given[6:] if array.ndim == 2]
    sizes = dict(sizes, aligned=all(array.shape[0] % 8 == 0 for array in matrices))
    devices = sizes["gx"] * sizes["gy"]
    pairs, length, text_width = text_tokens.shape
    regions, image_width = image_regions.shape[1:]
    inner = text_query.shape[1]

    vectors = (
        text_gain_cross,
        image_gain_cross,
        text_bias,
        text_gain_ffn,
        image_bias,
        image_gain_ffn,
        text_gain_self,
        image_gain_self,
    )
    text_pieces = jnp.split(text_up, text_up.shape[1] // text_width, 1) + [text_down]
    text_pieces += jnp.split(text_self, 3, 1) + [text_mix, text_merge]
    image_pieces = [image_query, text_key, text_value, image_merge, image_up, image_down]
    image_pieces += jnp.split(image_self, 3, 1) + [image_mix]
    def starts(pieces):
        marks = [0]
        for piece in pieces:
            marks.append(marks[-1] + piece.shape[0])
        return list(zip(marks[:-1], marks[1:]))

    def taken(block, at):
        return whole(block[:, at[0] : at[1]])

    def side_by_side(block, spans):
        return jnp.concatenate([taken(block, at) for at in spans], 1)

    text_at, image_at = starts(text_pieces), starts(image_pieces)
    packed = []

    def pack_image():
        shards = [image_query, text_key, text_value, image_merge, image_up, image_down, image_self, image_mix]
        packed.append(pack_rows(shards, inner))

    Order.last = []
    all_text = gather(copy_rows([text_up, text_down, text_self, text_mix, text_merge], text_width))
    weight_text_query, weight_image_held, all_vectors = gather_weights(
        [[text_query], [image_key, image_value]], vectors, sizes, pack_image
    )
    (packed_image,) = packed

    text_slots, image_slots = round_up(length, 8), round_up(regions, 8)

    def padded(array, slots):
        array = jnp.pad(array, ((0, 0), (0, slots - array.shape[1]), (0, 0)))
        return array.reshape(pairs * slots, array.shape[2])

    def rows_of(array):
        return array.reshape(-1, array.shape[-1])

    def pairs_of(array):
        return array.reshape(pairs, array.shape[0] // pairs, array.shape[1])

    def fill_of(live, count):
        slots = live.shape[1]
        fill = jnp.where(live, 0.0, jnp.where(jnp.arange(slots)[None, :] < count, MASKED, PADDED))
        return jnp.broadcast_to(fill[:, :, None], (pairs, slots, LANES)).astype(F32)

    text_rows, image_rows = padded(text_tokens, text_slots), padded(image_regions, image_slots)
    d_text_out = padded(text_cotangent, text_slots)
    d_image_out = padded(image_cotangent, image_slots)
    text_live = jnp.arange(text_slots)[None, :] < caption_lengths[:, None]
    image_live = jnp.pad(region_mask, ((0, 0), (0, image_slots - regions))) > 0
    text_fill, image_fill = fill_of(text_live, length), fill_of(image_live, regions)
    text_keep = text_live.astype(F32).reshape(-1, 1)
    image_keep = image_live.astype(F32).reshape(-1, 1)

    query_text = pairs_of(project(text_rows, weight_text_query).astype(BF16))
    held_image = pairs_of(project(image_rows, weight_image_held).astype(BF16))
    mixed_cross = attend((query_text, 0), (held_image, 0), (held_image, 1), image_fill, inner, HEADS)
    mixed_cross, packed_image = tie(mixed_cross, packed_image)
    all_image = gather(packed_image)
    cross_text = rows_of(mixed_cross)
    ups = text_up.shape[1] // text_width
    full_text_merge = taken(all_text, text_at[ups + 5])
    unit_text_1, rate_text_1 = normed_rows(text_rows.astype(F32) + project(cross_text, full_text_merge))

    full_text_up = side_by_side(all_text, text_at[:ups])
    full_text_down = taken(all_text, text_at[ups])
    full_text_self = side_by_side(all_text, text_at[ups + 1 : ups + 4])
    full_text_mix = taken(all_text, text_at[ups + 4])
    full = {
        name: all_vectors.reshape(devices, len(vectors), inner)[:, at, : piece.shape[0]].reshape(-1).astype(F32)
        for at, (name, piece) in enumerate(zip(VECTOR_NAMES, vectors))
    }

    def forward(unit_1, gain_1, up, bias, down, gain_2, joint, mix, gain_3, fill, keep, heads):
        width = unit_1.shape[1]
        first = unit_1 * gain_1
        first_low = first.astype(BF16)
        hidden = project(first_low, up) + bias
        active, slope = tie(gelu(hidden).astype(BF16), gelu_slope(hidden).astype(BF16))
        unit_2, rate_2 = normed_rows(first + project(active, down))
        second = unit_2 * gain_2
        second_low = second.astype(BF16)
        triple = pairs_of(project(second_low, joint).astype(BF16))
        mixed = rows_of(attend((triple, 0), (triple, 1), (triple, 2), fill, width, heads))
        unit_3, rate_3 = normed_rows(second + project(mixed, mix))
        out = (unit_3 * gain_3 * keep).astype(BF16)
        return out, (first_low, active, slope, unit_2, rate_2, second_low, triple, mixed, unit_3, rate_3)

    def self_backward(saved, gain_2, joint, mix, gain_3, fill, keep, d_out, heads):
        _, _, _, unit_2, rate_2, second_low, triple, mixed, unit_3, rate_3 = saved
        width = unit_2.shape[1]
        d_third, g_gain_3 = normed_back(unit_3, rate_3, gain_3, d_out.astype(F32) * keep)
        d_branch = d_third.astype(BF16)
        d_mixed = pairs_of(project_back(d_branch, mix).astype(BF16))
        d_triple = attend_back((triple, 0), (triple, 1), (triple, 2), fill, d_mixed, width, heads)
        d_triple = rows_of(jnp.concatenate(d_triple, -1))
        d_second = d_third + project_back(d_triple, joint)
        d_sum, g_gain_2 = normed_back(unit_2, rate_2, gain_2, d_second)
        return d_sum, (mixed, d_branch), (second_low, d_triple), g_gain_2, g_gain_3

    def feed_backward(saved, d_sum, unit_1, rate_1, gain_1, up, down):
        first_low, active, slope = saved[:3]
        d_sum_low = d_sum.astype(BF16)
        d_hidden = (slope.astype(F32) * project_back(d_sum_low, down)).astype(BF16)
        g_bias = jnp.sum(d_hidden.astype(F32), 0)
        d_first = d_sum + project_back(d_hidden, up)
        d_resid, g_gain_1 = normed_back(unit_1, rate_1, gain_1, d_first)
        return d_resid, (first_low, d_hidden), (active, d_sum_low), g_bias, g_gain_1

    out_text, saved_text = forward(
        unit_text_1,
        full["text_gain_cross"],
        full_text_up,
        full["text_bias"],
        full_text_down,
        full["text_gain_ffn"],
        full_text_self,
        full_text_mix,
        full["text_gain_self"],
        text_fill,
        text_keep,
        TEXT_HEADS,
    )
    d_sum_text, g_text_mix, g_text_self, g_text_gain_ffn, g_text_gain_self = self_backward(
        saved_text,
        full["text_gain_ffn"],
        full_text_self,
        full_text_mix,
        full["text_gain_self"],
        text_fill,
        text_keep,
        d_text_out,
        TEXT_HEADS,
    )
    row_text, row_image, row_down = text_query.shape[0], image_key.shape[0], text_down.shape[0]
    sum_a, sum_b = OwnerSum(text_width, sizes), OwnerSum(text_width, sizes)
    sum_c, sum_d, sum_e = OwnerSum(inner, sizes), OwnerSum(inner, sizes), OwnerSum(inner, sizes)
    sum_a.add(4 * row_text, (0, *g_text_self), (3 * row_text, *g_text_mix))
    d_resid_text, g_text_up, g_text_down, g_text_bias, g_text_gain_cross = feed_backward(
        saved_text, d_sum_text, unit_text_1, rate_text_1, full["text_gain_cross"], full_text_up, full_text_down
    )
    row_down, row_self = text_at[ups][0], text_at[ups + 1][0]
    sum_a.advance()
    sum_b.add(ups * row_text, (0, *g_text_up))
    sum_a.advance()
    sum_b.add(row_down, (0, *g_text_down))
    d_merge_text = d_resid_text.astype(BF16)
    sum_b.add(text_merge.shape[0], (0, cross_text, d_merge_text))
    d_heads_text = pairs_of(project_back(d_merge_text, full_text_merge).astype(BF16))
    d_query_text, d_key_image, d_value_image = map(
        rows_of,
        attend_back((query_text, 0), (held_image, 0), (held_image, 1), image_fill, d_heads_text, inner, HEADS),
    )
    sum_b.advance()
    sum_a.advance()
    row_first = round_up(2 * row_image, row_text)
    sums_first = scattered(
        [(0, image_rows, d_key_image), (row_image, image_rows, d_value_image), (row_first, text_rows, d_query_text)],
        row_first + row_text,
        inner,
        sizes,
    )
    weight_image_query = taken(all_image, image_at[0])
    weight_text_held = side_by_side(all_image, image_at[1:3])
    full_image_merge = taken(all_image, image_at[3])
    full_image_up = taken(all_image, image_at[4])
    full_image_down = taken(all_image, image_at[5])
    full_image_self = side_by_side(all_image, image_at[6:9])
    full_image_mix = taken(all_image, image_at[9])

    query_image = pairs_of(project(image_rows, weight_image_query).astype(BF16))
    held_text = pairs_of(project(text_rows, weight_text_held).astype(BF16))
    cross_image = rows_of(attend((query_image, 0), (held_text, 0), (held_text, 1), text_fill, inner, HEADS))
    sum_a.advance()
    unit_image_1, rate_image_1 = normed_rows(image_rows.astype(F32) + project(cross_image, full_image_merge))

    out_image, saved_image = forward(
        unit_image_1,
        full["image_gain_cross"],
        full_image_up,
        full["image_bias"],
        full_image_down,
        full["image_gain_ffn"],
        full_image_self,
        full_image_mix,
        full["image_gain_self"],
        image_fill,
        image_keep,
        IMAGE_HEADS,
    )
    sum_b.advance()
    sum_a.advance()
    d_sum_image, g_image_mix, g_image_self, g_image_gain_ffn, g_image_gain_self = self_backward(
        saved_image,
        full["image_gain_ffn"],
        full_image_self,
        full_image_mix,
        full["image_gain_self"],
        image_fill,
        image_keep,
        d_image_out,
        IMAGE_HEADS,
    )
    sum_c.add(4 * row_image, (0, *g_image_self), (3 * row_image, *g_image_mix))
    sum_b.advance()
    d_resid_image, g_image_up, g_image_down, g_image_bias, g_image_gain_cross = feed_backward(
        saved_image,
        d_sum_image,
        unit_image_1,
        rate_image_1,
        full["image_gain_cross"],
        full_image_up,
        full_image_down,
    )

    sum_c.advance()
    sum_b.advance()
    d_merge_image = d_resid_image.astype(BF16)
    sum_e.add(
        3 * row_image,
        (0, cross_image, d_merge_image),
        (row_image, *g_image_up),
        (2 * row_image, *g_image_down),
    )
    d_heads_image = pairs_of(project_back(d_merge_image, full_image_merge).astype(BF16))
    d_query_image, d_key_text, d_value_text = map(
        rows_of,
        attend_back((query_image, 0), (held_text, 0), (held_text, 1), text_fill, d_heads_image, inner, HEADS),
    )
    g_vectors = (
        g_text_gain_cross,
        g_image_gain_cross,
        g_text_bias,
        g_text_gain_ffn,
        g_image_bias,
        g_image_gain_ffn,
        g_text_gain_self,
        g_image_gain_self,
    )
    row_vector = 2 * row_text
    vector_rows = max(len(vectors), round_up(row_vector + len(vectors), row_image) - row_vector)
    row_query = row_vector + vector_rows
    g_vector = jnp.stack(
        [
            jnp.pad(owned, ((0, 0), (0, inner - owned.shape[1])))
            for owned in (piece.astype(BF16).reshape(devices, -1) for piece in g_vectors)
        ],
        1,
    )
    g_vector = jnp.pad(g_vector, ((0, 0), (0, vector_rows - len(vectors)), (0, 0)))
    sum_c.advance()
    sum_e.advance()
    sum_b.advance()
    sum_d.add(
        row_query + row_image,
        (0, text_rows, d_key_text),
        (row_text, text_rows, d_value_text),
        (row_query, image_rows, d_query_image),
        (row_vector, g_vector),
    )
    sum_c.advance()
    sum_d.advance()
    grad_text = (
        d_resid_text
        + project_back(d_query_text, weight_text_query)
        + project_back(jnp.concatenate([d_key_text, d_value_text], 1), weight_text_held)
    )
    grad_image = (
        d_resid_image
        + project_back(d_query_image, weight_image_query)
        + project_back(jnp.concatenate([d_key_image, d_value_image], 1), weight_image_held)
    )
    sum_e.advance()
    sum_c.advance()
    sum_d.advance()
    sum_e.advance()
    sum_c.advance()
    sum_d.advance()
    sum_e.advance()
    sum_d.advance()
    sum_e.advance()
    sum_d.advance()

    def owned(total, pieces):
        return [total[start:end] for start, end in starts(pieces)]

    sums_first = widened(sums_first)
    sums_a, sums_b, sums_c, sums_d, sums_e = [one.result() for one in (sum_a, sum_b, sum_c, sum_d, sum_e)]
    text_selfs = owned(sums_a, text_pieces[ups + 1 : ups + 5])
    text_sums = owned(sums_b, text_pieces[: ups + 1] + [text_merge])
    image_firsts = owned(sums_first, [image_key, image_value]) + [sums_first[row_first : row_first + row_text]]
    image_selfs = owned(sums_c, image_pieces[6:10])
    image_sums = owned(sums_e, image_pieces[3:6]) + owned(sums_d, [text_key, text_value])
    sum_vector = sums_d[row_vector:row_query]
    owned_vector = {
        name: sum_vector[at, : piece.shape[0]] for at, (name, piece) in enumerate(zip(VECTOR_NAMES, vectors))
    }
    return (
        pairs_of(out_text)[:, :length],
        pairs_of(out_image)[:, :regions],
        pairs_of(grad_text)[:, :length],
        pairs_of(grad_image)[:, :regions],
        image_firsts[2],
        image_firsts[0],
        image_firsts[1],
        text_sums[ups + 1],
        owned_vector["text_gain_cross"],
        sums_d[row_query:],
        image_sums[3],
        image_sums[4],
        image_sums[0],
        owned_vector["image_gain_cross"],
        jnp.concatenate(text_sums[:ups], 1),
        owned_vector["text_bias"],
        text_sums[ups],
        owned_vector["text_gain_ffn"],
        image_sums[1],
        owned_vector["image_bias"],
        image_sums[2],
        owned_vector["image_gain_ffn"],
        jnp.concatenate(text_selfs[:3], 1),
        text_selfs[3],
        owned_vector["text_gain_self"],
        jnp.concatenate(image_selfs[:3], 1),
        image_selfs[3],
        owned_vector["image_gain_self"],
    )


def solution(mesh):
    split = {1: P(AXES), 2: P(AXES, None), 3: P(AXES, None, None)}
    in_ranks = (3, 3, 1, 2, 3, 3) + tuple(
        1 if at in (4, 9, 11, 13, 15, 17, 20, 23) else 2 for at in range(24)
    )
    out_ranks = (3, 3, 3, 3) + in_ranks[6:]
    return jax.shard_map(
        functools.partial(per_device, dict(mesh.shape)),
        mesh=mesh,
        in_specs=tuple(split[rank] for rank in in_ranks),
        out_specs=tuple(split[rank] for rank in out_ranks),
        check_vma=False,
    )
```

```python
import functools
import math

import jax
import jax.numpy as jnp
from jax import lax
from jax.experimental import pallas as pl
from jax.experimental.pallas import tpu as pltpu
from jax.sharding import PartitionSpec as P

HEADS = 8
TEXT_HEADS = 12
IMAGE_HEADS = 8
EPSILON = 1e-05
MASKED = -1000000000.0
PADDED = -2000000000.0
LANES = 128
AXES = ("gx", "gy")
F32 = jnp.float32
BF16 = jnp.bfloat16
VMEM_BYTES = 48 * 1024 * 1024
VECTOR_NAMES = (
    "text_gain_cross",
    "image_gain_cross",
    "text_bias",
    "text_gain_ffn",
    "image_bias",
    "image_gain_ffn",
    "text_gain_self",
    "image_gain_self",
)


def project(left, right):
    return jnp.dot(left, right, preferred_element_type=F32)


def project_back(left, right):
    return lax.dot_general(left, right, (((1,), (1,)), ((), ())), preferred_element_type=F32)


def weight_grad(left, right):
    return lax.dot_general(left, right, (((0,), (0,)), ((), ())), preferred_element_type=F32)


def round_up(size, step):
    return -(-size // step) * step


def takes(microseconds):
    return pl.CostEstimate(flops=0, bytes_accessed=int(3.2e6 * microseconds), transcendentals=0)


class Order:
    last = []


def ordered_call(kernel, arrays, in_specs, **rest):
    after = [one for one in Order.last if all(one is not array for array in arrays)]
    given = len(arrays)

    def body(*refs):
        kernel(*refs[:given], *refs[given + len(after) :])

    out = pl.pallas_call(
        body,
        in_specs=list(in_specs) + [pl.BlockSpec(memory_space=pl.ANY)] * len(after),
        compiler_params=pltpu.CompilerParams(vmem_limit_bytes=VMEM_BYTES),
        **rest,
    )(*arrays, *after)
    Order.last = [out[0] if isinstance(out, (list, tuple)) else out]
    return out


def stack_halves(rows):
    wide = rows.astype(F32)
    first = lax.broadcasted_iota(jnp.int32, wide.shape, 1) < LANES // 2
    zero = jnp.zeros_like(wide)
    return jnp.concatenate([jnp.where(first, wide, zero), jnp.where(first, zero, wide)], 0).astype(BF16)


def join_halves(rows):
    count = rows.shape[0] // 2
    first = lax.broadcasted_iota(jnp.int32, (count, LANES), 1) < LANES // 2
    return jnp.where(first, rows[:count], rows[count:])


def probabilities(keys, queries, fill, scale):
    scores = project_back(keys, queries) * scale
    scores = jnp.where(fill < 0.0, fill, scores)
    powers = jnp.exp(scores - jnp.max(scores, 0, keepdims=True))
    return powers * (1.0 / jnp.sum(powers, 0, keepdims=True))


def head_blocks(queries_ref, size):
    count, _, width = queries_ref.shape
    return [(pair, slice(at, at + LANES)) for pair in range(count) for at in range(0, width, LANES)], size < LANES


def attend_kernel(size, queries_ref, keys_ref, values_ref, fill_ref, mixed_ref):
    scale = 1.0 / math.sqrt(size)
    blocks, split = head_blocks(queries_ref, size)
    queries = [stack_halves(queries_ref[p, :, b]) if split else queries_ref[p, :, b] for p, b in blocks]
    probs = [
        probabilities(keys_ref[p, :, b], query, fill_ref[p][:, :1], scale).astype(BF16)
        for (p, b), query in zip(blocks, queries)
    ]
    mixed = [weight_grad(prob, values_ref[p, :, b]) for (p, b), prob in zip(blocks, probs)]
    for (p, b), rows in zip(blocks, mixed):
        mixed_ref[p, :, b] = (join_halves(rows) if split else rows).astype(BF16)


def attend_back_kernel(
    size, queries_ref, keys_ref, values_ref, fill_ref, d_mixed_ref, d_queries_ref, d_keys_ref, d_values_ref
):
    scale = 1.0 / math.sqrt(size)
    blocks, split = head_blocks(queries_ref, size)
    fills = [fill_ref[p][:, :1] for p, _ in blocks]
    queries = [stack_halves(queries_ref[p, :, b]) if split else queries_ref[p, :, b] for p, b in blocks]
    grads = [stack_halves(d_mixed_ref[p, :, b]) if split else d_mixed_ref[p, :, b] for p, b in blocks]
    probs = [
        probabilities(keys_ref[p, :, b], query, fill, scale) for (p, b), query, fill in zip(blocks, queries, fills)
    ]
    d_probs = [project_back(values_ref[p, :, b], grad) for (p, b), grad in zip(blocks, grads)]
    for (p, b), prob, grad in zip(blocks, probs, grads):
        d_values_ref[p, :, b] = project(prob.astype(BF16), grad).astype(BF16)
    d_scores = [
        prob * (d_prob - jnp.sum(prob * d_prob, 0, keepdims=True)) for prob, d_prob in zip(probs, d_probs)
    ]
    d_scores = [jnp.where(fill < 0.0, 0.0, one).astype(BF16) for fill, one in zip(fills, d_scores)]
    for (p, b), one, query in zip(blocks, d_scores, queries):
        d_keys_ref[p, :, b] = (project(one, query) * scale).astype(BF16)
    for (p, b), one in zip(blocks, d_scores):
        rows = weight_grad(one, keys_ref[p, :, b]) * scale
        d_queries_ref[p, :, b] = (join_halves(rows) if split else rows).astype(BF16)


def attention_call(kernel, together, inputs, outputs, microseconds):
    pairs = inputs[0][0].shape[0]
    together = math.gcd(pairs, together)

    def spec(rows, width, column):
        return pl.BlockSpec((together, rows, width), lambda step: (step, 0, column))

    return ordered_call(
        kernel,
        [array for array, _, _ in inputs],
        [spec(array.shape[1], width, column) for array, width, column in inputs],
        grid=(pairs // together,),
        out_specs=[spec(rows, width, 0) for rows, width in outputs],
        out_shape=[jax.ShapeDtypeStruct((pairs, rows, width), BF16) for rows, width in outputs],
        cost_estimate=takes(microseconds),
    )


def attend(queries, keys, values, fill, width, heads):
    pairs, count = queries[0].shape[:2]
    inputs = [(array, width, column) for array, column in (queries, keys, values)] + [(fill, LANES, 0)]
    kernel = functools.partial(attend_kernel, width // heads)
    return attention_call(kernel, 4, inputs, [(count, width)], 4)[0]


def attend_back(queries, keys, values, fill, d_mixed, width, heads):
    pairs, count = queries[0].shape[:2]
    inputs = [(array, width, column) for array, column in (queries, keys, values)]
    inputs += [(fill, LANES, 0), (d_mixed, width, 0)]
    keyed = keys[0].shape[1]
    kernel = functools.partial(attend_back_kernel, width // heads)
    return attention_call(kernel, 2, inputs, [(count, width), (keyed, width), (keyed, width)], 7)


def tie(*values):
    return lax.optimization_barrier(values)


def gather(packed):
    return lax.all_gather(packed, AXES, axis=0, tiled=False)


def in_vmem(kernel, arrays, shapes, where):
    vmem, scalar = pl.BlockSpec(memory_space=pltpu.VMEM), pl.BlockSpec(memory_space=pltpu.SMEM)
    return ordered_call(
        kernel,
        [jnp.stack(where).astype(jnp.int32), *arrays],
        [scalar] + [vmem] * len(arrays),
        out_specs=[vmem] * len(shapes),
        out_shape=[jax.ShapeDtypeStruct(shape, BF16) for shape in shapes],
        cost_estimate=takes(3),
    )


def bit_of(which):
    return (lax.axis_index(which[0]) >> which[1]) & 1


def exchange(block, which):
    axis, bit = which
    return lax.ppermute(block, axis, [(at, at ^ (1 << bit)) for at in range(lax.axis_size(axis))])


def pack_kernel(pieces, *refs):
    out_ref = refs[-1]
    width = out_ref.shape[1]
    for source, column, row in pieces:
        wide = min(width, refs[source].shape[1] - column)
        out_ref[row : row + refs[source].shape[0], :wide] = refs[source][:, column : column + wide]


def pack_rows(arrays, width):
    arrays = [array[None, :] if array.ndim == 1 else array for array in arrays]
    pieces, row = [], 0
    for source, array in enumerate(arrays):
        for column in range(0, array.shape[1], width):
            pieces.append((source, column, row))
            row += array.shape[0]
    if any(array.shape[0] % 8 and array.shape[0] > 1 for array in arrays):
        blocks = [arrays[source][:, column : column + width] for source, column, _ in pieces]
        return jnp.concatenate([jnp.pad(one, ((0, 0), (0, width - one.shape[1]))) for one in blocks], 0)
    return ordered_call(
        functools.partial(pack_kernel, pieces),
        arrays,
        [pl.BlockSpec(array.shape, lambda step: (0, 0)) for array in arrays],
        grid=(1,),
        out_specs=pl.BlockSpec((row, width), lambda step: (0, 0)),
        out_shape=jax.ShapeDtypeStruct((row, width), BF16),
        cost_estimate=takes(1),
    )


def copy_kernel(pieces, *refs):
    out_ref, done = refs[-2:]
    width = out_ref.shape[1]
    copies = []
    for at, (source, column, row) in enumerate(pieces):
        rows = refs[source].shape[0]
        copies.append(
            pltpu.make_async_copy(
                refs[source].at[:, column : column + width], out_ref.at[row : row + rows, :], done.at[at]
            )
        )
    for one in copies:
        one.start()
    for one in copies:
        one.wait()


def copy_rows(arrays, width):
    pieces, row = [], 0
    for source, array in enumerate(arrays):
        for column in range(0, array.shape[1], width):
            pieces.append((source, column, row))
            row += array.shape[0]
    if any(array.shape[0] % 8 for array in arrays):
        return jnp.concatenate([arrays[source][:, column : column + width] for source, column, _ in pieces], 0)
    anywhere = pl.BlockSpec(memory_space=pl.ANY)
    return ordered_call(
        functools.partial(copy_kernel, pieces),
        arrays,
        [anywhere] * len(arrays),
        out_specs=anywhere,
        out_shape=jax.ShapeDtypeStruct((row, width), BF16),
        scratch_shapes=[pltpu.SemaphoreType.DMA((len(pieces),))],
        cost_estimate=takes(2),
    )


def join_kernel(count, where_ref, *refs):
    outs = refs[2 * count :]
    shares = len(outs) // count
    for part in range(count):
        own, (block_ref, got_ref) = where_ref[part], refs[2 * part : 2 * part + 2]
        for share in range(shares):
            out_ref = outs[part * shares + share]
            width = out_ref.shape[-1]
            columns = slice(share * width, (share + 1) * width)
            for before in range(block_ref.shape[0]):
                out_ref[before, own] = block_ref[before, :, :, columns]
                out_ref[before, 1 - own] = got_ref[before, :, :, columns]


def joined(pairs, shares=1):
    arrays, shapes, where, news = [], [], [], []
    for block, got, have, which in pairs:
        new = [one for one in which[1] if one in have or one == which[0]]
        place = new.index(which[0])
        before, behind = 1 << place, 1 << (len(have) - place)
        rows, width = block.shape[-2:]
        arrays += [one.reshape(before, behind, rows, width) for one in (block, got)]
        shapes += [(before, 2, behind, rows, width // shares)] * shares
        where.append(bit_of(which[0]))
        news.append(new)
    outs = in_vmem(functools.partial(join_kernel, len(pairs)), arrays, shapes, where)
    return [
        (out.reshape((2,) * len(news[at // shares]) + out.shape[-2:]), news[at // shares])
        for at, out in enumerate(outs)
    ]


def unpack_kernel(pieces, own_ref, *refs):
    parts, outs = refs[: len(refs) - len(pieces)], refs[len(refs) - len(pieces) :]
    shares = len(parts) // 2
    for out_ref, firsts in zip(outs, pieces):
        rows = out_ref.shape[3]
        for source in range(2):
            core = own_ref[0] if source == 0 else 1 - own_ref[0]
            at = 0
            for first in firsts:
                for part_ref in parts[source * shares : (source + 1) * shares]:
                    width = part_ref.shape[-1]
                    out_ref[0, core, :, :, at : at + width] = part_ref[0, :, first : first + rows, :]
                    at += width


def gather_weights(pieces, vectors, sizes, meanwhile):
    core, y_bits, x_bits, z_bits = mesh_axes_bits(sizes)
    order = mesh_bits(sizes)
    shards = [shard for group in pieces for shard in group]
    width = shards[0].shape[1]
    packed = pack_rows(shards + list(vectors), width)
    if not sizes["aligned"] or len(core) != 1 or len(x_bits) != len(y_bits) or not z_bits:
        meanwhile()
        gathered, at, out = gather(packed), 0, []
        for group in pieces:
            blocks = []
            for shard in group:
                blocks.append(whole(gathered[:, at : at + shard.shape[0]]))
                at += shard.shape[0]
            out.append(jnp.concatenate(blocks, 1))
        return out + [whole(gathered[:, at:])]
    meanwhile()
    parts = [(packed, [])]
    for step, which in enumerate(reversed(z_bits)):
        block, have = parts[0]
        parts = joined([(block, exchange(block, which), have, (which, order))], 2 if step == len(z_bits) - 1 else 1)
    for steps in zip(y_bits + x_bits, x_bits + y_bits):
        flying = [(block, exchange(block, which), have, (which, order)) for (block, have), which in zip(parts, steps)]
        parts = joined(flying)
    groups, others, rows = sizes["gx"] // 2, sizes["gy"], packed.shape[0]
    halves = [block.reshape(groups, others, rows, width // 2) for block, _ in parts]
    halves += [exchange(block, core[0]) for block in halves]
    firsts, shapes, at = [], [], 0
    for group in pieces:
        firsts.append([])
        for shard in group:
            firsts[-1].append(at)
            at += shard.shape[0]
        shapes.append((groups, 2, others, group[0].shape[0], width * len(group)))
    firsts.append([at])
    shapes.append((groups, 2, others, len(vectors), width))
    out = ordered_call(
        functools.partial(unpack_kernel, firsts),
        [bit_of(core[0]).astype(jnp.int32).reshape(1), *halves],
        [pl.BlockSpec(memory_space=pltpu.SMEM)]
        + [pl.BlockSpec((1, others, rows, width // 2), lambda step: (step, 0, 0, 0))] * 4,
        grid=(groups,),
        out_specs=[pl.BlockSpec((1,) + shape[1:], lambda step: (step, 0, 0, 0, 0)) for shape in shapes],
        out_shape=[jax.ShapeDtypeStruct(shape, BF16) for shape in shapes],
        cost_estimate=takes(6),
    )
    return [whole(block) for block in out]


def whole(block):
    return block.reshape(-1, block.shape[-1])


def owned_rows(matrix, devices):
    return matrix.reshape(devices, matrix.shape[0] // devices, matrix.shape[1])


def mesh_bits(sizes):
    bits = []
    for axis in AXES:
        bits += [(axis, bit) for bit in reversed(range(sizes[axis].bit_length() - 1))]
    return bits


def mesh_axes_bits(sizes):
    low = (sizes["gy"].bit_length() - 1) // 2
    bits = mesh_bits(sizes)[::-1]
    core = [one for one in bits if one == ("gx", 0)]
    rows = [one for one in bits if one[0] == "gx" and one[1] > 0]
    columns = [one for one in bits if one[0] == "gy" and one[1] < low]
    rest = [one for one in bits if one[0] == "gy" and one[1] >= low]
    return core, rows, columns, rest


def grad_kernel(per_core, left_ref, right_ref, core_ref, *refs):
    away_ref, kept_ref, whole_ref = refs[-3:]
    own = core_ref[0]
    grad = weight_grad(left_ref[...], right_ref[...])
    groups, _, width = whole_ref.shape
    if grad.shape[1] < width:
        grad = jnp.pad(grad, ((0, 0), (0, width - grad.shape[1])))
    whole_ref[...] = grad.reshape(whole_ref.shape)
    for group in range(groups // 2):
        shape = kept_ref.shape[1:]
        kept_ref[group] = whole_ref[2 * group + own].reshape(shape).astype(BF16)
        away_ref[group] = whole_ref[2 * group + 1 - own].reshape(shape).astype(BF16)


def grad_rows_kernel(left_ref, right_ref, core_ref, *refs):
    away_ref, kept_ref = refs[-2:]
    stays = pl.program_id(0) % 2 == core_ref[0]
    shape = kept_ref.shape[1:]
    grad = weight_grad(left_ref[...], right_ref[...]).astype(BF16).reshape(shape)

    @pl.when(stays)
    def _():
        kept_ref[0] = grad

    @pl.when(jnp.logical_not(stays))
    def _():
        away_ref[0] = grad


def place_kernel(terms_ref, core_ref, *refs):
    away_ref, kept_ref = refs[-2:]
    own = core_ref[0]
    for group in range(kept_ref.shape[0]):
        kept_ref[group] = terms_ref[group, own]
        away_ref[group] = terms_ref[group, 1 - own]


def pack_terms(pieces, rows, width, sizes):
    groups, others = sizes["gx"] // 2, sizes["gy"]
    core = (lax.axis_index("gx") & 1).astype(jnp.int32).reshape(1)
    shape = jax.ShapeDtypeStruct((groups, others, rows, width), BF16)
    buffers = []
    for piece in pieces:
        first, scratch = piece[0], []
        scalar = pl.BlockSpec(memory_space=pltpu.SMEM)
        if len(piece) == 2:
            terms = piece[1].reshape((groups, 2, others) + piece[1].shape[1:])
            count = terms.shape[3]
            kernel, arrays, grid, flops = place_kernel, [terms], (1,), 0
            in_specs = [pl.BlockSpec(terms.shape, lambda step: (0,) * 5)]
            place = pl.BlockSpec((groups, others, count, width), lambda step, at=first // count: (0, 0, at, 0))
        else:
            left, right = piece[1:]
            height, tall = left.shape
            count = tall // (2 * groups * others)
            arrays, flops = [left, right], 2 * height * tall * right.shape[1]
            if right.shape[1] <= width and tall >= 2048:
                kernel, grid = grad_rows_kernel, (2 * groups,)
                in_specs = [
                    pl.BlockSpec((height, tall // (2 * groups)), lambda step: (0, step)),
                    pl.BlockSpec(right.shape, lambda step: (0, 0)),
                ]
                place = pl.BlockSpec((1, others, count, width), lambda step, at=first // count: (step // 2, 0, at, 0))
            else:
                each = min(width, right.shape[1])
                kernel, grid = functools.partial(grad_kernel, groups), (right.shape[1] // each,)
                in_specs = [
                    pl.BlockSpec(left.shape, lambda step: (0, 0)),
                    pl.BlockSpec((height, each), lambda step: (0, step)),
                ]
                place = pl.BlockSpec(
                    (groups, others, count, width), lambda step, at=first // count: (0, 0, at + step, 0)
                )
                scratch = [pltpu.VMEM((2 * groups, tall // (2 * groups), width), F32)]
        assert first % count == 0
        arrays = arrays + [core] + buffers
        in_specs = in_specs + [scalar] + [pl.BlockSpec(memory_space=pl.ANY)] * len(buffers)
        buffers = list(
            ordered_call(
                kernel,
                arrays,
                in_specs,
                grid=grid,
                out_specs=[place, place],
                out_shape=[shape, shape],
                scratch_shapes=scratch,
                input_output_aliases={len(arrays) - 2: 0, len(arrays) - 1: 1} if buffers else {},
                cost_estimate=takes(1 + flops / 4.5e8),
            )
        )
    return buffers


def whole_kernel(left_ref, right_ref, *refs):
    refs[-1][...] = weight_grad(left_ref[...], right_ref[...]).reshape(refs[-1].shape).astype(BF16)


def scattered(pieces, rows, width, sizes):
    devices = sizes["gx"] * sizes["gy"]
    if not sizes["aligned"]:
        packed = jnp.zeros((devices, rows, width), BF16)
        for first, left, right in pieces:
            grad = weight_grad(left, right).astype(BF16)
            packed = lax.dynamic_update_slice(packed, grad.reshape(devices, -1, width), (0, first, 0))
    else:
        buffers = []
        for first, left, right in pieces:
            count = left.shape[1] // devices
            block = pl.BlockSpec((devices, count, width), lambda step, at=first // count: (0, at, 0))
            buffers = [
                ordered_call(
                    whole_kernel,
                    [left, right] + buffers,
                    [pl.BlockSpec(one.shape, lambda step: (0, 0)) for one in (left, right)]
                    + [pl.BlockSpec(memory_space=pl.ANY)] * len(buffers),
                    grid=(1,),
                    out_specs=block,
                    out_shape=jax.ShapeDtypeStruct((devices, rows, width), BF16),
                    input_output_aliases={2: 0} if buffers else {},
                    cost_estimate=takes(3),
                )
            ]
        (packed,) = buffers
    return lax.psum_scatter(packed.reshape(devices * rows, width), AXES, scatter_dimension=0, tiled=True)


def widen_kernel(low_ref, high_ref):
    high_ref[...] = low_ref[...].astype(F32)


def widened(low):
    whole_block = pl.BlockSpec(low.shape, lambda step: (0, 0))
    return ordered_call(
        widen_kernel,
        [low],
        [whole_block],
        grid=(1,),
        out_specs=whole_block,
        out_shape=jax.ShapeDtypeStruct(low.shape, F32),
        cost_estimate=takes(1),
    )


def split_kernel(where_ref, *refs):
    away_x_ref, kept_x_ref, away_y_ref, kept_y_ref = refs[-4:]
    x, y = where_ref[0], where_ref[1]
    half = kept_x_ref.shape[-1]
    left, right = slice(0, half), slice(half, 2 * half)
    stays = pl.program_id(2) == y
    row = 0
    for kept_ref, got_ref in zip(refs[:-4:2], refs[1:-4:2]):
        rows = slice(row, row + kept_ref.shape[-2])
        row += kept_ref.shape[-2]

        def added(at, columns, kept_ref=kept_ref, got_ref=got_ref):
            total = kept_ref[0, 0, 0, at, :, columns].astype(F32) + got_ref[0, 0, 0, at, :, columns].astype(F32)
            return total.astype(BF16)

        kept_x_ref[0, 0, 0, rows, :] = added(x, left)
        away_x_ref[0, 0, 0, rows, :] = added(1 - x, left)

        @pl.when(stays)
        def _(added=added, rows=rows):
            for at in range(2):
                kept_y_ref[0, 0, at, rows, :] = added(at, right)

        @pl.when(jnp.logical_not(stays))
        def _(added=added, rows=rows):
            for at in range(2):
                away_y_ref[0, 0, at, rows, :] = added(at, right)


def split_terms(pairs):
    groups, others, _, width = pairs[0][0].shape
    rows = sum(kept.shape[2] for kept, _ in pairs)
    where = jnp.stack([lax.axis_index("gy") & 1, (lax.axis_index("gx") >> 1) & 1]).astype(jnp.int32)
    high, z, half = groups // 2, others // 2, width // 2
    arrays = [one.reshape((high, 2, z, 2) + one.shape[2:]) for pair in pairs for one in pair]
    along_x = pl.BlockSpec((1, 1, 1, rows, half), lambda high, z, y: (high, y, z, 0, 0))
    along_y = pl.BlockSpec((1, 1, 2, rows, half), lambda high, z, y: (high, z, 0, 0, 0))
    shape_x = jax.ShapeDtypeStruct((high, 2, z, rows, half), BF16)
    shape_y = jax.ShapeDtypeStruct((high, z, 2, rows, half), BF16)
    size = groups * others * rows * width
    return ordered_call(
        split_kernel,
        [where] + arrays,
        [pl.BlockSpec(memory_space=pltpu.SMEM)]
        + [pl.BlockSpec((1, 1, 1) + array.shape[3:], lambda high, z, y: (high, y, z, 0, 0, 0)) for array in arrays],
        grid=(high, z, 2),
        out_specs=[along_x, along_x, along_y, along_y],
        out_shape=[shape_x, shape_x, shape_y, shape_y],
        cost_estimate=takes(2.8e-6 * size),
    )


def halve_kernel(count, where_ref, *refs):
    outs = refs[2 * count :]
    side = 0
    for part in range(count):
        own, (kept_ref, got_ref) = where_ref[part], refs[2 * part : 2 * part + 2]
        width = kept_ref.shape[-1]
        away_ref, stay_ref = (refs[-2], refs[-1]) if refs[-1].shape[-1] > width else refs[-2 * (count - part) :][:2]
        columns = slice(side, side + width) if refs[-1].shape[-1] > width else slice(0, width)
        side += width
        for before in range(kept_ref.shape[0]):
            for behind in range(kept_ref.shape[2]):
                for out_ref, at in ((away_ref, 1 - own), (stay_ref, own)):
                    total = kept_ref[before, at, behind].astype(F32) + got_ref[before, at, behind].astype(F32)
                    out_ref[before, behind, :, columns] = total.astype(BF16)


def halve_terms(parts, steps, join):
    arrays, where, shapes, lefts = [], [], [], []
    for (kept, got, bits), which in zip(parts, steps):
        place = bits.index(which)
        rows, width = kept.shape[-2:]
        before, behind = 1 << place, 1 << (len(bits) - place - 1)
        arrays += [one.reshape(before, 2, behind, rows, width) for one in (kept, got)]
        where.append(bit_of(which))
        lefts.append([one for one in bits if one != which])
        shapes += [(before, behind, rows, width)] * 2
    if join:
        shapes = [shape[:-1] + (2 * shape[-1],) for shape in shapes[:2]]
    outs = in_vmem(functools.partial(halve_kernel, len(parts)), arrays, shapes, where)
    outs = [out.reshape((2,) * len(lefts[0]) + out.shape[-2:]) for out in outs]
    return [
        tuple(outs[2 * at : 2 * at + 2]) + which + (left,)
        for at, (which, left) in enumerate(zip(steps[: len(outs) // 2], lefts))
    ]


def passed_kernel(given_ref, same_ref):
    pass


def passed(array):
    anywhere = pl.BlockSpec(memory_space=pl.ANY)
    return ordered_call(
        passed_kernel,
        [array],
        [anywhere],
        out_specs=anywhere,
        out_shape=jax.ShapeDtypeStruct(array.shape, array.dtype),
        input_output_aliases={0: 0},
        cost_estimate=takes(0),
    )


def added_kernel(kept_ref, got_ref, total_ref):
    total_ref[...] = kept_ref[...].astype(F32) + got_ref[...].astype(F32)


def added(kept, got):
    vmem = pl.BlockSpec(memory_space=pltpu.VMEM)
    return ordered_call(
        added_kernel,
        [kept, got],
        [vmem, vmem],
        out_specs=vmem,
        out_shape=jax.ShapeDtypeStruct(kept.shape, F32),
        cost_estimate=takes(1),
    )


class OwnerSum:
    def __init__(self, width, sizes):
        core, y_bits, x_bits, z_bits = mesh_axes_bits(sizes)
        self.width, self.sizes, self.core, self.bits = width, sizes, core, mesh_bits(sizes)
        self.plan = [list(pair) for pair in zip(x_bits + y_bits, y_bits + x_bits)] + [[which] for which in z_bits]
        self.kernels = sizes["aligned"] and len(core) == 1 and bool(y_bits) and len(x_bits) == len(y_bits)
        self.held, self.terms, self.flying, self.parts = [], [], [], None

    def add(self, rows, *pieces, later=False):
        devices = self.sizes["gx"] * self.sizes["gy"]
        if self.kernels:
            away, kept = pack_terms(pieces, rows, self.width, self.sizes)
            self.held.append((away, kept))
            if not later:
                self.send()
            return
        packed = jnp.zeros((devices, rows, self.width), BF16)
        for piece in pieces:
            blocks = [piece[1]]
            if len(piece) == 3:
                grad = weight_grad(*piece[1:]).astype(BF16)
                blocks = jnp.split(grad, max(1, grad.shape[1] // self.width), 1)
            at = piece[0]
            for block in blocks:
                block = block.reshape(devices, -1, block.shape[-1])
                packed = lax.dynamic_update_slice(packed, block, (0, at, 0))
                at += block.shape[1]
        self.terms.append(packed)

    def send(self):
        for away, kept in self.held:
            self.terms.append((kept, exchange(away, self.core[0])))
        self.held = []

    def hold(self):
        self.held = [(passed(away), kept) for away, kept in self.held]

    def advance(self):
        sends = None
        if self.terms and self.kernels:
            sends = self.first_split()
        elif self.terms:
            packed = jnp.concatenate(self.terms, 1)
            self.parts = [(packed.reshape((2,) * len(self.bits) + packed.shape[1:]), self.bits)]
            self.plan = [[which] for which in self.core] + self.plan
        elif self.plan and self.kernels:
            sends = self.next_sends()
        elif self.kernels:
            self.parts = [(added(*self.flying[0][:2]), [])]
        else:
            self.parts = [
                ((kept.astype(F32) + got.astype(F32)).astype(BF16 if self.plan else F32), bits)
                for kept, got, bits in self.flying
            ]
        self.terms, self.flying = [], []
        if sends is None and self.plan:
            sends = self.halves()
        for away, kept, axis, bit, left in sends or []:
            self.flying.append((kept, exchange(away, (axis, bit)), left))

    def first_split(self):
        bits = [one for one in self.bits if one not in self.core]
        out = split_terms(self.terms)
        sends = []
        for part, which in enumerate(self.plan.pop(0)):
            left = [one for one in bits if one != which]
            away, kept = (one.reshape((2,) * len(left) + one.shape[-2:]) for one in out[2 * part : 2 * part + 2])
            sends.append((away, kept) + which + (left,))
        return sends

    def next_sends(self):
        steps = self.plan.pop(0)
        join = len(steps) < len(self.flying)
        return halve_terms(self.flying, steps * 2 if join else steps, join)

    def halves(self):
        step = self.plan.pop(0)
        if len(step) == 2 and len(self.parts) == 1:
            total, bits = self.parts[0]
            self.parts = [(total[..., : self.width // 2], bits), (total[..., self.width // 2 :], bits)]
        if len(step) == 1 and len(self.parts) == 2:
            self.parts = [(jnp.concatenate([self.parts[0][0], self.parts[1][0]], -1), self.parts[0][1])]
        sends = []
        for (total, bits), (axis, bit) in zip(self.parts, step):
            place = bits.index((axis, bit))
            own = (lax.axis_index(axis) >> bit) & 1
            away = lax.dynamic_index_in_dim(total, 1 - own, place, keepdims=False)
            kept = lax.dynamic_index_in_dim(total, own, place, keepdims=False)
            sends.append((away, kept, axis, bit, [one for one in bits if one != (axis, bit)]))
        return sends

    def result(self):
        while self.plan or self.flying:
            self.advance()
        return self.parts[0][0].astype(F32)


def normed_rows(values_in):
    centred = values_in - jnp.mean(values_in, -1, keepdims=True)
    rate = lax.rsqrt(jnp.mean(centred * centred, -1, keepdims=True) + EPSILON)
    return centred * rate, rate


def normed_back(unit, rate, gain, d_out):
    d_unit = d_out * gain
    mean_unit = jnp.mean(d_unit, -1, keepdims=True)
    mean_cross = jnp.mean(d_unit * unit, -1, keepdims=True)
    return rate * (d_unit - mean_unit - unit * mean_cross), jnp.sum(d_out * unit, 0)


GELU_RATE = math.sqrt(2.0 / math.pi)
GELU_CUBE = 0.044715


def gelu(values_in):
    inner = jnp.tanh(GELU_RATE * (values_in + GELU_CUBE * values_in * values_in * values_in))
    return 0.5 * values_in * (1.0 + inner)


def gelu_slope(values_in):
    square = values_in * values_in
    inner = jnp.tanh(GELU_RATE * values_in * (1.0 + GELU_CUBE * square))
    return 0.5 * (1.0 + inner) + 0.5 * values_in * (1.0 - inner * inner) * GELU_RATE * (1.0 + 3.0 * GELU_CUBE * square)


def per_device(sizes, *given):
    (
        text_tokens,
        image_regions,
        caption_lengths,
        region_mask,
        text_cotangent,
        image_cotangent,
        text_query,
        image_key,
        image_value,
        text_merge,
        text_gain_cross,
        image_query,
        text_key,
        text_value,
        image_merge,
        image_gain_cross,
        text_up,
        text_bias,
        text_down,
        text_gain_ffn,
        image_up,
        image_bias,
        image_down,
        image_gain_ffn,
        text_self,
        text_mix,
        text_gain_self,
        image_self,
        image_mix,
        image_gain_self,
    ) = given
    matrices = [array for array in given[6:] if array.ndim == 2]
    sizes = dict(sizes, aligned=all(array.shape[0] % 8 == 0 for array in matrices))
    devices = sizes["gx"] * sizes["gy"]
    pairs, length, text_width = text_tokens.shape
    regions, image_width = image_regions.shape[1:]
    inner = text_query.shape[1]

    vectors = (
        text_gain_cross,
        image_gain_cross,
        text_bias,
        text_gain_ffn,
        image_bias,
        image_gain_ffn,
        text_gain_self,
        image_gain_self,
    )
    text_pieces = jnp.split(text_up, text_up.shape[1] // text_width, 1) + [text_down]
    text_pieces += jnp.split(text_self, 3, 1) + [text_mix, text_merge]
    image_pieces = [image_query, text_key, text_value, image_merge, image_up, image_down]
    image_pieces += jnp.split(image_self, 3, 1) + [image_mix]
    def starts(pieces):
        marks = [0]
        for piece in pieces:
            marks.append(marks[-1] + piece.shape[0])
        return list(zip(marks[:-1], marks[1:]))

    def taken(block, at):
        return whole(block[:, at[0] : at[1]])

    def side_by_side(block, spans):
        return jnp.concatenate([taken(block, at) for at in spans], 1)

    text_at, image_at = starts(text_pieces), starts(image_pieces)
    packed = []

    def pack_image():
        shards = [image_query, text_key, text_value, image_merge, image_up, image_down, image_self, image_mix]
        packed.append(pack_rows(shards, inner))

    Order.last = []
    all_text = gather(copy_rows([text_up, text_down, text_self, text_mix, text_merge], text_width))
    weight_text_query, weight_image_held, all_vectors = gather_weights(
        [[text_query], [image_key, image_value]], vectors, sizes, pack_image
    )
    (packed_image,) = packed

    text_slots, image_slots = round_up(length, 8), round_up(regions, 8)

    def padded(array, slots):
        array = jnp.pad(array, ((0, 0), (0, slots - array.shape[1]), (0, 0)))
        return array.reshape(pairs * slots, array.shape[2])

    def rows_of(array):
        return array.reshape(-1, array.shape[-1])

    def pairs_of(array):
        return array.reshape(pairs, array.shape[0] // pairs, array.shape[1])

    def fill_of(live, count):
        slots = live.shape[1]
        fill = jnp.where(live, 0.0, jnp.where(jnp.arange(slots)[None, :] < count, MASKED, PADDED))
        return jnp.broadcast_to(fill[:, :, None], (pairs, slots, LANES)).astype(F32)

    text_rows, image_rows = padded(text_tokens, text_slots), padded(image_regions, image_slots)
    d_text_out = padded(text_cotangent, text_slots)
    d_image_out = padded(image_cotangent, image_slots)
    text_live = jnp.arange(text_slots)[None, :] < caption_lengths[:, None]
    image_live = jnp.pad(region_mask, ((0, 0), (0, image_slots - regions))) > 0
    text_fill, image_fill = fill_of(text_live, length), fill_of(image_live, regions)
    text_keep = text_live.astype(F32).reshape(-1, 1)
    image_keep = image_live.astype(F32).reshape(-1, 1)

    query_text = pairs_of(project(text_rows, weight_text_query).astype(BF16))
    held_image = pairs_of(project(image_rows, weight_image_held).astype(BF16))
    mixed_cross = attend((query_text, 0), (held_image, 0), (held_image, 1), image_fill, inner, HEADS)
    mixed_cross, packed_image = tie(mixed_cross, packed_image)
    all_image = gather(packed_image)
    cross_text = rows_of(mixed_cross)
    ups = text_up.shape[1] // text_width
    full_text_merge = taken(all_text, text_at[ups + 5])
    unit_text_1, rate_text_1 = normed_rows(text_rows.astype(F32) + project(cross_text, full_text_merge))

    full_text_up = side_by_side(all_text, text_at[:ups])
    full_text_down = taken(all_text, text_at[ups])
    full_text_self = side_by_side(all_text, text_at[ups + 1 : ups + 4])
    full_text_mix = taken(all_text, text_at[ups + 4])
    full = {
        name: all_vectors.reshape(devices, len(vectors), inner)[:, at, : piece.shape[0]].reshape(-1).astype(F32)
        for at, (name, piece) in enumerate(zip(VECTOR_NAMES, vectors))
    }

    def forward(unit_1, gain_1, up, bias, down, gain_2, joint, mix, gain_3, fill, keep, heads):
        width = unit_1.shape[1]
        first = unit_1 * gain_1
        first_low = first.astype(BF16)
        hidden = project(first_low, up) + bias
        active, slope = tie(gelu(hidden).astype(BF16), gelu_slope(hidden).astype(BF16))
        unit_2, rate_2 = normed_rows(first + project(active, down))
        second = unit_2 * gain_2
        second_low = second.astype(BF16)
        triple = pairs_of(project(second_low, joint).astype(BF16))
        mixed = rows_of(attend((triple, 0), (triple, 1), (triple, 2), fill, width, heads))
        unit_3, rate_3 = normed_rows(second + project(mixed, mix))
        out = (unit_3 * gain_3 * keep).astype(BF16)
        return out, (first_low, active, slope, unit_2, rate_2, second_low, triple, mixed, unit_3, rate_3)

    def self_backward(saved, gain_2, joint, mix, gain_3, fill, keep, d_out, heads):
        _, _, _, unit_2, rate_2, second_low, triple, mixed, unit_3, rate_3 = saved
        width = unit_2.shape[1]
        d_third, g_gain_3 = normed_back(unit_3, rate_3, gain_3, d_out.astype(F32) * keep)
        d_branch = d_third.astype(BF16)
        d_mixed = pairs_of(project_back(d_branch, mix).astype(BF16))
        d_triple = attend_back((triple, 0), (triple, 1), (triple, 2), fill, d_mixed, width, heads)
        d_triple = rows_of(jnp.concatenate(d_triple, -1))
        d_second = d_third + project_back(d_triple, joint)
        d_sum, g_gain_2 = normed_back(unit_2, rate_2, gain_2, d_second)
        return d_sum, (mixed, d_branch), (second_low, d_triple), g_gain_2, g_gain_3

    def feed_backward(saved, d_sum, unit_1, rate_1, gain_1, up, down):
        first_low, active, slope = saved[:3]
        d_sum_low = d_sum.astype(BF16)
        d_hidden = (slope.astype(F32) * project_back(d_sum_low, down)).astype(BF16)
        g_bias = jnp.sum(d_hidden.astype(F32), 0)
        d_first = d_sum + project_back(d_hidden, up)
        d_resid, g_gain_1 = normed_back(unit_1, rate_1, gain_1, d_first)
        return d_resid, (first_low, d_hidden), (active, d_sum_low), g_bias, g_gain_1

    out_text, saved_text = forward(
        unit_text_1,
        full["text_gain_cross"],
        full_text_up,
        full["text_bias"],
        full_text_down,
        full["text_gain_ffn"],
        full_text_self,
        full_text_mix,
        full["text_gain_self"],
        text_fill,
        text_keep,
        TEXT_HEADS,
    )
    d_sum_text, g_text_mix, g_text_self, g_text_gain_ffn, g_text_gain_self = self_backward(
        saved_text,
        full["text_gain_ffn"],
        full_text_self,
        full_text_mix,
        full["text_gain_self"],
        text_fill,
        text_keep,
        d_text_out,
        TEXT_HEADS,
    )
    row_text, row_image, row_down = text_query.shape[0], image_key.shape[0], text_down.shape[0]
    sum_a, sum_b = OwnerSum(text_width, sizes), OwnerSum(text_width, sizes)
    sum_c, sum_d, sum_e = OwnerSum(inner, sizes), OwnerSum(inner, sizes), OwnerSum(inner, sizes)
    sum_a.add(4 * row_text, (0, *g_text_self), (3 * row_text, *g_text_mix))
    d_resid_text, g_text_up, g_text_down, g_text_bias, g_text_gain_cross = feed_backward(
        saved_text, d_sum_text, unit_text_1, rate_text_1, full["text_gain_cross"], full_text_up, full_text_down
    )
    row_down, row_self = text_at[ups][0], text_at[ups + 1][0]
    sum_a.advance()
    sum_b.add(ups * row_text, (0, *g_text_up))
    sum_a.advance()
    sum_b.add(row_down, (0, *g_text_down))
    d_merge_text = d_resid_text.astype(BF16)
    sum_b.add(text_merge.shape[0], (0, cross_text, d_merge_text))
    d_heads_text = pairs_of(project_back(d_merge_text, full_text_merge).astype(BF16))
    d_query_text, d_key_image, d_value_image = map(
        rows_of,
        attend_back((query_text, 0), (held_image, 0), (held_image, 1), image_fill, d_heads_text, inner, HEADS),
    )
    sum_b.advance()
    sum_a.advance()
    row_first = round_up(2 * row_image, row_text)
    sums_first = scattered(
        [(0, image_rows, d_key_image), (row_image, image_rows, d_value_image), (row_first, text_rows, d_query_text)],
        row_first + row_text,
        inner,
        sizes,
    )
    weight_image_query = taken(all_image, image_at[0])
    weight_text_held = side_by_side(all_image, image_at[1:3])
    full_image_merge = taken(all_image, image_at[3])
    full_image_up = taken(all_image, image_at[4])
    full_image_down = taken(all_image, image_at[5])
    full_image_self = side_by_side(all_image, image_at[6:9])
    full_image_mix = taken(all_image, image_at[9])

    query_image = pairs_of(project(image_rows, weight_image_query).astype(BF16))
    held_text = pairs_of(project(text_rows, weight_text_held).astype(BF16))
    cross_image = rows_of(attend((query_image, 0), (held_text, 0), (held_text, 1), text_fill, inner, HEADS))
    sum_a.advance()
    unit_image_1, rate_image_1 = normed_rows(image_rows.astype(F32) + project(cross_image, full_image_merge))

    out_image, saved_image = forward(
        unit_image_1,
        full["image_gain_cross"],
        full_image_up,
        full["image_bias"],
        full_image_down,
        full["image_gain_ffn"],
        full_image_self,
        full_image_mix,
        full["image_gain_self"],
        image_fill,
        image_keep,
        IMAGE_HEADS,
    )
    sum_b.advance()
    sum_a.advance()
    d_sum_image, g_image_mix, g_image_self, g_image_gain_ffn, g_image_gain_self = self_backward(
        saved_image,
        full["image_gain_ffn"],
        full_image_self,
        full_image_mix,
        full["image_gain_self"],
        image_fill,
        image_keep,
        d_image_out,
        IMAGE_HEADS,
    )
    sum_c.add(4 * row_image, (0, *g_image_self), (3 * row_image, *g_image_mix))
    sum_b.advance()
    d_resid_image, g_image_up, g_image_down, g_image_bias, g_image_gain_cross = feed_backward(
        saved_image,
        d_sum_image,
        unit_image_1,
        rate_image_1,
        full["image_gain_cross"],
        full_image_up,
        full_image_down,
    )

    sum_c.advance()
    sum_b.advance()
    d_merge_image = d_resid_image.astype(BF16)
    sum_e.add(
        3 * row_image,
        (0, cross_image, d_merge_image),
        (row_image, *g_image_up),
        (2 * row_image, *g_image_down),
    )
    d_heads_image = pairs_of(project_back(d_merge_image, full_image_merge).astype(BF16))
    d_query_image, d_key_text, d_value_text = map(
        rows_of,
        attend_back((query_image, 0), (held_text, 0), (held_text, 1), text_fill, d_heads_image, inner, HEADS),
    )
    g_vectors = (
        g_text_gain_cross,
        g_image_gain_cross,
        g_text_bias,
        g_text_gain_ffn,
        g_image_bias,
        g_image_gain_ffn,
        g_text_gain_self,
        g_image_gain_self,
    )
    row_vector = 2 * row_text
    vector_rows = max(len(vectors), round_up(row_vector + len(vectors), row_image) - row_vector)
    row_query = row_vector + vector_rows
    g_vector = jnp.stack(
        [
            jnp.pad(owned, ((0, 0), (0, inner - owned.shape[1])))
            for owned in (piece.astype(BF16).reshape(devices, -1) for piece in g_vectors)
        ],
        1,
    )
    g_vector = jnp.pad(g_vector, ((0, 0), (0, vector_rows - len(vectors)), (0, 0)))
    sum_d.add(
        row_query + row_image,
        (0, text_rows, d_key_text),
        (row_text, text_rows, d_value_text),
        (row_query, image_rows, d_query_image),
        (row_vector, g_vector),
        later=True,
    )
    sum_c.advance()
    sum_d.hold()
    sum_d.send()
    sum_e.advance()
    sum_d.advance()
    sum_c.advance()
    sum_b.advance()
    grad_text = (
        d_resid_text
        + project_back(d_query_text, weight_text_query)
        + project_back(jnp.concatenate([d_key_text, d_value_text], 1), weight_text_held)
    )
    grad_image = (
        d_resid_image
        + project_back(d_query_image, weight_image_query)
        + project_back(jnp.concatenate([d_key_image, d_value_image], 1), weight_image_held)
    )
    sum_e.advance()
    sums_first = widened(sums_first)
    sum_c.advance()
    sum_d.advance()
    sum_e.advance()
    sum_c.advance()
    sum_d.advance()
    sum_e.advance()
    sum_d.advance()

    def owned(total, pieces):
        return [total[start:end] for start, end in starts(pieces)]

    sums_a, sums_b, sums_c, sums_e, sums_d = [one.result() for one in (sum_a, sum_b, sum_c, sum_e, sum_d)]
    text_selfs = owned(sums_a, text_pieces[ups + 1 : ups + 5])
    text_sums = owned(sums_b, text_pieces[: ups + 1] + [text_merge])
    image_firsts = owned(sums_first, [image_key, image_value]) + [sums_first[row_first : row_first + row_text]]
    image_selfs = owned(sums_c, image_pieces[6:10])
    image_sums = owned(sums_e, image_pieces[3:6]) + owned(sums_d, [text_key, text_value])
    sum_vector = sums_d[row_vector:row_query]
    owned_vector = {
        name: sum_vector[at, : piece.shape[0]] for at, (name, piece) in enumerate(zip(VECTOR_NAMES, vectors))
    }
    return (
        pairs_of(out_text)[:, :length],
        pairs_of(out_image)[:, :regions],
        pairs_of(grad_text)[:, :length],
        pairs_of(grad_image)[:, :regions],
        image_firsts[2],
        image_firsts[0],
        image_firsts[1],
        text_sums[ups + 1],
        owned_vector["text_gain_cross"],
        sums_d[row_query:],
        image_sums[3],
        image_sums[4],
        image_sums[0],
        owned_vector["image_gain_cross"],
        jnp.concatenate(text_sums[:ups], 1),
        owned_vector["text_bias"],
        text_sums[ups],
        owned_vector["text_gain_ffn"],
        image_sums[1],
        owned_vector["image_bias"],
        image_sums[2],
        owned_vector["image_gain_ffn"],
        jnp.concatenate(text_selfs[:3], 1),
        text_selfs[3],
        owned_vector["text_gain_self"],
        jnp.concatenate(image_selfs[:3], 1),
        image_selfs[3],
        owned_vector["image_gain_self"],
    )


def solution(mesh):
    split = {1: P(AXES), 2: P(AXES, None), 3: P(AXES, None, None)}
    in_ranks = (3, 3, 1, 2, 3, 3) + tuple(
        1 if at in (4, 9, 11, 13, 15, 17, 20, 23) else 2 for at in range(24)
    )
    out_ranks = (3, 3, 3, 3) + in_ranks[6:]
    return jax.shard_map(
        functools.partial(per_device, dict(mesh.shape)),
        mesh=mesh,
        in_specs=tuple(split[rank] for rank in in_ranks),
        out_specs=tuple(split[rank] for rank in out_ranks),
        check_vma=False,
    )
```

```python
import functools
import math

import jax
import jax.numpy as jnp
from jax import lax
from jax.experimental import pallas as pl
from jax.experimental.pallas import tpu as pltpu
from jax.sharding import PartitionSpec as P

HEADS = 8
TEXT_HEADS = 12
IMAGE_HEADS = 8
EPSILON = 1e-05
MASKED = -1000000000.0
PADDED = -2000000000.0
LANES = 128
AXES = ("gx", "gy")
F32 = jnp.float32
BF16 = jnp.bfloat16
VMEM_BYTES = 48 * 1024 * 1024
VECTOR_NAMES = (
    "text_gain_cross",
    "image_gain_cross",
    "text_bias",
    "text_gain_ffn",
    "image_bias",
    "image_gain_ffn",
    "text_gain_self",
    "image_gain_self",
)


def project(left, right):
    return jnp.dot(left, right, preferred_element_type=F32)


def project_back(left, right):
    return lax.dot_general(left, right, (((1,), (1,)), ((), ())), preferred_element_type=F32)


def weight_grad(left, right):
    return lax.dot_general(left, right, (((0,), (0,)), ((), ())), preferred_element_type=F32)


def round_up(size, step):
    return -(-size // step) * step


def takes(microseconds):
    return pl.CostEstimate(flops=0, bytes_accessed=int(3.2e6 * microseconds), transcendentals=0)


class Order:
    last = []


def ordered_call(kernel, arrays, in_specs, **rest):
    after = [one for one in Order.last if all(one is not array for array in arrays)]
    given = len(arrays)

    def body(*refs):
        kernel(*refs[:given], *refs[given + len(after) :])

    out = pl.pallas_call(
        body,
        in_specs=list(in_specs) + [pl.BlockSpec(memory_space=pl.ANY)] * len(after),
        compiler_params=pltpu.CompilerParams(vmem_limit_bytes=VMEM_BYTES),
        **rest,
    )(*arrays, *after)
    Order.last = [out[0] if isinstance(out, (list, tuple)) else out]
    return out


def stack_halves(rows):
    wide = rows.astype(F32)
    first = lax.broadcasted_iota(jnp.int32, wide.shape, 1) < LANES // 2
    zero = jnp.zeros_like(wide)
    return jnp.concatenate([jnp.where(first, wide, zero), jnp.where(first, zero, wide)], 0).astype(BF16)


def join_halves(rows):
    count = rows.shape[0] // 2
    first = lax.broadcasted_iota(jnp.int32, (count, LANES), 1) < LANES // 2
    return jnp.where(first, rows[:count], rows[count:])


def probabilities(keys, queries, fill, scale):
    scores = project_back(keys, queries) * scale
    scores = jnp.where(fill < 0.0, fill, scores)
    powers = jnp.exp(scores - jnp.max(scores, 0, keepdims=True))
    return powers * (1.0 / jnp.sum(powers, 0, keepdims=True))


def head_blocks(queries_ref, size):
    count, _, width = queries_ref.shape
    return [(pair, slice(at, at + LANES)) for pair in range(count) for at in range(0, width, LANES)], size < LANES


def attend_kernel(size, queries_ref, keys_ref, values_ref, fill_ref, mixed_ref):
    scale = 1.0 / math.sqrt(size)
    blocks, split = head_blocks(queries_ref, size)
    queries = [stack_halves(queries_ref[p, :, b]) if split else queries_ref[p, :, b] for p, b in blocks]
    probs = [
        probabilities(keys_ref[p, :, b], query, fill_ref[p][:, :1], scale).astype(BF16)
        for (p, b), query in zip(blocks, queries)
    ]
    mixed = [weight_grad(prob, values_ref[p, :, b]) for (p, b), prob in zip(blocks, probs)]
    for (p, b), rows in zip(blocks, mixed):
        mixed_ref[p, :, b] = (join_halves(rows) if split else rows).astype(BF16)


def attend_back_kernel(
    size, queries_ref, keys_ref, values_ref, fill_ref, d_mixed_ref, d_queries_ref, d_keys_ref, d_values_ref
):
    scale = 1.0 / math.sqrt(size)
    blocks, split = head_blocks(queries_ref, size)
    fills = [fill_ref[p][:, :1] for p, _ in blocks]
    queries = [stack_halves(queries_ref[p, :, b]) if split else queries_ref[p, :, b] for p, b in blocks]
    grads = [stack_halves(d_mixed_ref[p, :, b]) if split else d_mixed_ref[p, :, b] for p, b in blocks]
    probs = [
        probabilities(keys_ref[p, :, b], query, fill, scale) for (p, b), query, fill in zip(blocks, queries, fills)
    ]
    d_probs = [project_back(values_ref[p, :, b], grad) for (p, b), grad in zip(blocks, grads)]
    for (p, b), prob, grad in zip(blocks, probs, grads):
        d_values_ref[p, :, b] = project(prob.astype(BF16), grad).astype(BF16)
    d_scores = [
        prob * (d_prob - jnp.sum(prob * d_prob, 0, keepdims=True)) for prob, d_prob in zip(probs, d_probs)
    ]
    d_scores = [jnp.where(fill < 0.0, 0.0, one).astype(BF16) for fill, one in zip(fills, d_scores)]
    for (p, b), one, query in zip(blocks, d_scores, queries):
        d_keys_ref[p, :, b] = (project(one, query) * scale).astype(BF16)
    for (p, b), one in zip(blocks, d_scores):
        rows = weight_grad(one, keys_ref[p, :, b]) * scale
        d_queries_ref[p, :, b] = (join_halves(rows) if split else rows).astype(BF16)


def attention_call(kernel, together, inputs, outputs, microseconds):
    pairs = inputs[0][0].shape[0]
    together = math.gcd(pairs, together)

    def spec(rows, width, column):
        return pl.BlockSpec((together, rows, width), lambda step: (step, 0, column))

    return ordered_call(
        kernel,
        [array for array, _, _ in inputs],
        [spec(array.shape[1], width, column) for array, width, column in inputs],
        grid=(pairs // together,),
        out_specs=[spec(rows, width, 0) for rows, width in outputs],
        out_shape=[jax.ShapeDtypeStruct((pairs, rows, width), BF16) for rows, width in outputs],
        cost_estimate=takes(microseconds),
    )


def attend(queries, keys, values, fill, width, heads):
    pairs, count = queries[0].shape[:2]
    inputs = [(array, width, column) for array, column in (queries, keys, values)] + [(fill, LANES, 0)]
    kernel = functools.partial(attend_kernel, width // heads)
    return attention_call(kernel, 4, inputs, [(count, width)], 4)[0]


def attend_back(queries, keys, values, fill, d_mixed, width, heads):
    pairs, count = queries[0].shape[:2]
    inputs = [(array, width, column) for array, column in (queries, keys, values)]
    inputs += [(fill, LANES, 0), (d_mixed, width, 0)]
    keyed = keys[0].shape[1]
    kernel = functools.partial(attend_back_kernel, width // heads)
    return attention_call(kernel, 2, inputs, [(count, width), (keyed, width), (keyed, width)], 7)


def tie(*values):
    return lax.optimization_barrier(values)


def gather(packed):
    return lax.all_gather(packed, AXES, axis=0, tiled=False)


def in_vmem(kernel, arrays, shapes, where):
    vmem, scalar = pl.BlockSpec(memory_space=pltpu.VMEM), pl.BlockSpec(memory_space=pltpu.SMEM)
    return ordered_call(
        kernel,
        [jnp.stack(where).astype(jnp.int32), *arrays],
        [scalar] + [vmem] * len(arrays),
        out_specs=[vmem] * len(shapes),
        out_shape=[jax.ShapeDtypeStruct(shape, BF16) for shape in shapes],
        cost_estimate=takes(3),
    )


def bit_of(which):
    return (lax.axis_index(which[0]) >> which[1]) & 1


def exchange(block, which):
    axis, bit = which
    return lax.ppermute(block, axis, [(at, at ^ (1 << bit)) for at in range(lax.axis_size(axis))])


def pack_kernel(pieces, *refs):
    out_ref = refs[-1]
    width = out_ref.shape[1]
    for source, column, row in pieces:
        wide = min(width, refs[source].shape[1] - column)
        out_ref[row : row + refs[source].shape[0], :wide] = refs[source][:, column : column + wide]


def pack_rows(arrays, width):
    arrays = [array[None, :] if array.ndim == 1 else array for array in arrays]
    pieces, row = [], 0
    for source, array in enumerate(arrays):
        for column in range(0, array.shape[1], width):
            pieces.append((source, column, row))
            row += array.shape[0]
    if any(array.shape[0] % 8 and array.shape[0] > 1 for array in arrays):
        blocks = [arrays[source][:, column : column + width] for source, column, _ in pieces]
        return jnp.concatenate([jnp.pad(one, ((0, 0), (0, width - one.shape[1]))) for one in blocks], 0)
    return ordered_call(
        functools.partial(pack_kernel, pieces),
        arrays,
        [pl.BlockSpec(array.shape, lambda step: (0, 0)) for array in arrays],
        grid=(1,),
        out_specs=pl.BlockSpec((row, width), lambda step: (0, 0)),
        out_shape=jax.ShapeDtypeStruct((row, width), BF16),
        cost_estimate=takes(1),
    )


def copy_kernel(pieces, *refs):
    out_ref, done = refs[-2:]
    width = out_ref.shape[1]
    copies = []
    for at, (source, column, row) in enumerate(pieces):
        rows = refs[source].shape[0]
        copies.append(
            pltpu.make_async_copy(
                refs[source].at[:, column : column + width], out_ref.at[row : row + rows, :], done.at[at]
            )
        )
    for one in copies:
        one.start()
    for one in copies:
        one.wait()


def copy_rows(arrays, width):
    pieces, row = [], 0
    for source, array in enumerate(arrays):
        for column in range(0, array.shape[1], width):
            pieces.append((source, column, row))
            row += array.shape[0]
    if any(array.shape[0] % 8 for array in arrays):
        return jnp.concatenate([arrays[source][:, column : column + width] for source, column, _ in pieces], 0)
    anywhere = pl.BlockSpec(memory_space=pl.ANY)
    return ordered_call(
        functools.partial(copy_kernel, pieces),
        arrays,
        [anywhere] * len(arrays),
        out_specs=anywhere,
        out_shape=jax.ShapeDtypeStruct((row, width), BF16),
        scratch_shapes=[pltpu.SemaphoreType.DMA((len(pieces),))],
        cost_estimate=takes(2),
    )


def join_kernel(count, where_ref, *refs):
    outs = refs[2 * count :]
    shares = len(outs) // count
    for part in range(count):
        own, (block_ref, got_ref) = where_ref[part], refs[2 * part : 2 * part + 2]
        for share in range(shares):
            out_ref = outs[part * shares + share]
            width = out_ref.shape[-1]
            columns = slice(share * width, (share + 1) * width)
            for before in range(block_ref.shape[0]):
                out_ref[before, own] = block_ref[before, :, :, columns]
                out_ref[before, 1 - own] = got_ref[before, :, :, columns]


def joined(pairs, shares=1):
    arrays, shapes, where, news = [], [], [], []
    for block, got, have, which in pairs:
        new = [one for one in which[1] if one in have or one == which[0]]
        place = new.index(which[0])
        before, behind = 1 << place, 1 << (len(have) - place)
        rows, width = block.shape[-2:]
        arrays += [one.reshape(before, behind, rows, width) for one in (block, got)]
        shapes += [(before, 2, behind, rows, width // shares)] * shares
        where.append(bit_of(which[0]))
        news.append(new)
    outs = in_vmem(functools.partial(join_kernel, len(pairs)), arrays, shapes, where)
    return [
        (out.reshape((2,) * len(news[at // shares]) + out.shape[-2:]), news[at // shares])
        for at, out in enumerate(outs)
    ]


def unpack_kernel(pieces, own_ref, *refs):
    parts, outs = refs[: len(refs) - len(pieces)], refs[len(refs) - len(pieces) :]
    shares = len(parts) // 2
    for out_ref, firsts in zip(outs, pieces):
        rows = out_ref.shape[3]
        for source in range(2):
            core = own_ref[0] if source == 0 else 1 - own_ref[0]
            at = 0
            for first in firsts:
                for part_ref in parts[source * shares : (source + 1) * shares]:
                    width = part_ref.shape[-1]
                    out_ref[0, core, :, :, at : at + width] = part_ref[0, :, first : first + rows, :]
                    at += width


def gather_weights(pieces, vectors, sizes, meanwhile):
    core, y_bits, x_bits, z_bits = mesh_axes_bits(sizes)
    order = mesh_bits(sizes)
    shards = [shard for group in pieces for shard in group]
    width = shards[0].shape[1]
    packed = pack_rows(shards + list(vectors), width)
    if not sizes["aligned"] or len(core) != 1 or len(x_bits) != len(y_bits) or not z_bits:
        meanwhile()
        gathered, at, out = gather(packed), 0, []
        for group in pieces:
            blocks = []
            for shard in group:
                blocks.append(whole(gathered[:, at : at + shard.shape[0]]))
                at += shard.shape[0]
            out.append(jnp.concatenate(blocks, 1))
        return out + [whole(gathered[:, at:])]
    meanwhile()
    parts = [(packed, [])]
    for step, which in enumerate(reversed(z_bits)):
        block, have = parts[0]
        parts = joined([(block, exchange(block, which), have, (which, order))], 2 if step == len(z_bits) - 1 else 1)
    for steps in zip(y_bits + x_bits, x_bits + y_bits):
        flying = [(block, exchange(block, which), have, (which, order)) for (block, have), which in zip(parts, steps)]
        parts = joined(flying)
    groups, others, rows = sizes["gx"] // 2, sizes["gy"], packed.shape[0]
    halves = [block.reshape(groups, others, rows, width // 2) for block, _ in parts]
    halves += [exchange(block, core[0]) for block in halves]
    firsts, shapes, at = [], [], 0
    for group in pieces:
        firsts.append([])
        for shard in group:
            firsts[-1].append(at)
            at += shard.shape[0]
        shapes.append((groups, 2, others, group[0].shape[0], width * len(group)))
    firsts.append([at])
    shapes.append((groups, 2, others, len(vectors), width))
    out = ordered_call(
        functools.partial(unpack_kernel, firsts),
        [bit_of(core[0]).astype(jnp.int32).reshape(1), *halves],
        [pl.BlockSpec(memory_space=pltpu.SMEM)]
        + [pl.BlockSpec((1, others, rows, width // 2), lambda step: (step, 0, 0, 0))] * 4,
        grid=(groups,),
        out_specs=[pl.BlockSpec((1,) + shape[1:], lambda step: (step, 0, 0, 0, 0)) for shape in shapes],
        out_shape=[jax.ShapeDtypeStruct(shape, BF16) for shape in shapes],
        cost_estimate=takes(6),
    )
    return [whole(block) for block in out]


def whole(block):
    return block.reshape(-1, block.shape[-1])


def owned_rows(matrix, devices):
    return matrix.reshape(devices, matrix.shape[0] // devices, matrix.shape[1])


def mesh_bits(sizes):
    bits = []
    for axis in AXES:
        bits += [(axis, bit) for bit in reversed(range(sizes[axis].bit_length() - 1))]
    return bits


def mesh_axes_bits(sizes):
    low = (sizes["gy"].bit_length() - 1) // 2
    bits = mesh_bits(sizes)[::-1]
    core = [one for one in bits if one == ("gx", 0)]
    rows = [one for one in bits if one[0] == "gx" and one[1] > 0]
    columns = [one for one in bits if one[0] == "gy" and one[1] < low]
    rest = [one for one in bits if one[0] == "gy" and one[1] >= low]
    return core, rows, columns, rest


def grad_kernel(per_core, left_ref, right_ref, core_ref, *refs):
    away_ref, kept_ref, whole_ref = refs[-3:]
    own = core_ref[0]
    grad = weight_grad(left_ref[...], right_ref[...])
    groups, _, width = whole_ref.shape
    if grad.shape[1] < width:
        grad = jnp.pad(grad, ((0, 0), (0, width - grad.shape[1])))
    whole_ref[...] = grad.reshape(whole_ref.shape)
    for group in range(groups // 2):
        shape = kept_ref.shape[1:]
        kept_ref[group] = whole_ref[2 * group + own].reshape(shape).astype(BF16)
        away_ref[group] = whole_ref[2 * group + 1 - own].reshape(shape).astype(BF16)


def grad_rows_kernel(left_ref, right_ref, core_ref, *refs):
    away_ref, kept_ref = refs[-2:]
    stays = pl.program_id(0) % 2 == core_ref[0]
    shape = kept_ref.shape[1:]
    grad = weight_grad(left_ref[...], right_ref[...]).astype(BF16).reshape(shape)

    @pl.when(stays)
    def _():
        kept_ref[0] = grad

    @pl.when(jnp.logical_not(stays))
    def _():
        away_ref[0] = grad


def place_kernel(terms_ref, core_ref, *refs):
    away_ref, kept_ref = refs[-2:]
    own = core_ref[0]
    for group in range(kept_ref.shape[0]):
        kept_ref[group] = terms_ref[group, own]
        away_ref[group] = terms_ref[group, 1 - own]


def pack_terms(pieces, rows, width, sizes):
    groups, others = sizes["gx"] // 2, sizes["gy"]
    core = (lax.axis_index("gx") & 1).astype(jnp.int32).reshape(1)
    shape = jax.ShapeDtypeStruct((groups, others, rows, width), BF16)
    buffers = []
    for piece in pieces:
        first, scratch = piece[0], []
        scalar = pl.BlockSpec(memory_space=pltpu.SMEM)
        if len(piece) == 2:
            terms = piece[1].reshape((groups, 2, others) + piece[1].shape[1:])
            count = terms.shape[3]
            kernel, arrays, grid, flops = place_kernel, [terms], (1,), 0
            in_specs = [pl.BlockSpec(terms.shape, lambda step: (0,) * 5)]
            place = pl.BlockSpec((groups, others, count, width), lambda step, at=first // count: (0, 0, at, 0))
        else:
            left, right = piece[1:]
            height, tall = left.shape
            count = tall // (2 * groups * others)
            arrays, flops = [left, right], 2 * height * tall * right.shape[1]
            if right.shape[1] <= width and tall >= 2048:
                kernel, grid = grad_rows_kernel, (2 * groups,)
                in_specs = [
                    pl.BlockSpec((height, tall // (2 * groups)), lambda step: (0, step)),
                    pl.BlockSpec(right.shape, lambda step: (0, 0)),
                ]
                place = pl.BlockSpec((1, others, count, width), lambda step, at=first // count: (step // 2, 0, at, 0))
            else:
                each = min(width, right.shape[1])
                kernel, grid = functools.partial(grad_kernel, groups), (right.shape[1] // each,)
                in_specs = [
                    pl.BlockSpec(left.shape, lambda step: (0, 0)),
                    pl.BlockSpec((height, each), lambda step: (0, step)),
                ]
                place = pl.BlockSpec(
                    (groups, others, count, width), lambda step, at=first // count: (0, 0, at + step, 0)
                )
                scratch = [pltpu.VMEM((2 * groups, tall // (2 * groups), width), F32)]
        assert first % count == 0
        arrays = arrays + [core] + buffers
        in_specs = in_specs + [scalar] + [pl.BlockSpec(memory_space=pl.ANY)] * len(buffers)
        buffers = list(
            ordered_call(
                kernel,
                arrays,
                in_specs,
                grid=grid,
                out_specs=[place, place],
                out_shape=[shape, shape],
                scratch_shapes=scratch,
                input_output_aliases={len(arrays) - 2: 0, len(arrays) - 1: 1} if buffers else {},
                cost_estimate=takes(1 + flops / 4.5e8),
            )
        )
    return buffers


def whole_kernel(left_ref, right_ref, *refs):
    refs[-1][...] = weight_grad(left_ref[...], right_ref[...]).reshape(refs[-1].shape).astype(BF16)


def scattered(pieces, rows, width, sizes):
    devices = sizes["gx"] * sizes["gy"]
    if not sizes["aligned"]:
        packed = jnp.zeros((devices, rows, width), BF16)
        for first, left, right in pieces:
            grad = weight_grad(left, right).astype(BF16)
            packed = lax.dynamic_update_slice(packed, grad.reshape(devices, -1, width), (0, first, 0))
    else:
        buffers = []
        for first, left, right in pieces:
            count = left.shape[1] // devices
            block = pl.BlockSpec((devices, count, width), lambda step, at=first // count: (0, at, 0))
            buffers = [
                ordered_call(
                    whole_kernel,
                    [left, right] + buffers,
                    [pl.BlockSpec(one.shape, lambda step: (0, 0)) for one in (left, right)]
                    + [pl.BlockSpec(memory_space=pl.ANY)] * len(buffers),
                    grid=(1,),
                    out_specs=block,
                    out_shape=jax.ShapeDtypeStruct((devices, rows, width), BF16),
                    input_output_aliases={2: 0} if buffers else {},
                    cost_estimate=takes(3),
                )
            ]
        (packed,) = buffers
    return lax.psum_scatter(packed.reshape(devices * rows, width), AXES, scatter_dimension=0, tiled=True)


def widen_kernel(low_ref, high_ref):
    high_ref[...] = low_ref[...].astype(F32)


def widened(low):
    whole_block = pl.BlockSpec(low.shape, lambda step: (0, 0))
    return ordered_call(
        widen_kernel,
        [low],
        [whole_block],
        grid=(1,),
        out_specs=whole_block,
        out_shape=jax.ShapeDtypeStruct(low.shape, F32),
        cost_estimate=takes(1),
    )


def split_kernel(where_ref, *refs):
    away_x_ref, kept_x_ref, away_y_ref, kept_y_ref = refs[-4:]
    x, y = where_ref[0], where_ref[1]
    half = kept_x_ref.shape[-1]
    left, right = slice(0, half), slice(half, 2 * half)
    stays = pl.program_id(2) == y
    row = 0
    for kept_ref, got_ref in zip(refs[:-4:2], refs[1:-4:2]):
        rows = slice(row, row + kept_ref.shape[-2])
        row += kept_ref.shape[-2]

        def added(at, columns, kept_ref=kept_ref, got_ref=got_ref):
            total = kept_ref[0, 0, 0, at, :, columns].astype(F32) + got_ref[0, 0, 0, at, :, columns].astype(F32)
            return total.astype(BF16)

        kept_x_ref[0, 0, 0, rows, :] = added(x, left)
        away_x_ref[0, 0, 0, rows, :] = added(1 - x, left)

        @pl.when(stays)
        def _(added=added, rows=rows):
            for at in range(2):
                kept_y_ref[0, 0, at, rows, :] = added(at, right)

        @pl.when(jnp.logical_not(stays))
        def _(added=added, rows=rows):
            for at in range(2):
                away_y_ref[0, 0, at, rows, :] = added(at, right)


def split_terms(pairs):
    groups, others, _, width = pairs[0][0].shape
    rows = sum(kept.shape[2] for kept, _ in pairs)
    where = jnp.stack([lax.axis_index("gy") & 1, (lax.axis_index("gx") >> 1) & 1]).astype(jnp.int32)
    high, z, half = groups // 2, others // 2, width // 2
    arrays = [one.reshape((high, 2, z, 2) + one.shape[2:]) for pair in pairs for one in pair]
    along_x = pl.BlockSpec((1, 1, 1, rows, half), lambda high, z, y: (high, y, z, 0, 0))
    along_y = pl.BlockSpec((1, 1, 2, rows, half), lambda high, z, y: (high, z, 0, 0, 0))
    shape_x = jax.ShapeDtypeStruct((high, 2, z, rows, half), BF16)
    shape_y = jax.ShapeDtypeStruct((high, z, 2, rows, half), BF16)
    size = groups * others * rows * width
    return ordered_call(
        split_kernel,
        [where] + arrays,
        [pl.BlockSpec(memory_space=pltpu.SMEM)]
        + [pl.BlockSpec((1, 1, 1) + array.shape[3:], lambda high, z, y: (high, y, z, 0, 0, 0)) for array in arrays],
        grid=(high, z, 2),
        out_specs=[along_x, along_x, along_y, along_y],
        out_shape=[shape_x, shape_x, shape_y, shape_y],
        cost_estimate=takes(2.8e-6 * size),
    )


def halve_kernel(count, where_ref, *refs):
    outs = refs[2 * count :]
    side = 0
    for part in range(count):
        own, (kept_ref, got_ref) = where_ref[part], refs[2 * part : 2 * part + 2]
        width = kept_ref.shape[-1]
        away_ref, stay_ref = (refs[-2], refs[-1]) if refs[-1].shape[-1] > width else refs[-2 * (count - part) :][:2]
        columns = slice(side, side + width) if refs[-1].shape[-1] > width else slice(0, width)
        side += width
        for before in range(kept_ref.shape[0]):
            for behind in range(kept_ref.shape[2]):
                for out_ref, at in ((away_ref, 1 - own), (stay_ref, own)):
                    total = kept_ref[before, at, behind].astype(F32) + got_ref[before, at, behind].astype(F32)
                    out_ref[before, behind, :, columns] = total.astype(BF16)


def halve_terms(parts, steps, join):
    arrays, where, shapes, lefts = [], [], [], []
    for (kept, got, bits), which in zip(parts, steps):
        place = bits.index(which)
        rows, width = kept.shape[-2:]
        before, behind = 1 << place, 1 << (len(bits) - place - 1)
        arrays += [one.reshape(before, 2, behind, rows, width) for one in (kept, got)]
        where.append(bit_of(which))
        lefts.append([one for one in bits if one != which])
        shapes += [(before, behind, rows, width)] * 2
    if join:
        shapes = [shape[:-1] + (2 * shape[-1],) for shape in shapes[:2]]
    outs = in_vmem(functools.partial(halve_kernel, len(parts)), arrays, shapes, where)
    outs = [out.reshape((2,) * len(lefts[0]) + out.shape[-2:]) for out in outs]
    return [
        tuple(outs[2 * at : 2 * at + 2]) + which + (left,)
        for at, (which, left) in enumerate(zip(steps[: len(outs) // 2], lefts))
    ]


def passed_kernel(given_ref, same_ref):
    pass


def passed(array):
    anywhere = pl.BlockSpec(memory_space=pl.ANY)
    return ordered_call(
        passed_kernel,
        [array],
        [anywhere],
        out_specs=anywhere,
        out_shape=jax.ShapeDtypeStruct(array.shape, array.dtype),
        input_output_aliases={0: 0},
        cost_estimate=takes(0),
    )


def added_kernel(kept_ref, got_ref, total_ref):
    total_ref[...] = kept_ref[...].astype(F32) + got_ref[...].astype(F32)


def added(kept, got):
    vmem = pl.BlockSpec(memory_space=pltpu.VMEM)
    return ordered_call(
        added_kernel,
        [kept, got],
        [vmem, vmem],
        out_specs=vmem,
        out_shape=jax.ShapeDtypeStruct(kept.shape, F32),
        cost_estimate=takes(1),
    )


class OwnerSum:
    def __init__(self, width, sizes):
        core, y_bits, x_bits, z_bits = mesh_axes_bits(sizes)
        self.width, self.sizes, self.core, self.bits = width, sizes, core, mesh_bits(sizes)
        self.plan = [list(pair) for pair in zip(x_bits + y_bits, y_bits + x_bits)] + [[which] for which in z_bits]
        self.kernels = sizes["aligned"] and len(core) == 1 and bool(y_bits) and len(x_bits) == len(y_bits)
        self.held, self.terms, self.flying, self.parts = [], [], [], None

    def add(self, rows, *pieces, later=False):
        devices = self.sizes["gx"] * self.sizes["gy"]
        if self.kernels:
            away, kept = pack_terms(pieces, rows, self.width, self.sizes)
            self.held.append((away, kept))
            if not later:
                self.send()
            return
        packed = jnp.zeros((devices, rows, self.width), BF16)
        for piece in pieces:
            blocks = [piece[1]]
            if len(piece) == 3:
                grad = weight_grad(*piece[1:]).astype(BF16)
                blocks = jnp.split(grad, max(1, grad.shape[1] // self.width), 1)
            at = piece[0]
            for block in blocks:
                block = block.reshape(devices, -1, block.shape[-1])
                packed = lax.dynamic_update_slice(packed, block, (0, at, 0))
                at += block.shape[1]
        self.terms.append(packed)

    def send(self):
        for away, kept in self.held:
            self.terms.append((kept, exchange(away, self.core[0])))
        self.held = []

    def hold(self):
        self.held = [(passed(away), kept) for away, kept in self.held]

    def advance(self):
        sends = None
        if self.terms and self.kernels:
            sends = self.first_split()
        elif self.terms:
            packed = jnp.concatenate(self.terms, 1)
            self.parts = [(packed.reshape((2,) * len(self.bits) + packed.shape[1:]), self.bits)]
            self.plan = [[which] for which in self.core] + self.plan
        elif self.plan and self.kernels:
            sends = self.next_sends()
        elif self.kernels:
            self.parts = [(added(*self.flying[0][:2]), [])]
        else:
            self.parts = [
                ((kept.astype(F32) + got.astype(F32)).astype(BF16 if self.plan else F32), bits)
                for kept, got, bits in self.flying
            ]
        self.terms, self.flying = [], []
        if sends is None and self.plan:
            sends = self.halves()
        for away, kept, axis, bit, left in sends or []:
            self.flying.append((kept, exchange(away, (axis, bit)), left))

    def first_split(self):
        bits = [one for one in self.bits if one not in self.core]
        out = split_terms(self.terms)
        sends = []
        for part, which in enumerate(self.plan.pop(0)):
            left = [one for one in bits if one != which]
            away, kept = (one.reshape((2,) * len(left) + one.shape[-2:]) for one in out[2 * part : 2 * part + 2])
            sends.append((away, kept) + which + (left,))
        return sends

    def next_sends(self):
        steps = self.plan.pop(0)
        join = len(steps) < len(self.flying)
        return halve_terms(self.flying, steps * 2 if join else steps, join)

    def halves(self):
        step = self.plan.pop(0)
        if len(step) == 2 and len(self.parts) == 1:
            total, bits = self.parts[0]
            self.parts = [(total[..., : self.width // 2], bits), (total[..., self.width // 2 :], bits)]
        if len(step) == 1 and len(self.parts) == 2:
            self.parts = [(jnp.concatenate([self.parts[0][0], self.parts[1][0]], -1), self.parts[0][1])]
        sends = []
        for (total, bits), (axis, bit) in zip(self.parts, step):
            place = bits.index((axis, bit))
            own = (lax.axis_index(axis) >> bit) & 1
            away = lax.dynamic_index_in_dim(total, 1 - own, place, keepdims=False)
            kept = lax.dynamic_index_in_dim(total, own, place, keepdims=False)
            sends.append((away, kept, axis, bit, [one for one in bits if one != (axis, bit)]))
        return sends

    def result(self):
        while self.plan or self.flying:
            self.advance()
        return self.parts[0][0].astype(F32)


def normed_rows(values_in):
    centred = values_in - jnp.mean(values_in, -1, keepdims=True)
    rate = lax.rsqrt(jnp.mean(centred * centred, -1, keepdims=True) + EPSILON)
    return centred * rate, rate


def normed_back(unit, rate, gain, d_out):
    d_unit = d_out * gain
    mean_unit = jnp.mean(d_unit, -1, keepdims=True)
    mean_cross = jnp.mean(d_unit * unit, -1, keepdims=True)
    return rate * (d_unit - mean_unit - unit * mean_cross), jnp.sum(d_out * unit, 0)


GELU_RATE = math.sqrt(2.0 / math.pi)
GELU_CUBE = 0.044715


def gelu(values_in):
    inner = jnp.tanh(GELU_RATE * (values_in + GELU_CUBE * values_in * values_in * values_in))
    return 0.5 * values_in * (1.0 + inner)


def gelu_slope(values_in):
    square = values_in * values_in
    inner = jnp.tanh(GELU_RATE * values_in * (1.0 + GELU_CUBE * square))
    return 0.5 * (1.0 + inner) + 0.5 * values_in * (1.0 - inner * inner) * GELU_RATE * (1.0 + 3.0 * GELU_CUBE * square)


def per_device(sizes, *given):
    (
        text_tokens,
        image_regions,
        caption_lengths,
        region_mask,
        text_cotangent,
        image_cotangent,
        text_query,
        image_key,
        image_value,
        text_merge,
        text_gain_cross,
        image_query,
        text_key,
        text_value,
        image_merge,
        image_gain_cross,
        text_up,
        text_bias,
        text_down,
        text_gain_ffn,
        image_up,
        image_bias,
        image_down,
        image_gain_ffn,
        text_self,
        text_mix,
        text_gain_self,
        image_self,
        image_mix,
        image_gain_self,
    ) = given
    matrices = [array for array in given[6:] if array.ndim == 2]
    sizes = dict(sizes, aligned=all(array.shape[0] % 8 == 0 for array in matrices))
    devices = sizes["gx"] * sizes["gy"]
    pairs, length, text_width = text_tokens.shape
    regions, image_width = image_regions.shape[1:]
    inner = text_query.shape[1]

    vectors = (
        text_gain_cross,
        image_gain_cross,
        text_bias,
        text_gain_ffn,
        image_bias,
        image_gain_ffn,
        text_gain_self,
        image_gain_self,
    )
    text_pieces = jnp.split(text_up, text_up.shape[1] // text_width, 1) + [text_down]
    text_pieces += jnp.split(text_self, 3, 1) + [text_mix, text_merge]
    image_pieces = [image_query, text_key, text_value, image_merge, image_up, image_down]
    image_pieces += jnp.split(image_self, 3, 1) + [image_mix]
    def starts(pieces):
        marks = [0]
        for piece in pieces:
            marks.append(marks[-1] + piece.shape[0])
        return list(zip(marks[:-1], marks[1:]))

    def taken(block, at):
        return whole(block[:, at[0] : at[1]])

    def side_by_side(block, spans):
        return jnp.concatenate([taken(block, at) for at in spans], 1)

    text_at, image_at = starts(text_pieces), starts(image_pieces)
    packed = []

    def pack_image():
        shards = [image_query, text_key, text_value, image_merge, image_up, image_down, image_self, image_mix]
        packed.append(pack_rows(shards, inner))

    Order.last = []
    all_text = gather(copy_rows([text_up, text_down, text_self, text_mix, text_merge], text_width))
    weight_text_query, weight_image_held, all_vectors = gather_weights(
        [[text_query], [image_key, image_value]], vectors, sizes, pack_image
    )
    (packed_image,) = packed

    text_slots, image_slots = round_up(length, 8), round_up(regions, 8)

    def padded(array, slots):
        array = jnp.pad(array, ((0, 0), (0, slots - array.shape[1]), (0, 0)))
        return array.reshape(pairs * slots, array.shape[2])

    def rows_of(array):
        return array.reshape(-1, array.shape[-1])

    def pairs_of(array):
        return array.reshape(pairs, array.shape[0] // pairs, array.shape[1])

    def fill_of(live, count):
        slots = live.shape[1]
        fill = jnp.where(live, 0.0, jnp.where(jnp.arange(slots)[None, :] < count, MASKED, PADDED))
        return jnp.broadcast_to(fill[:, :, None], (pairs, slots, LANES)).astype(F32)

    text_rows, image_rows = padded(text_tokens, text_slots), padded(image_regions, image_slots)
    d_text_out = padded(text_cotangent, text_slots)
    d_image_out = padded(image_cotangent, image_slots)
    text_live = jnp.arange(text_slots)[None, :] < caption_lengths[:, None]
    image_live = jnp.pad(region_mask, ((0, 0), (0, image_slots - regions))) > 0
    text_fill, image_fill = fill_of(text_live, length), fill_of(image_live, regions)
    text_keep = text_live.astype(F32).reshape(-1, 1)
    image_keep = image_live.astype(F32).reshape(-1, 1)

    query_text = pairs_of(project(text_rows, weight_text_query).astype(BF16))
    held_image = pairs_of(project(image_rows, weight_image_held).astype(BF16))
    mixed_cross = attend((query_text, 0), (held_image, 0), (held_image, 1), image_fill, inner, HEADS)
    mixed_cross, packed_image = tie(mixed_cross, packed_image)
    all_image = gather(packed_image)
    cross_text = rows_of(mixed_cross)
    ups = text_up.shape[1] // text_width
    full_text_merge = taken(all_text, text_at[ups + 5])
    unit_text_1, rate_text_1 = normed_rows(text_rows.astype(F32) + project(cross_text, full_text_merge))

    full_text_up = side_by_side(all_text, text_at[:ups])
    full_text_down = taken(all_text, text_at[ups])
    full_text_self = side_by_side(all_text, text_at[ups + 1 : ups + 4])
    full_text_mix = taken(all_text, text_at[ups + 4])
    full = {
        name: all_vectors.reshape(devices, len(vectors), inner)[:, at, : piece.shape[0]].reshape(-1).astype(F32)
        for at, (name, piece) in enumerate(zip(VECTOR_NAMES, vectors))
    }

    def forward(unit_1, gain_1, up, bias, down, gain_2, joint, mix, gain_3, fill, keep, heads):
        width = unit_1.shape[1]
        first = unit_1 * gain_1
        first_low = first.astype(BF16)
        hidden = project(first_low, up) + bias
        active, slope = tie(gelu(hidden).astype(BF16), gelu_slope(hidden).astype(BF16))
        unit_2, rate_2 = normed_rows(first + project(active, down))
        second = unit_2 * gain_2
        second_low = second.astype(BF16)
        triple = pairs_of(project(second_low, joint).astype(BF16))
        mixed = rows_of(attend((triple, 0), (triple, 1), (triple, 2), fill, width, heads))
        unit_3, rate_3 = normed_rows(second + project(mixed, mix))
        out = (unit_3 * gain_3 * keep).astype(BF16)
        return out, (first_low, active, slope, unit_2, rate_2, second_low, triple, mixed, unit_3, rate_3)

    def self_backward(saved, gain_2, joint, mix, gain_3, fill, keep, d_out, heads):
        _, _, _, unit_2, rate_2, second_low, triple, mixed, unit_3, rate_3 = saved
        width = unit_2.shape[1]
        d_third, g_gain_3 = normed_back(unit_3, rate_3, gain_3, d_out.astype(F32) * keep)
        d_branch = d_third.astype(BF16)
        d_mixed = pairs_of(project_back(d_branch, mix).astype(BF16))
        d_triple = attend_back((triple, 0), (triple, 1), (triple, 2), fill, d_mixed, width, heads)
        d_triple = rows_of(jnp.concatenate(d_triple, -1))
        d_second = d_third + project_back(d_triple, joint)
        d_sum, g_gain_2 = normed_back(unit_2, rate_2, gain_2, d_second)
        return d_sum, (mixed, d_branch), (second_low, d_triple), g_gain_2, g_gain_3

    def feed_backward(saved, d_sum, unit_1, rate_1, gain_1, up, down):
        first_low, active, slope = saved[:3]
        d_sum_low = d_sum.astype(BF16)
        d_hidden = (slope.astype(F32) * project_back(d_sum_low, down)).astype(BF16)
        g_bias = jnp.sum(d_hidden.astype(F32), 0)
        d_first = d_sum + project_back(d_hidden, up)
        d_resid, g_gain_1 = normed_back(unit_1, rate_1, gain_1, d_first)
        return d_resid, (first_low, d_hidden), (active, d_sum_low), g_bias, g_gain_1

    out_text, saved_text = forward(
        unit_text_1,
        full["text_gain_cross"],
        full_text_up,
        full["text_bias"],
        full_text_down,
        full["text_gain_ffn"],
        full_text_self,
        full_text_mix,
        full["text_gain_self"],
        text_fill,
        text_keep,
        TEXT_HEADS,
    )
    d_sum_text, g_text_mix, g_text_self, g_text_gain_ffn, g_text_gain_self = self_backward(
        saved_text,
        full["text_gain_ffn"],
        full_text_self,
        full_text_mix,
        full["text_gain_self"],
        text_fill,
        text_keep,
        d_text_out,
        TEXT_HEADS,
    )
    row_text, row_image, row_down = text_query.shape[0], image_key.shape[0], text_down.shape[0]
    sum_a, sum_b = OwnerSum(text_width, sizes), OwnerSum(text_width, sizes)
    sum_c, sum_d, sum_e = OwnerSum(inner, sizes), OwnerSum(inner, sizes), OwnerSum(inner, sizes)
    sum_a.add(4 * row_text, (0, *g_text_self), (3 * row_text, *g_text_mix))
    d_resid_text, g_text_up, g_text_down, g_text_bias, g_text_gain_cross = feed_backward(
        saved_text, d_sum_text, unit_text_1, rate_text_1, full["text_gain_cross"], full_text_up, full_text_down
    )
    row_down, row_self = text_at[ups][0], text_at[ups + 1][0]
    sum_a.advance()
    sum_b.add(ups * row_text, (0, *g_text_up))
    sum_a.advance()
    sum_b.add(row_down, (0, *g_text_down))
    d_merge_text = d_resid_text.astype(BF16)
    sum_b.add(text_merge.shape[0], (0, cross_text, d_merge_text))
    d_heads_text = pairs_of(project_back(d_merge_text, full_text_merge).astype(BF16))
    d_query_text, d_key_image, d_value_image = map(
        rows_of,
        attend_back((query_text, 0), (held_image, 0), (held_image, 1), image_fill, d_heads_text, inner, HEADS),
    )
    sum_b.advance()
    sum_a.advance()
    row_first = round_up(2 * row_image, row_text)
    sums_first = scattered(
        [(0, image_rows, d_key_image), (row_image, image_rows, d_value_image), (row_first, text_rows, d_query_text)],
        row_first + row_text,
        inner,
        sizes,
    )
    weight_image_query = taken(all_image, image_at[0])
    weight_text_held = side_by_side(all_image, image_at[1:3])
    full_image_merge = taken(all_image, image_at[3])
    full_image_up = taken(all_image, image_at[4])
    full_image_down = taken(all_image, image_at[5])
    full_image_self = side_by_side(all_image, image_at[6:9])
    full_image_mix = taken(all_image, image_at[9])

    query_image = pairs_of(project(image_rows, weight_image_query).astype(BF16))
    held_text = pairs_of(project(text_rows, weight_text_held).astype(BF16))
    cross_image = rows_of(attend((query_image, 0), (held_text, 0), (held_text, 1), text_fill, inner, HEADS))
    sum_a.advance()
    unit_image_1, rate_image_1 = normed_rows(image_rows.astype(F32) + project(cross_image, full_image_merge))

    out_image, saved_image = forward(
        unit_image_1,
        full["image_gain_cross"],
        full_image_up,
        full["image_bias"],
        full_image_down,
        full["image_gain_ffn"],
        full_image_self,
        full_image_mix,
        full["image_gain_self"],
        image_fill,
        image_keep,
        IMAGE_HEADS,
    )
    sum_b.advance()
    sum_a.advance()
    d_sum_image, g_image_mix, g_image_self, g_image_gain_ffn, g_image_gain_self = self_backward(
        saved_image,
        full["image_gain_ffn"],
        full_image_self,
        full_image_mix,
        full["image_gain_self"],
        image_fill,
        image_keep,
        d_image_out,
        IMAGE_HEADS,
    )
    sum_c.add(4 * row_image, (0, *g_image_self), (3 * row_image, *g_image_mix))
    sum_b.advance()
    d_resid_image, g_image_up, g_image_down, g_image_bias, g_image_gain_cross = feed_backward(
        saved_image,
        d_sum_image,
        unit_image_1,
        rate_image_1,
        full["image_gain_cross"],
        full_image_up,
        full_image_down,
    )

    sum_c.advance()
    d_merge_image = d_resid_image.astype(BF16)
    sum_e.add(
        3 * row_image,
        (0, cross_image, d_merge_image),
        (row_image, *g_image_up),
        (2 * row_image, *g_image_down),
    )
    d_heads_image = pairs_of(project_back(d_merge_image, full_image_merge).astype(BF16))
    d_query_image, d_key_text, d_value_text = map(
        rows_of,
        attend_back((query_image, 0), (held_text, 0), (held_text, 1), text_fill, d_heads_image, inner, HEADS),
    )
    sum_b.advance()
    sum_c.advance()
    g_vectors = (
        g_text_gain_cross,
        g_image_gain_cross,
        g_text_bias,
        g_text_gain_ffn,
        g_image_bias,
        g_image_gain_ffn,
        g_text_gain_self,
        g_image_gain_self,
    )
    row_vector = 2 * row_text
    vector_rows = max(len(vectors), round_up(row_vector + len(vectors), row_image) - row_vector)
    row_query = row_vector + vector_rows
    g_vector = jnp.stack(
        [
            jnp.pad(owned, ((0, 0), (0, inner - owned.shape[1])))
            for owned in (piece.astype(BF16).reshape(devices, -1) for piece in g_vectors)
        ],
        1,
    )
    g_vector = jnp.pad(g_vector, ((0, 0), (0, vector_rows - len(vectors)), (0, 0)))
    sum_d.add(
        row_query + row_image,
        (0, text_rows, d_key_text),
        (row_text, text_rows, d_value_text),
        (row_query, image_rows, d_query_image),
        (row_vector, g_vector),
        later=True,
    )
    sums_first = widened(sums_first)
    sum_d.hold()
    sum_d.send()
    sum_e.advance()
    sum_d.advance()
    sum_c.advance()
    sum_b.advance()
    grad_text = (
        d_resid_text
        + project_back(d_query_text, weight_text_query)
        + project_back(jnp.concatenate([d_key_text, d_value_text], 1), weight_text_held)
    )
    grad_image = (
        d_resid_image
        + project_back(d_query_image, weight_image_query)
        + project_back(jnp.concatenate([d_key_image, d_value_image], 1), weight_image_held)
    )
    sum_e.advance()
    sum_c.advance()
    sum_d.advance()
    sum_e.advance()
    sum_c.advance()
    sum_d.advance()
    sum_e.advance()
    sum_d.advance()

    def owned(total, pieces):
        return [total[start:end] for start, end in starts(pieces)]

    sums_a, sums_b, sums_c, sums_e, sums_d = [one.result() for one in (sum_a, sum_b, sum_c, sum_e, sum_d)]
    text_selfs = owned(sums_a, text_pieces[ups + 1 : ups + 5])
    text_sums = owned(sums_b, text_pieces[: ups + 1] + [text_merge])
    image_firsts = owned(sums_first, [image_key, image_value]) + [sums_first[row_first : row_first + row_text]]
    image_selfs = owned(sums_c, image_pieces[6:10])
    image_sums = owned(sums_e, image_pieces[3:6]) + owned(sums_d, [text_key, text_value])
    sum_vector = sums_d[row_vector:row_query]
    owned_vector = {
        name: sum_vector[at, : piece.shape[0]] for at, (name, piece) in enumerate(zip(VECTOR_NAMES, vectors))
    }
    return (
        pairs_of(out_text)[:, :length],
        pairs_of(out_image)[:, :regions],
        pairs_of(grad_text)[:, :length],
        pairs_of(grad_image)[:, :regions],
        image_firsts[2],
        image_firsts[0],
        image_firsts[1],
        text_sums[ups + 1],
        owned_vector["text_gain_cross"],
        sums_d[row_query:],
        image_sums[3],
        image_sums[4],
        image_sums[0],
        owned_vector["image_gain_cross"],
        jnp.concatenate(text_sums[:ups], 1),
        owned_vector["text_bias"],
        text_sums[ups],
        owned_vector["text_gain_ffn"],
        image_sums[1],
        owned_vector["image_bias"],
        image_sums[2],
        owned_vector["image_gain_ffn"],
        jnp.concatenate(text_selfs[:3], 1),
        text_selfs[3],
        owned_vector["text_gain_self"],
        jnp.concatenate(image_selfs[:3], 1),
        image_selfs[3],
        owned_vector["image_gain_self"],
    )


def solution(mesh):
    split = {1: P(AXES), 2: P(AXES, None), 3: P(AXES, None, None)}
    in_ranks = (3, 3, 1, 2, 3, 3) + tuple(
        1 if at in (4, 9, 11, 13, 15, 17, 20, 23) else 2 for at in range(24)
    )
    out_ranks = (3, 3, 3, 3) + in_ranks[6:]
    return jax.shard_map(
        functools.partial(per_device, dict(mesh.shape)),
        mesh=mesh,
        in_specs=tuple(split[rank] for rank in in_ranks),
        out_specs=tuple(split[rank] for rank in out_ranks),
        check_vma=False,
    )
```
